32 devices in a mesh: req: 8 (over z, x), head: 4 (over y, core).
Axes of the slice: x: 2, y: 2, z: 4, core: 2. Of those that a mesh axis runs over, the one named last changes fastest.
Arguments:
- hidden: bfloat16 [256, 2048], P('req', 'head'), may hold values from -6 to 6
- lengths: int32 [256], P('req'), may hold values from 1 to 384, as said below
- expert_ids: int32 [256, 8], P('req'), may hold values from 0 to 63, all different within a row
- route_weights: float32 [256, 8], P('req'), may hold values from 0.25 to 2.5
- w_qkv: bfloat16 [3, 2048, 2048], P(None, None, 'head'), may hold values from -0.125 to 0.125
- w_out: bfloat16 [2048, 2048], P('head'), may hold values from -0.125 to 0.125
- k_cache: bfloat16 [256, 384, 16, 128], P('req', None, 'head'), may hold values from -400 to 400
- v_cache: bfloat16 [256, 384, 16, 128], P('req', None, 'head'), may hold values from -12 to 12
- w_in: bfloat16 [2048, 64, 2048], P(None, 'head', 'req'), may hold values from -0.125 to 0.125
- w_down: bfloat16 [64, 1024, 2048], P('head', 'req'), may hold values from -0.1875 to 0.1875
Outputs:
- output: bfloat16 [256, 2048], P('req', 'head')
The draws below stay inside these ranges and needn't reach their ends.
Inputs may be any that keep to these rules, and one draw needn't show every extreme that they name: `lengths`: some request has exactly 384 cached positions.
All inputs are finite; a program needn't handle non-finite values.
Results may differ from the reference program's by a relative error of at most 0.023.
Values may be sent and summed in bfloat16 or wider, within the bound.
No kernel may reach another device: no remote copies, remote signals or barrier semaphores. Data moves between devices by JAX's collectives and lax.ppermute only.
A program may use at most 128 MiB of HBM per device.

```python
import math
import jax
import jax.numpy as jnp
from jax import lax

D = 2048
HEADS = 16
HEAD_DIM = 128
EXPERTS = 64
FF = 1024
TOPK = 8
UNIT_BLOCK = 64
MAX_LEN = 384
REQUESTS = 256


def draw_lengths(key, part):
    group_count = REQUESTS // 8 + 1
    levels = jax.random.randint(jax.random.fold_in(key, 11), (group_count,), 0, 4)
    ceiling = jnp.right_shift(jnp.full((group_count,), MAX_LEN, jnp.int32), levels.astype(jnp.int32))
    per_request = ceiling[jnp.arange(REQUESTS, dtype=jnp.int32) // 8]
    drawn = jax.random.randint(jax.random.fold_in(key, 12), (REQUESTS,), 1, per_request + 1)
    chosen = jax.random.randint(jax.random.fold_in(key, 13), (), 0, REQUESTS)
    return jnp.where(jnp.arange(REQUESTS, dtype=jnp.int32) == chosen, MAX_LEN, drawn).astype(jnp.int32)


def draw_k_cache(key, part):
    shape = (REQUESTS, MAX_LEN, HEADS, HEAD_DIM)
    values = jnp.clip(jax.random.normal(jax.random.fold_in(key, 21), shape, jnp.float32), -6.0, 6.0)
    return values.astype(jnp.bfloat16)


def draw_v_cache(key, part):
    shape = (REQUESTS, MAX_LEN, HEADS, HEAD_DIM)
    base = jnp.clip(jax.random.normal(jax.random.fold_in(key, 31), (REQUESTS, 1, HEADS, HEAD_DIM), jnp.float32), -6.0, 6.0)
    noise = jnp.clip(jax.random.normal(jax.random.fold_in(key, 32), shape, jnp.float32), -6.0, 6.0)
    return (base + noise).astype(jnp.bfloat16)


def block_levels(own_key, extent, cuts, smallest, top_value):
    def one(axis_at, shards_of):
        draws = jax.random.uniform(jax.random.fold_in(jax.random.fold_in(own_key, 6), axis_at), (shards_of,), jnp.float32, smallest / len(cuts), top_value / len(cuts))
        return jnp.repeat(jnp.exp(draws), extent[axis_at] // shards_of).reshape((-1,) + (1,) * (len(extent) - axis_at - 1))

    level = one(*cuts[0])
    for cut in cuts[1:]:
        level = level * one(*cut)
    return level


def different_ones(stream_key, rows, count, top, lift):
    ranking = jax.random.permutation(jax.random.fold_in(stream_key, 1), count)
    boost = ranking
    for power in range(3):
        boost = boost * boost // count
    boost = boost * lift // count
    chance = jax.random.randint(jax.random.fold_in(stream_key, 2), (rows, count), 0, 4096) + boost
    sure = jax.random.permutation(jax.random.fold_in(stream_key, 3), rows)[jnp.arange(count) % rows]
    chance = jnp.where(jnp.arange(rows)[:, None] == sure[None, :], 1 << 14, chance)
    priority = chance * count + jnp.arange(count)
    return lax.top_k(priority.astype(jnp.int32), top)[1].astype(jnp.int32)


def bell_draw(rng, extent, spread, reach, split=(), kind=jnp.bfloat16):
    level = block_levels(rng, extent, split, -0.22, 0.18) if split else 1.0
    array = jax.random.normal(rng, extent, jnp.float32) * spread * level
    return jnp.minimum(jnp.maximum(array, -reach), reach).astype(kind)


def setup_inputs(seed: int = 0) -> dict:
    splits = jax.random.split(jax.random.key(seed), 11)
    return {
        "hidden": bell_draw(splits[0], (REQUESTS, D), 1.0, 6.0, ((0, 8), (1, 4))),
        "lengths": draw_lengths(jax.random.fold_in(splits[10], 71), 0),
        "expert_ids": different_ones(splits[2], REQUESTS, EXPERTS, TOPK, 1024),
        "route_weights": jnp.clip(jnp.exp(math.log(2.5) - 2.3025851 * jax.random.uniform(splits[3], (REQUESTS, TOPK), jnp.float32) ** block_levels(splits[3], (REQUESTS, TOPK), ((0, 8),), -0.2, 0.2)), 0.25, 2.5),
        "w_qkv": bell_draw(splits[4], (3, D, HEADS * HEAD_DIM), D ** -0.5, 0.125, ((2, 4),)),
        "w_out": bell_draw(splits[5], (HEADS * HEAD_DIM, D), (HEADS * HEAD_DIM) ** -0.5, 0.125, ((0, 4),)),
        "k_cache": draw_k_cache(jax.random.fold_in(splits[10], 71), 0),
        "v_cache": draw_v_cache(jax.random.fold_in(splits[10], 71), 0),
        "w_in": bell_draw(splits[8], (D, EXPERTS, 2 * FF), D ** -0.5, 0.125, ((1, 4), (2, 8))),
        "w_down": bell_draw(splits[9], (EXPERTS, FF, D), FF ** -0.5, 0.1875, ((0, 4), (1, 8))),
    }


rope_theta = 50000.0
norm_eps = 1e-05

def rotate(values, positions):
    half_dim = values.shape[-1] // 2
    freqs = rope_theta ** (-jnp.arange(half_dim, dtype=jnp.float32) / half_dim)
    angles = positions.astype(jnp.float32)[:, None] * freqs[None, :]
    cosine = jnp.cos(angles)[:, None, :]
    sine = jnp.sin(angles)[:, None, :]
    first_half = values[..., :half_dim]
    second_half = values[..., half_dim:]
    return jnp.concatenate([first_half * cosine - second_half * sine, second_half * cosine + first_half * sine], axis=-1)

def rms_normed(values):
    return (values * lax.rsqrt(lax.optimization_barrier(jnp.mean(values * values, axis=-1, keepdims=True)) + norm_eps)).astype(jnp.bfloat16)

def reference(hidden, lengths, expert_ids, route_weights, w_qkv, w_out, k_cache, v_cache, w_in, w_down):
    hidden_f = hidden.astype(jnp.float32)
    normed = rms_normed(hidden_f)
    projected = jnp.einsum('td,cdn->ctn', normed.astype(jnp.float32), w_qkv.astype(jnp.float32))
    projected = projected.reshape(3, REQUESTS, HEADS, HEAD_DIM)
    query = rotate(projected[0], lengths).astype(jnp.bfloat16)
    key_new = rotate(projected[1], lengths).astype(jnp.bfloat16)
    value_new = projected[2].astype(jnp.bfloat16)
    score_scale = HEAD_DIM ** (-0.5)

    def one_request(inputs):
        query_row, key_row, value_row, keys, values, length = inputs
        scores = jnp.einsum('hd,lhd->hl', query_row.astype(jnp.float32), keys.astype(jnp.float32)) * score_scale
        scores = jnp.where(jnp.arange(MAX_LEN, dtype=jnp.int32)[None, :] < length, scores, -jnp.inf)
        self_score = lax.optimization_barrier(jnp.sum(query_row.astype(jnp.float32) * key_row.astype(jnp.float32), axis=-1)) * score_scale
        row_top = jnp.maximum(lax.optimization_barrier(jnp.max(scores, axis=-1)), self_score)
        exponent = jnp.exp(scores - row_top[:, None])
        self_exp = jnp.exp(self_score - row_top)
        denominator = lax.optimization_barrier(jnp.sum(exponent, axis=-1)) + self_exp
        weights = (exponent / denominator[:, None]).astype(jnp.bfloat16)
        self_weight = (self_exp / denominator).astype(jnp.bfloat16)
        summed = jnp.einsum('hl,lhd->hd', weights.astype(jnp.float32), values.astype(jnp.float32))
        summed = summed + self_weight.astype(jnp.float32)[:, None] * value_row.astype(jnp.float32)
        return summed.astype(jnp.bfloat16)
    attended = lax.map(one_request, (query, key_new, value_new, k_cache, v_cache, lengths))
    attended = attended.reshape(REQUESTS, HEADS * HEAD_DIM)
    resid = hidden_f + jnp.dot(attended, w_out, preferred_element_type=jnp.float32)
    mixed = rms_normed(resid)
    expert_range = jnp.arange(EXPERTS, dtype=jnp.int32)
    share = lax.optimization_barrier(jnp.sum(route_weights[:, :, None] * (expert_ids[:, :, None] == expert_range[None, None, :]).astype(jnp.float32), axis=1))

    def one_expert(accum, inputs):
        weight_in, weight_down, expert_share = inputs
        gate_up = jnp.dot(mixed, weight_in, preferred_element_type=jnp.float32)
        gate_up = gate_up.reshape(REQUESTS, FF // UNIT_BLOCK, 2, UNIT_BLOCK)
        gate = gate_up[:, :, 0, :].reshape(REQUESTS, FF)
        upward = gate_up[:, :, 1, :].reshape(REQUESTS, FF)
        units = (expert_share[:, None] * (jax.nn.silu(gate) * upward)).astype(jnp.bfloat16)
        return (accum + jnp.dot(units, weight_down, preferred_element_type=jnp.float32), None)
    moe_sum, unused = lax.scan(one_expert, jnp.zeros((REQUESTS, D), jnp.float32), (jnp.moveaxis(w_in, 1, 0), w_down, share.T))
    return (resid + moe_sum).astype(jnp.bfloat16)
```

```python
import jax
import jax.numpy as jnp
from jax import lax
from jax.sharding import PartitionSpec as P

UNIT_BLOCK = 64
KEY_BLOCK = 128


rope_theta = 50000.0
norm_eps = 1e-05


def rotate(values, positions):
    half_dim = values.shape[-1] // 2
    freqs = rope_theta ** (-jnp.arange(half_dim, dtype=jnp.float32) / half_dim)
    angles = positions.astype(jnp.float32)[:, None] * freqs[None, :]
    cosine = jnp.cos(angles)[:, None, :]
    sine = jnp.sin(angles)[:, None, :]
    first_half = values[..., :half_dim]
    second_half = values[..., half_dim:]
    return jnp.concatenate(
        [first_half * cosine - second_half * sine, second_half * cosine + first_half * sine],
        axis=-1,
    )


def rms_normed(values):
    return (
        values * lax.rsqrt(jnp.mean(values * values, axis=-1, keepdims=True) + norm_eps)
    ).astype(jnp.bfloat16)


def swap(value, axis, size, mask):
    return lax.ppermute(value, axis, [(i, i ^ mask) for i in range(size)])


def attention(normed, lengths, w_qkv, k_cache, v_cache):
    req_local = normed.shape[0]
    heads_local = k_cache.shape[2]
    head_size = k_cache.shape[3]
    cache_len = k_cache.shape[1]
    projected = jnp.einsum("td,cdn->ctn", normed, w_qkv, preferred_element_type=jnp.float32)
    projected = projected.reshape(3, req_local, heads_local, head_size)
    query = rotate(projected[0], lengths).astype(jnp.bfloat16)
    key_new = rotate(projected[1], lengths).astype(jnp.bfloat16)
    value_new = projected[2].astype(jnp.bfloat16)
    score_scale = head_size ** (-0.5)
    block_count = (jnp.max(lengths) + KEY_BLOCK - 1) // KEY_BLOCK

    def score_block(block_idx, buffer):
        keys_block = lax.dynamic_slice_in_dim(k_cache, block_idx * KEY_BLOCK, KEY_BLOCK, 1)
        block_scores = (
            jnp.einsum("rhd,rlhd->rhl", query, keys_block, preferred_element_type=jnp.float32)
            * score_scale
        )
        return lax.dynamic_update_slice_in_dim(buffer, block_scores, block_idx * KEY_BLOCK, 2)

    buffer = jnp.full((req_local, heads_local, cache_len), -jnp.inf, jnp.float32)
    buffer = lax.fori_loop(0, block_count, score_block, buffer)
    positions = jnp.arange(cache_len, dtype=jnp.int32)
    scores = jnp.where(positions[None, None, :] < lengths[:, None, None], buffer, -jnp.inf)
    self_score = (
        jnp.einsum("rhd,rhd->rh", query, key_new, preferred_element_type=jnp.float32) * score_scale
    )
    row_top = jnp.maximum(jnp.max(scores, axis=-1), self_score)
    exponent = jnp.exp(scores - row_top[:, :, None])
    self_exp = jnp.exp(self_score - row_top)
    denominator = jnp.sum(exponent, axis=-1) + self_exp
    weights = (exponent / denominator[:, :, None]).astype(jnp.bfloat16)
    self_weight = (self_exp / denominator).astype(jnp.bfloat16)

    def value_block(block_idx, accum):
        weights_block = lax.dynamic_slice_in_dim(weights, block_idx * KEY_BLOCK, KEY_BLOCK, 2)
        values_block = lax.dynamic_slice_in_dim(v_cache, block_idx * KEY_BLOCK, KEY_BLOCK, 1)
        return accum + jnp.einsum(
            "rhl,rlhd->rhd", weights_block, values_block, preferred_element_type=jnp.float32
        )

    accum = lax.fori_loop(
        0, block_count, value_block, jnp.zeros((req_local, heads_local, head_size), jnp.float32)
    )
    accum = accum + self_weight.astype(jnp.float32)[:, :, None] * value_new.astype(jnp.float32)
    return accum.astype(jnp.bfloat16).reshape(req_local, heads_local * head_size)


def per_device(
    hidden, lengths, expert_ids, route_weights, w_qkv, w_out, k_cache, v_cache, w_in, w_down
):
    req_size = lax.axis_size("req")
    head_size = lax.axis_size("head")
    me = lax.axis_index("head")
    rows, cols = hidden.shape
    experts_local, units_local, width = w_down.shape
    even = range(0, head_size, 2)

    pieces = [hidden] + [swap(hidden, "head", head_size, j) for j in range(1, head_size)]
    stacked = jnp.stack(pieces)
    full_rows = jnp.concatenate(
        [lax.dynamic_index_in_dim(stacked, me ^ b, 0, False) for b in range(head_size)], axis=1
    )
    normed = rms_normed(full_rows.astype(jnp.float32))
    attended = attention(normed, lengths, w_qkv, k_cache, v_cache)
    head_terms = jnp.dot(attended, w_out, preferred_element_type=jnp.float32)
    head_terms = head_terms.astype(jnp.bfloat16).reshape(rows, head_size, cols)

    def block(array, j):
        return lax.dynamic_index_in_dim(array, me ^ j, array.ndim - 2, False)

    keep = jnp.concatenate([block(head_terms, j) for j in even], axis=1)
    send = jnp.concatenate([block(head_terms, j + 1) for j in even], axis=1)
    half = keep.astype(jnp.float32) + swap(send, "head", head_size, 1).astype(jnp.float32)
    half = half.astype(jnp.bfloat16)
    others = [swap(half, "head", head_size, j) for j in even if j]
    total = half.astype(jnp.float32).reshape(rows, head_size // 2, cols)
    for j, other in zip([j for j in even if j], others):
        other = other.reshape(rows, head_size // 2, cols)
        total = total + jnp.stack(
            [other[:, t ^ (j // 2)] for t in range(head_size // 2)], axis=1
        ).astype(jnp.float32)
    own_x = jnp.stack([pieces[j] for j in even], axis=1)
    resid = (own_x.astype(jnp.float32) + total).reshape(rows, head_size // 2 * cols)

    every = jnp.arange(head_size * experts_local, dtype=jnp.int32)
    matches = (expert_ids[:, :, None] == every[None, None, :]).astype(jnp.float32)
    shares = jnp.sum(route_weights[:, :, None] * matches, axis=1).astype(jnp.bfloat16)
    payload = jnp.concatenate([resid.astype(jnp.bfloat16), shares], axis=1)

    steps = range(2, req_size, 2)
    line = jnp.concatenate([payload] + [swap(payload, "req", req_size, k) for k in steps])
    mine = jnp.concatenate([line, swap(line, "req", req_size, 1)])
    states = mine[:, : resid.shape[1]]
    share = mine[:, resid.shape[1] :]
    other_states = swap(states, "head", head_size, 1)

    tokens = states.shape[0]
    square = jnp.sum(states.astype(jnp.float32) ** 2, axis=1) + jnp.sum(
        other_states.astype(jnp.float32) ** 2, axis=1
    )
    scale = lax.rsqrt(square / width + norm_eps)
    both = jnp.stack(
        [
            states.reshape(tokens, head_size // 2, cols),
            other_states.reshape(tokens, head_size // 2, cols),
        ],
        axis=2,
    ).reshape(tokens, head_size, cols)
    ordered = jnp.concatenate([block(both, b) for b in range(head_size)], axis=1)
    w_flat = w_in.transpose(1, 0, 2)
    gate_up = jnp.einsum("td,edn->etn", ordered, w_flat, preferred_element_type=jnp.float32)
    gate_up = gate_up * scale[None, :, None]
    gate_up = gate_up.reshape(experts_local, tokens, units_local // UNIT_BLOCK, 2, UNIT_BLOCK)
    local = lax.dynamic_slice_in_dim(share, me * experts_local, experts_local, 1)
    units = local.T.astype(jnp.float32)[:, :, None, None] * (
        jax.nn.silu(gate_up[:, :, :, 0]) * gate_up[:, :, :, 1]
    )
    units = units.astype(jnp.bfloat16).reshape(experts_local, tokens, units_local)
    w_blocks = w_down.reshape(experts_local, units_local, head_size, cols)

    def down(blocks):
        return jnp.concatenate(
            [
                jnp.einsum(
                    "etu,eun->tn", units, block(w_blocks, j), preferred_element_type=jnp.float32
                ).astype(jnp.bfloat16)
                for j in blocks
            ],
            axis=1,
        )

    sent = swap(down([j + 1 for j in even]), "head", head_size, 1)
    summed = down(even).astype(jnp.float32) + sent.astype(jnp.float32)
    summed = summed.astype(jnp.bfloat16).reshape(2, tokens // 2, head_size // 2, cols)
    total = summed[0, :, 0].astype(jnp.float32)
    for j in even:
        for k in range(2):
            if j or k:
                pairs = [
                    (r * head_size + h, (r ^ k) * head_size + (h ^ j))
                    for r in range(req_size)
                    for h in range(head_size)
                ]
                got = lax.ppermute(summed[k, :, j // 2], ("req", "head"), pairs)
                total = total + got.astype(jnp.float32)
    chunks = total.astype(jnp.bfloat16).reshape(req_size // 2, rows, cols)
    out = chunks[0].astype(jnp.float32)
    for k in steps:
        out = out + swap(chunks[k // 2], "req", req_size, k).astype(jnp.float32)
    return (out + resid[:, :cols]).astype(jnp.bfloat16)


def solution(mesh):
    in_specs = (
        P("req", "head"),
        P("req"),
        P("req", None),
        P("req", None),
        P(None, None, "head"),
        P("head", None),
        P("req", None, "head", None),
        P("req", None, "head", None),
        P(None, "head", "req"),
        P("head", "req", None),
    )
    out_specs = P("req", "head")
    return jax.shard_map(
        per_device, mesh=mesh, in_specs=in_specs, out_specs=out_specs, check_vma=False
    )
```

```python
import functools
import jax
import jax.numpy as jnp
from jax import lax
from jax.experimental import pallas as pl
from jax.experimental.pallas import tpu as pltpu
from jax.sharding import PartitionSpec as P

UNIT_BLOCK = 64


rope_theta = 50000.0
norm_eps = 1e-05
LANES = 128
SUBLANES = 8
CHUNK = 64
GROUP = 8
MASKED = -1e30


def attention_kernel(
    head_count, lengths_ref, me_ref, cos_ref, sin_ref, *refs
):
    pieces = refs[:head_count]
    (
        w_qkv_ref, w_out_ref, k_ref, v_ref, keep_ref, send_ref,
        w_qkv_s, w_out_s, k_s, v_s, query_s, key_s, value_s, attended_s,
        qkv_sem, out_sem, k_sem, v_sem,
    ) = refs[head_count:]
    rows, cols = pieces[0].shape
    heads_local = cols // LANES
    chunk_rows = CHUNK * heads_local
    me = me_ref[0]

    def qkv_copy(c, j):
        first = pl.multiple_of((me ^ j) * cols, cols)
        return pltpu.make_async_copy(
            w_qkv_ref.at[c, pl.ds(first, cols)], w_qkv_s.at[c, j], qkv_sem.at[c, j]
        )

    def out_copy(j):
        first = pl.multiple_of((me ^ j) * cols, cols)
        return pltpu.make_async_copy(
            w_out_ref.at[:, pl.ds(first, cols)], w_out_s.at[j], out_sem.at[j]
        )

    def cache_copy(source, target, sem, r):
        used = pl.multiple_of((lengths_ref[r] + 7) // 8 * (8 * heads_local), 8 * heads_local)
        return pltpu.make_async_copy(
            source.at[r, pl.ds(0, used)], target.at[r, pl.ds(0, used)], sem.at[r]
        )

    for c in range(3):
        for j in range(head_count):
            qkv_copy(c, j).start()

    @pl.loop(0, rows)
    def _(r):
        cache_copy(k_ref, k_s, k_sem, r).start()
        last = pl.multiple_of((lengths_ref[r] - 1) // CHUNK * chunk_rows, chunk_rows)
        v_s[r, pl.ds(last, chunk_rows)] = jnp.zeros((chunk_rows, LANES), jnp.bfloat16)
        cache_copy(v_ref, v_s, v_sem, r).start()

    for j in range(head_count):
        out_copy(j).start()

    states = [piece[...].astype(jnp.float32) for piece in pieces]
    square = sum(jnp.sum(state * state, axis=1, keepdims=True) for state in states)
    scale = lax.rsqrt(square / (cols * head_count) + norm_eps)
    normed = [(state * scale).astype(jnp.bfloat16) for state in states]
    cosine, sine = cos_ref[...], sin_ref[...]
    if heads_local < SUBLANES:
        query_s[...] = jnp.zeros_like(query_s)
        key_s[...] = jnp.zeros_like(key_s)
        value_s[...] = jnp.zeros_like(value_s)
    for c, target in enumerate((query_s, key_s, value_s)):
        projected = jnp.zeros((rows, cols), jnp.float32)
        for j in range(head_count):
            qkv_copy(c, j).wait()
            projected += jnp.dot(normed[j], w_qkv_s[c, j], preferred_element_type=jnp.float32)
        for h in range(heads_local):
            part = projected[:, h * LANES : (h + 1) * LANES]
            if c < 2:
                part = part * cosine + pltpu.roll(part, LANES // 2, 1) * sine
            target[:, h, :] = part.astype(jnp.bfloat16).astype(jnp.float32)

    column = lax.broadcasted_iota(jnp.int32, (SUBLANES, chunk_rows), 1)
    row = lax.broadcasted_iota(jnp.int32, (SUBLANES, chunk_rows), 0)
    same_head = column % heads_local == row
    score_scale = LANES**-0.5

    @pl.loop(0, rows // GROUP)
    def _(g):
        requests = [g * GROUP + i for i in range(GROUP)]
        lengths = [lengths_ref[r] for r in requests]
        queries = [query_s[r].astype(jnp.bfloat16) for r in requests]
        top = [
            jnp.sum(query_s[r] * key_s[r], axis=1, keepdims=True) * score_scale for r in requests
        ]
        total = [jnp.ones((SUBLANES, 1), jnp.float32)] * GROUP
        accum = [value_s[r] for r in requests]
        longest = functools.reduce(jnp.maximum, lengths)
        for r in requests:
            cache_copy(k_ref, k_s, k_sem, r).wait()
            cache_copy(v_ref, v_s, v_sem, r).wait()

        def step(c, carry):
            top, total, accum = carry
            starts = [
                pl.multiple_of(jnp.minimum(c, (n - 1) // CHUNK) * chunk_rows, chunk_rows)
                for n in lengths
            ]
            scores = [
                lax.dot_general(
                    queries[i],
                    k_s[r, pl.ds(starts[i], chunk_rows)],
                    (((1,), (1,)), ((), ())),
                    preferred_element_type=jnp.float32,
                )
                for i, r in enumerate(requests)
            ]
            scores = [
                jnp.where(
                    same_head & (column < (n - c * CHUNK) * heads_local), s * score_scale, MASKED
                )
                for n, s in zip(lengths, scores)
            ]
            new_top = [
                jnp.maximum(t, jnp.max(s, axis=1, keepdims=True)) for t, s in zip(top, scores)
            ]
            weights = [jnp.exp(s - t) for s, t in zip(scores, new_top)]
            fade = [jnp.exp(a - b) for a, b in zip(top, new_top)]
            total = [
                t * f + jnp.sum(w, axis=1, keepdims=True) for t, f, w in zip(total, fade, weights)
            ]
            accum = [
                a * f
                + jnp.dot(
                    w.astype(jnp.bfloat16),
                    v_s[r, pl.ds(starts[i], chunk_rows)],
                    preferred_element_type=jnp.float32,
                )
                for i, (r, a, f, w) in enumerate(zip(requests, accum, fade, weights))
            ]
            return new_top, total, accum

        top, total, accum = lax.fori_loop(
            0, (longest + CHUNK - 1) // CHUNK, step, (top, total, accum)
        )
        for r, t, a in zip(requests, total, accum):
            attended_s[r] = a / t

    attended = jnp.concatenate(
        [attended_s[:, h, :] for h in range(heads_local)], axis=1
    ).astype(jnp.bfloat16)
    for j in range(head_count):
        out_copy(j).wait()
        target = send_ref if j % 2 else keep_ref
        target[:, j // 2 * cols : (j // 2 + 1) * cols] = jnp.dot(
            attended, w_out_s[j], preferred_element_type=jnp.float32
        ).astype(jnp.bfloat16)


def attention(pieces, me, lengths, cosine, sine, w_qkv, w_out, k_cache, v_cache):
    head_count = len(pieces)
    rows, cols = pieces[0].shape
    cache_len, heads_local, head_dim = k_cache.shape[1:]
    flat = (rows, cache_len * heads_local, head_dim)
    vmem = pl.BlockSpec(memory_space=pltpu.VMEM)
    smem = pl.BlockSpec(memory_space=pltpu.SMEM)
    anywhere = pl.BlockSpec(memory_space=pl.ANY)
    half = jax.ShapeDtypeStruct((rows, head_count // 2 * cols), jnp.bfloat16)
    return pl.pallas_call(
        functools.partial(attention_kernel, head_count),
        out_shape=(half, half),
        in_specs=[smem, smem, vmem, vmem] + [vmem] * head_count + [anywhere] * 4,
        out_specs=(vmem, vmem),
        scratch_shapes=[
            pltpu.VMEM((3, head_count, cols, cols), jnp.bfloat16),
            pltpu.VMEM((head_count, cols, cols), jnp.bfloat16),
            pltpu.VMEM(flat, jnp.bfloat16),
            pltpu.VMEM(flat, jnp.bfloat16),
        ]
        + [pltpu.VMEM((rows, SUBLANES, LANES), jnp.float32)] * 4
        + [
            pltpu.SemaphoreType.DMA((3, head_count)),
            pltpu.SemaphoreType.DMA((head_count,)),
            pltpu.SemaphoreType.DMA((rows,)),
            pltpu.SemaphoreType.DMA((rows,)),
        ],
        compiler_params=pltpu.CompilerParams(vmem_limit_bytes=44 * 2**20),
        cost_estimate=pl.CostEstimate(
            flops=2 * rows * 4 * cols * head_count * cols,
            bytes_accessed=8 * cols * cols * head_count + 4 * rows * cache_len * cols // 2,
            transcendentals=0,
        ),
        name="attention",
    )(lengths, me, cosine, sine, *pieces, w_qkv, w_out, k_cache.reshape(flat), v_cache.reshape(flat))


def swap(value, axis, size, mask):
    return lax.ppermute(value, axis, [(i, i ^ mask) for i in range(size)])


def per_device(
    hidden, lengths, expert_ids, route_weights, w_qkv, w_out, k_cache, v_cache, w_in, w_down
):
    req_size = lax.axis_size("req")
    head_size = lax.axis_size("head")
    me = lax.axis_index("head")
    rows, cols = hidden.shape
    experts_local, units_local, width = w_down.shape
    even = range(0, head_size, 2)

    def block(array, j):
        return lax.dynamic_index_in_dim(array, me ^ j, array.ndim - 2, False)

    pieces = [hidden] + [swap(hidden, "head", head_size, j) for j in range(1, head_size)]
    half_dim = k_cache.shape[3] // 2
    freqs = rope_theta ** (-jnp.arange(half_dim, dtype=jnp.float32) / half_dim)
    angles = lengths.astype(jnp.float32)[:, None] * freqs[None, :]
    cosine, sine = jnp.cos(angles), jnp.sin(angles)
    keep, send = attention(
        pieces,
        me[None].astype(jnp.int32),
        lengths,
        jnp.concatenate([cosine, cosine], axis=1),
        jnp.concatenate([-sine, sine], axis=1),
        w_qkv,
        w_out,
        k_cache,
        v_cache,
    )
    half = keep.astype(jnp.float32) + swap(send, "head", head_size, 1).astype(jnp.float32)
    half = half.astype(jnp.bfloat16)
    others = [swap(half, "head", head_size, j) for j in even if j]
    total = half.astype(jnp.float32).reshape(rows, head_size // 2, cols)
    for j, other in zip([j for j in even if j], others):
        other = other.reshape(rows, head_size // 2, cols)
        total = total + jnp.stack(
            [other[:, t ^ (j // 2)] for t in range(head_size // 2)], axis=1
        ).astype(jnp.float32)
    own_x = jnp.stack([pieces[j] for j in even], axis=1)
    resid = (own_x.astype(jnp.float32) + total).reshape(rows, head_size // 2 * cols)

    every = jnp.arange(head_size * experts_local, dtype=jnp.int32)
    matches = (expert_ids[:, :, None] == every[None, None, :]).astype(jnp.float32)
    shares = jnp.sum(route_weights[:, :, None] * matches, axis=1).astype(jnp.bfloat16)
    payload = jnp.concatenate([resid.astype(jnp.bfloat16), shares], axis=1)

    steps = range(2, req_size, 2)
    line = jnp.concatenate([payload] + [swap(payload, "req", req_size, k) for k in steps])
    mine = jnp.concatenate([line, swap(line, "req", req_size, 1)])
    states = mine[:, : resid.shape[1]]
    share = mine[:, resid.shape[1] :]
    other_states = swap(states, "head", head_size, 1)

    tokens = states.shape[0]
    square = jnp.sum(states.astype(jnp.float32) ** 2, axis=1) + jnp.sum(
        other_states.astype(jnp.float32) ** 2, axis=1
    )
    scale = lax.rsqrt(square / width + norm_eps)
    both = jnp.stack(
        [
            states.reshape(tokens, head_size // 2, cols),
            other_states.reshape(tokens, head_size // 2, cols),
        ],
        axis=2,
    ).reshape(tokens, head_size, cols)
    ordered = jnp.concatenate([block(both, b) for b in range(head_size)], axis=1)
    w_flat = w_in.transpose(1, 0, 2)
    gate_up = jnp.einsum("td,edn->etn", ordered, w_flat, preferred_element_type=jnp.float32)
    gate_up = gate_up * scale[None, :, None]
    gate_up = gate_up.reshape(experts_local, tokens, units_local // UNIT_BLOCK, 2, UNIT_BLOCK)
    local = lax.dynamic_slice_in_dim(share, me * experts_local, experts_local, 1)
    units = local.T.astype(jnp.float32)[:, :, None, None] * (
        jax.nn.silu(gate_up[:, :, :, 0]) * gate_up[:, :, :, 1]
    )
    units = units.astype(jnp.bfloat16).reshape(experts_local, tokens, units_local)
    w_blocks = w_down.reshape(experts_local, units_local, head_size, cols)

    def down(blocks):
        return jnp.concatenate(
            [
                jnp.einsum(
                    "etu,eun->tn", units, block(w_blocks, j), preferred_element_type=jnp.float32
                ).astype(jnp.bfloat16)
                for j in blocks
            ],
            axis=1,
        )

    sent = swap(down([j + 1 for j in even]), "head", head_size, 1)
    summed = down(even).astype(jnp.float32) + sent.astype(jnp.float32)
    summed = summed.astype(jnp.bfloat16).reshape(2, tokens // 2, head_size // 2, cols)
    total = summed[0, :, 0].astype(jnp.float32)
    for j in even:
        for k in range(2):
            if j or k:
                pairs = [
                    (r * head_size + h, (r ^ k) * head_size + (h ^ j))
                    for r in range(req_size)
                    for h in range(head_size)
                ]
                got = lax.ppermute(summed[k, :, j // 2], ("req", "head"), pairs)
                total = total + got.astype(jnp.float32)
    chunks = total.astype(jnp.bfloat16).reshape(req_size // 2, rows, cols)
    out = chunks[0].astype(jnp.float32)
    for k in steps:
        out = out + swap(chunks[k // 2], "req", req_size, k).astype(jnp.float32)
    return (out + resid[:, :cols]).astype(jnp.bfloat16)


def solution(mesh):
    in_specs = (
        P("req", "head"),
        P("req"),
        P("req", None),
        P("req", None),
        P(None, None, "head"),
        P("head", None),
        P("req", None, "head", None),
        P("req", None, "head", None),
        P(None, "head", "req"),
        P("head", "req", None),
    )
    out_specs = P("req", "head")
    return jax.shard_map(
        per_device, mesh=mesh, in_specs=in_specs, out_specs=out_specs, check_vma=False
    )
```

```python
import functools
import jax
import jax.numpy as jnp
from jax import lax
from jax.experimental import pallas as pl
from jax.experimental.pallas import tpu as pltpu
from jax.sharding import PartitionSpec as P

rope_theta = 50000.0
norm_eps = 1e-05
LANES = 128
SUBLANES = 8
CHUNK = 64
GROUP = 8
MASKED = -1e30


def attention_kernel(
    head_count, lengths_ref, me_ref, cos_ref, sin_ref, *refs
):
    pieces = refs[:head_count]
    (
        w_qkv_ref, w_out_ref, k_ref, v_ref, keep_ref, send_ref,
        w_qkv_s, w_out_s, k_s, v_s, query_s, key_s, value_s, attended_s,
        qkv_sem, out_sem, k_sem, v_sem,
    ) = refs[head_count:]
    rows, cols = pieces[0].shape
    heads_local = cols // LANES
    chunk_rows = CHUNK * heads_local
    me = me_ref[0]

    def qkv_copy(c, j):
        first = pl.multiple_of((me ^ j) * cols, cols)
        return pltpu.make_async_copy(
            w_qkv_ref.at[c, pl.ds(first, cols)], w_qkv_s.at[c, j], qkv_sem.at[c, j]
        )

    def out_copy(j):
        first = pl.multiple_of((me ^ j) * cols, cols)
        return pltpu.make_async_copy(
            w_out_ref.at[:, pl.ds(first, cols)], w_out_s.at[j], out_sem.at[j]
        )

    def cache_copy(source, target, sem, r):
        used = pl.multiple_of((lengths_ref[r] + 7) // 8 * (8 * heads_local), 8 * heads_local)
        return pltpu.make_async_copy(
            source.at[r, pl.ds(0, used)], target.at[r, pl.ds(0, used)], sem.at[r]
        )

    for c in range(3):
        for j in range(head_count):
            qkv_copy(c, j).start()

    @pl.loop(0, rows)
    def _(r):
        cache_copy(k_ref, k_s, k_sem, r).start()
        last = pl.multiple_of((lengths_ref[r] - 1) // CHUNK * chunk_rows, chunk_rows)
        v_s[r, pl.ds(last, chunk_rows)] = jnp.zeros((chunk_rows, LANES), jnp.bfloat16)
        cache_copy(v_ref, v_s, v_sem, r).start()

    for j in range(head_count):
        out_copy(j).start()

    states = [piece[...].astype(jnp.float32) for piece in pieces]
    square = sum(jnp.sum(state * state, axis=1, keepdims=True) for state in states)
    scale = lax.rsqrt(square / (cols * head_count) + norm_eps)
    normed = [(state * scale).astype(jnp.bfloat16) for state in states]
    cosine, sine = cos_ref[...], sin_ref[...]
    if heads_local < SUBLANES:
        query_s[...] = jnp.zeros_like(query_s)
        key_s[...] = jnp.zeros_like(key_s)
        value_s[...] = jnp.zeros_like(value_s)
    for c, target in enumerate((query_s, key_s, value_s)):
        projected = jnp.zeros((rows, cols), jnp.float32)
        for j in range(head_count):
            qkv_copy(c, j).wait()
            projected += jnp.dot(normed[j], w_qkv_s[c, j], preferred_element_type=jnp.float32)
        for h in range(heads_local):
            part = projected[:, h * LANES : (h + 1) * LANES]
            if c < 2:
                part = part * cosine + pltpu.roll(part, LANES // 2, 1) * sine
            target[:, h, :] = part.astype(jnp.bfloat16).astype(jnp.float32)

    column = lax.broadcasted_iota(jnp.int32, (SUBLANES, chunk_rows), 1)
    row = lax.broadcasted_iota(jnp.int32, (SUBLANES, chunk_rows), 0)
    same_head = column % heads_local == row
    score_scale = LANES**-0.5

    @pl.loop(0, rows // GROUP)
    def _(g):
        requests = [g * GROUP + i for i in range(GROUP)]
        lengths = [lengths_ref[r] for r in requests]
        queries = [query_s[r].astype(jnp.bfloat16) for r in requests]
        top = [
            jnp.sum(query_s[r] * key_s[r], axis=1, keepdims=True) * score_scale for r in requests
        ]
        total = [jnp.ones((SUBLANES, 1), jnp.float32)] * GROUP
        accum = [value_s[r] for r in requests]
        longest = functools.reduce(jnp.maximum, lengths)
        for r in requests:
            cache_copy(k_ref, k_s, k_sem, r).wait()
            cache_copy(v_ref, v_s, v_sem, r).wait()

        def step(c, carry):
            top, total, accum = carry
            starts = [
                pl.multiple_of(jnp.minimum(c, (n - 1) // CHUNK) * chunk_rows, chunk_rows)
                for n in lengths
            ]
            scores = [
                lax.dot_general(
                    queries[i],
                    k_s[r, pl.ds(starts[i], chunk_rows)],
                    (((1,), (1,)), ((), ())),
                    preferred_element_type=jnp.float32,
                )
                for i, r in enumerate(requests)
            ]
            scores = [
                jnp.where(
                    same_head & (column < (n - c * CHUNK) * heads_local), s * score_scale, MASKED
                )
                for n, s in zip(lengths, scores)
            ]
            new_top = [
                jnp.maximum(t, jnp.max(s, axis=1, keepdims=True)) for t, s in zip(top, scores)
            ]
            weights = [jnp.exp(s - t) for s, t in zip(scores, new_top)]
            fade = [jnp.exp(a - b) for a, b in zip(top, new_top)]
            total = [
                t * f + jnp.sum(w, axis=1, keepdims=True) for t, f, w in zip(total, fade, weights)
            ]
            accum = [
                a * f
                + jnp.dot(
                    w.astype(jnp.bfloat16),
                    v_s[r, pl.ds(starts[i], chunk_rows)],
                    preferred_element_type=jnp.float32,
                )
                for i, (r, a, f, w) in enumerate(zip(requests, accum, fade, weights))
            ]
            return new_top, total, accum

        top, total, accum = lax.fori_loop(
            0, (longest + CHUNK - 1) // CHUNK, step, (top, total, accum)
        )
        for r, t, a in zip(requests, total, accum):
            attended_s[r] = a / t

    attended = jnp.concatenate(
        [attended_s[:, h, :] for h in range(heads_local)], axis=1
    ).astype(jnp.bfloat16)
    for j in range(head_count):
        out_copy(j).wait()
        target = send_ref if j % 2 else keep_ref
        target[:, j // 2 * cols : (j // 2 + 1) * cols] = jnp.dot(
            attended, w_out_s[j], preferred_element_type=jnp.float32
        ).astype(jnp.bfloat16)


def attention(pieces, me, lengths, cosine, sine, w_qkv, w_out, k_cache, v_cache):
    head_count = len(pieces)
    rows, cols = pieces[0].shape
    cache_len, heads_local, head_dim = k_cache.shape[1:]
    flat = (rows, cache_len * heads_local, head_dim)
    vmem = pl.BlockSpec(memory_space=pltpu.VMEM)
    smem = pl.BlockSpec(memory_space=pltpu.SMEM)
    anywhere = pl.BlockSpec(memory_space=pl.ANY)
    half = jax.ShapeDtypeStruct((rows, head_count // 2 * cols), jnp.bfloat16)
    return pl.pallas_call(
        functools.partial(attention_kernel, head_count),
        out_shape=(half, half),
        in_specs=[smem, smem, vmem, vmem] + [vmem] * head_count + [anywhere] * 4,
        out_specs=(vmem, vmem),
        scratch_shapes=[
            pltpu.VMEM((3, head_count, cols, cols), jnp.bfloat16),
            pltpu.VMEM((head_count, cols, cols), jnp.bfloat16),
            pltpu.VMEM(flat, jnp.bfloat16),
            pltpu.VMEM(flat, jnp.bfloat16),
        ]
        + [pltpu.VMEM((rows, SUBLANES, LANES), jnp.float32)] * 4
        + [
            pltpu.SemaphoreType.DMA((3, head_count)),
            pltpu.SemaphoreType.DMA((head_count,)),
            pltpu.SemaphoreType.DMA((rows,)),
            pltpu.SemaphoreType.DMA((rows,)),
        ],
        compiler_params=pltpu.CompilerParams(vmem_limit_bytes=44 * 2**20),
        cost_estimate=pl.CostEstimate(
            flops=2 * rows * 4 * cols * head_count * cols,
            bytes_accessed=8 * cols * cols * head_count + 4 * rows * cache_len * cols // 2,
            transcendentals=0,
        ),
        name="attention",
    )(lengths, me, cosine, sine, *pieces, w_qkv, w_out, k_cache.reshape(flat), v_cache.reshape(flat))


RELAYOUT_ROWS = 128
RELAYOUT_STEP = 16


def relayout_kernel(j, me_ref, w_ref, out_ref, in_s, in_sem):
    experts, cols, _ = out_ref.shape
    base = (me_ref[0] ^ j) * cols
    step = min(RELAYOUT_ROWS, cols)
    copies = [
        pltpu.make_async_copy(
            w_ref.at[pl.ds(pl.multiple_of(base + i * step, step), step)], in_s.at[i], in_sem.at[i]
        )
        for i in range(cols // step)
    ]
    for copy in copies:
        copy.start()
    for i, copy in enumerate(copies):
        copy.wait()

        @pl.loop(0, step // RELAYOUT_STEP, unroll=True)
        def _(s):
            first = pl.multiple_of(s * RELAYOUT_STEP, RELAYOUT_STEP)
            part = in_s[i, pl.ds(first, RELAYOUT_STEP)]
            out_ref[:, pl.ds(pl.multiple_of(i * step + first, RELAYOUT_STEP), RELAYOUT_STEP), :] = (
                jnp.swapaxes(part, 0, 1)
            )


def by_expert(j, me, w_in, head_count):
    width, experts, columns = w_in.shape
    cols = width // head_count
    step = min(RELAYOUT_ROWS, cols)
    return pl.pallas_call(
        functools.partial(relayout_kernel, j),
        out_shape=pltpu.VMEM((experts, cols, columns), jnp.bfloat16),
        in_specs=[pl.BlockSpec(memory_space=pltpu.SMEM), pl.BlockSpec(memory_space=pl.ANY)],
        out_specs=pl.BlockSpec(memory_space=pltpu.VMEM),
        scratch_shapes=[
            pltpu.VMEM((cols // step, step, experts, columns), jnp.bfloat16),
            pltpu.SemaphoreType.DMA((cols // step,)),
        ],
        compiler_params=pltpu.CompilerParams(vmem_limit_bytes=16 * 2**20),
        cost_estimate=pl.CostEstimate(
            flops=0, bytes_accessed=4 * cols * experts * columns, transcendentals=0
        ),
        name=f"by_expert_{j}",
    )(me, w_in)


def down_copy(w_ref, scratch, sem, me, j, t):
    cols = scratch.shape[2]
    first = pl.multiple_of((me ^ j) * cols, cols)
    return pltpu.make_async_copy(w_ref.at[:, pl.ds(first, cols)], scratch.at[t], sem.at[t])


def experts_kernel(head_count, me_ref, mine_ref, other_ref, *refs):
    weights = refs[:head_count]
    w_down_ref, units_ref, send_ref, down_s, down_sem = refs[head_count:]
    me = me_ref[0]
    blocks = head_count // 2
    for t in range(blocks):
        down_copy(w_down_ref, down_s, down_sem, me, 2 * t + 1, t).start()
    experts, cols, columns = weights[0].shape
    tokens = mine_ref.shape[0]
    states = [
        (other_ref if j % 2 else mine_ref)[:, j // 2 * cols : (j // 2 + 1) * cols]
        for j in range(head_count)
    ]
    shares = mine_ref[:, blocks * cols :]
    square = sum(
        jnp.sum(jnp.square(state.astype(jnp.float32)), axis=1, keepdims=True) for state in states
    )
    scale = lax.rsqrt(square / (head_count * cols) + norm_eps)
    per_step = max(1, 2 * LANES // columns)
    first_half = lax.broadcasted_iota(jnp.int32, (tokens, LANES), 1) < LANES // 2
    source = lax.broadcasted_iota(jnp.int32, (LANES, LANES), 0)
    lane = lax.broadcasted_iota(jnp.int32, (LANES, LANES), 1)

    @pl.loop(0, experts // per_step)
    def _(p):
        products = [
            sum(
                jnp.dot(state, w[p * per_step + i], preferred_element_type=jnp.float32)
                for state, w in zip(states, weights)
            )
            for i in range(per_step)
        ]
        product = products[0] if per_step == 1 else jnp.concatenate(products, axis=1)
        expert = me * experts + p * per_step + lane * per_step // LANES
        share = jnp.dot(
            shares, (source == expert).astype(jnp.bfloat16), preferred_element_type=jnp.float32
        )
        a, b = product[:, :LANES], product[:, LANES:]
        gate = jnp.where(first_half, a, pltpu.roll(b, LANES // 2, 1)) * scale
        upward = jnp.where(first_half, pltpu.roll(a, LANES // 2, 1), b) * scale
        units = share * (gate / (1.0 + jnp.exp(-gate)) * upward)
        units_ref[:, pl.ds(pl.multiple_of(p * LANES, LANES), LANES)] = units.astype(jnp.bfloat16)

    units = units_ref[...]
    for t in range(blocks):
        down_copy(w_down_ref, down_s, down_sem, me, 2 * t + 1, t).wait()
        send_ref[:, t * cols : (t + 1) * cols] = jnp.dot(
            units, down_s[t], preferred_element_type=jnp.float32
        ).astype(jnp.bfloat16)


def experts_part(me, mine, other, weights, w_down):
    head_count = len(weights)
    experts, cols, columns = weights[0].shape
    tokens = mine.shape[0]
    total_units = w_down.shape[0]
    vmem = pl.BlockSpec(memory_space=pltpu.VMEM)
    return pl.pallas_call(
        functools.partial(experts_kernel, head_count),
        out_shape=(
            jax.ShapeDtypeStruct((tokens, total_units), jnp.bfloat16),
            jax.ShapeDtypeStruct((tokens, head_count // 2 * cols), jnp.bfloat16),
        ),
        in_specs=[pl.BlockSpec(memory_space=pltpu.SMEM)]
        + [vmem] * (2 + head_count)
        + [pl.BlockSpec(memory_space=pl.ANY)],
        out_specs=(vmem, vmem),
        scratch_shapes=[
            pltpu.VMEM((head_count // 2, total_units, cols), jnp.bfloat16),
            pltpu.SemaphoreType.DMA((head_count // 2,)),
        ],
        compiler_params=pltpu.CompilerParams(vmem_limit_bytes=16 * 2**20),
        cost_estimate=pl.CostEstimate(
            flops=2 * tokens * head_count * cols * experts * columns,
            bytes_accessed=2 * head_count * cols * experts * columns,
            transcendentals=0,
        ),
        name="experts",
    )(me, mine, other, *[pltpu.with_memory_space_constraint(w, pltpu.VMEM) for w in weights], w_down)


def down_kernel(head_count, me_ref, units_ref, w_down_ref, keep_ref, down_s, down_sem):
    me = me_ref[0]
    cols = down_s.shape[2]
    blocks = head_count // 2
    for t in range(blocks):
        down_copy(w_down_ref, down_s, down_sem, me, 2 * t, t).start()
    units = units_ref[...]
    for t in range(blocks):
        down_copy(w_down_ref, down_s, down_sem, me, 2 * t, t).wait()
        keep_ref[:, t * cols : (t + 1) * cols] = jnp.dot(
            units, down_s[t], preferred_element_type=jnp.float32
        ).astype(jnp.bfloat16)


def down_part(me, units, w_down, head_count):
    tokens, total_units = units.shape
    cols = w_down.shape[1] // head_count
    vmem = pl.BlockSpec(memory_space=pltpu.VMEM)
    return pl.pallas_call(
        functools.partial(down_kernel, head_count),
        out_shape=jax.ShapeDtypeStruct((tokens, head_count // 2 * cols), jnp.bfloat16),
        in_specs=[
            pl.BlockSpec(memory_space=pltpu.SMEM),
            vmem,
            pl.BlockSpec(memory_space=pl.ANY),
        ],
        out_specs=vmem,
        scratch_shapes=[
            pltpu.VMEM((head_count // 2, total_units, cols), jnp.bfloat16),
            pltpu.SemaphoreType.DMA((head_count // 2,)),
        ],
        compiler_params=pltpu.CompilerParams(vmem_limit_bytes=16 * 2**20),
        cost_estimate=pl.CostEstimate(
            flops=2 * tokens * total_units * head_count // 2 * cols,
            bytes_accessed=2 * total_units * head_count // 2 * cols,
            transcendentals=0,
        ),
        name="down",
    )(me, units, w_down)


def swap(value, axis, size, mask):
    return lax.ppermute(value, axis, [(i, i ^ mask) for i in range(size)])


def per_device(
    hidden, lengths, expert_ids, route_weights, w_qkv, w_out, k_cache, v_cache, w_in, w_down
):
    req_size = lax.axis_size("req")
    head_size = lax.axis_size("head")
    me = lax.axis_index("head")
    me_ref = me[None].astype(jnp.int32)
    rows, cols = hidden.shape
    experts_local, units_local, width = w_down.shape
    even = range(0, head_size, 2)

    pieces = [hidden] + [swap(hidden, "head", head_size, j) for j in range(1, head_size)]
    half_dim = k_cache.shape[3] // 2
    freqs = rope_theta ** (-jnp.arange(half_dim, dtype=jnp.float32) / half_dim)
    angles = lengths.astype(jnp.float32)[:, None] * freqs[None, :]
    cosine, sine = jnp.cos(angles), jnp.sin(angles)
    keep, send = attention(
        pieces,
        me_ref,
        lengths,
        jnp.concatenate([cosine, cosine], axis=1),
        jnp.concatenate([-sine, sine], axis=1),
        w_qkv,
        w_out,
        k_cache,
        v_cache,
    )
    half = keep.astype(jnp.float32) + swap(send, "head", head_size, 1).astype(jnp.float32)
    half = half.astype(jnp.bfloat16)
    others = [swap(half, "head", head_size, j) for j in even if j]
    total = half.astype(jnp.float32).reshape(rows, head_size // 2, cols)
    for j, other in zip([j for j in even if j], others):
        other = other.reshape(rows, head_size // 2, cols)
        total = total + jnp.stack(
            [other[:, t ^ (j // 2)] for t in range(head_size // 2)], axis=1
        ).astype(jnp.float32)
    own_x = jnp.stack([pieces[j] for j in even], axis=1)
    resid = (own_x.astype(jnp.float32) + total).reshape(rows, head_size // 2 * cols)

    every = jnp.arange(head_size * experts_local, dtype=jnp.int32)
    matches = (expert_ids[:, :, None] == every[None, None, :]).astype(jnp.float32)
    shares = jnp.sum(route_weights[:, :, None] * matches, axis=1).astype(jnp.bfloat16)
    shares = jnp.pad(shares, ((0, 0), (0, -shares.shape[1] % LANES)))
    payload = jnp.concatenate([resid.astype(jnp.bfloat16), shares], axis=1)

    steps = range(2, req_size, 2)
    line = jnp.concatenate([payload] + [swap(payload, "req", req_size, k) for k in steps])
    mine = jnp.concatenate([line, swap(line, "req", req_size, 1)])
    other_states = swap(mine[:, : resid.shape[1]], "head", head_size, 1)
    weights = [by_expert(j, me_ref, w_in, head_size) for j in range(head_size)]
    w_down_flat = w_down.reshape(experts_local * units_local, width)
    units, send = experts_part(me_ref, mine, other_states, weights, w_down_flat)
    sent = swap(send, "head", head_size, 1)
    tokens = mine.shape[0]
    summed = down_part(me_ref, units, w_down_flat, head_size)
    summed = summed.astype(jnp.float32) + sent.astype(jnp.float32)
    summed = summed.astype(jnp.bfloat16).reshape(2, tokens // 2, head_size // 2, cols)
    total = summed[0, :, 0].astype(jnp.float32)
    for j in even:
        for k in range(2):
            if j or k:
                pairs = [
                    (r * head_size + h, (r ^ k) * head_size + (h ^ j))
                    for r in range(req_size)
                    for h in range(head_size)
                ]
                got = lax.ppermute(summed[k, :, j // 2], ("req", "head"), pairs)
                total = total + got.astype(jnp.float32)
    chunks = total.astype(jnp.bfloat16).reshape(req_size // 2, rows, cols)
    out = chunks[0].astype(jnp.float32)
    for k in steps:
        out = out + swap(chunks[k // 2], "req", req_size, k).astype(jnp.float32)
    return (out + resid[:, :cols]).astype(jnp.bfloat16)


def solution(mesh):
    in_specs = (
        P("req", "head"),
        P("req"),
        P("req", None),
        P("req", None),
        P(None, None, "head"),
        P("head", None),
        P("req", None, "head", None),
        P("req", None, "head", None),
        P(None, "head", "req"),
        P("head", "req", None),
    )
    out_specs = P("req", "head")
    return jax.shard_map(
        per_device, mesh=mesh, in_specs=in_specs, out_specs=out_specs, check_vma=False
    )
```

```python
import functools
import jax
import jax.numpy as jnp
from jax import lax
from jax.experimental import pallas as pl
from jax.experimental.pallas import tpu as pltpu
from jax.sharding import PartitionSpec as P

rope_theta = 50000.0
norm_eps = 1e-05
LANES = 128
SUBLANES = 8
CHUNK = 64
GROUP = 8
MASKED = -1e30


VMEM = pl.BlockSpec(memory_space=pltpu.VMEM)
SMEM = pl.BlockSpec(memory_space=pltpu.SMEM)
ANY = pl.BlockSpec(memory_space=pl.ANY)


def in_hbm(array):
    return pltpu.with_memory_space_constraint(array, pltpu.HBM)


def in_vmem(array):
    return pltpu.with_memory_space_constraint(array, pltpu.VMEM)


def attention_kernel(
    head_count, lengths_ref, me_ref, cos_ref, sin_ref, *refs
):
    pieces = refs[:head_count]
    (
        w_qkv_ref, w_out_ref, k_ref, v_ref, keep_ref, send_ref,
        w_qkv_s, w_out_s, k_s, v_s, query_s, key_s, value_s, attended_s,
        own_s, qkv_sem, out_sem, k_sem, v_sem, own_sem,
    ) = refs[head_count:]
    rows, cols = pieces[0].shape
    heads_local = cols // LANES
    chunk_rows = CHUNK * heads_local
    me = me_ref[0]

    def qkv_copy(c, j):
        first = pl.multiple_of((me ^ j) * cols, cols)
        return pltpu.make_async_copy(
            w_qkv_ref.at[c, pl.ds(first, cols)], w_qkv_s.at[c, j], qkv_sem.at[c, j]
        )

    def out_copy(j):
        first = pl.multiple_of((me ^ j) * cols, cols)
        return pltpu.make_async_copy(
            w_out_ref.at[:, pl.ds(first, cols)], w_out_s.at[j], out_sem.at[j]
        )

    def cache_copy(source, target, sem, r):
        used = pl.multiple_of((lengths_ref[r] + 7) // 8 * (8 * heads_local), 8 * heads_local)
        return pltpu.make_async_copy(
            source.at[r, pl.ds(0, used)], target.at[r, pl.ds(0, used)], sem.at[r]
        )

    own_copy = pltpu.make_async_copy(pieces[0], own_s, own_sem)
    own_copy.start()
    for c in range(3):
        for j in range(head_count):
            qkv_copy(c, j).start()

    @pl.loop(0, rows)
    def _(r):
        cache_copy(k_ref, k_s, k_sem, r).start()
        last = pl.multiple_of((lengths_ref[r] - 1) // CHUNK * chunk_rows, chunk_rows)
        v_s[r, pl.ds(last, chunk_rows)] = jnp.zeros((chunk_rows, LANES), jnp.bfloat16)
        cache_copy(v_ref, v_s, v_sem, r).start()

    for j in range(head_count):
        out_copy(j).start()

    own_copy.wait()
    states = [piece[...].astype(jnp.float32) for piece in (own_s, *pieces[1:])]
    square = sum(jnp.sum(state * state, axis=1, keepdims=True) for state in states)
    scale = lax.rsqrt(square / (cols * head_count) + norm_eps)
    normed = [(state * scale).astype(jnp.bfloat16) for state in states]
    cosine, sine = cos_ref[...], sin_ref[...]
    if heads_local < SUBLANES:
        query_s[...] = jnp.zeros_like(query_s)
        key_s[...] = jnp.zeros_like(key_s)
        value_s[...] = jnp.zeros_like(value_s)
    for c, target in enumerate((query_s, key_s, value_s)):
        projected = jnp.zeros((rows, cols), jnp.float32)
        for j in range(head_count):
            qkv_copy(c, j).wait()
            projected += jnp.dot(normed[j], w_qkv_s[c, j], preferred_element_type=jnp.float32)
        for h in range(heads_local):
            part = projected[:, h * LANES : (h + 1) * LANES]
            if c < 2:
                part = part * cosine + pltpu.roll(part, LANES // 2, 1) * sine
            target[:, h, :] = part.astype(jnp.bfloat16).astype(jnp.float32)

    column = lax.broadcasted_iota(jnp.int32, (SUBLANES, chunk_rows), 1)
    row = lax.broadcasted_iota(jnp.int32, (SUBLANES, chunk_rows), 0)
    same_head = column % heads_local == row
    score_scale = LANES**-0.5

    @pl.loop(0, rows // GROUP)
    def _(g):
        requests = [g * GROUP + i for i in range(GROUP)]
        lengths = [lengths_ref[r] for r in requests]
        queries = [query_s[r].astype(jnp.bfloat16) for r in requests]
        top = [
            jnp.sum(query_s[r] * key_s[r], axis=1, keepdims=True) * score_scale for r in requests
        ]
        total = [jnp.ones((SUBLANES, 1), jnp.float32)] * GROUP
        accum = [value_s[r] for r in requests]
        longest = functools.reduce(jnp.maximum, lengths)
        for r in requests:
            cache_copy(k_ref, k_s, k_sem, r).wait()
            cache_copy(v_ref, v_s, v_sem, r).wait()

        def step(c, carry):
            top, total, accum = carry
            starts = [
                pl.multiple_of(jnp.minimum(c, (n - 1) // CHUNK) * chunk_rows, chunk_rows)
                for n in lengths
            ]
            scores = [
                lax.dot_general(
                    queries[i],
                    k_s[r, pl.ds(starts[i], chunk_rows)],
                    (((1,), (1,)), ((), ())),
                    preferred_element_type=jnp.float32,
                )
                for i, r in enumerate(requests)
            ]
            scores = [
                jnp.where(
                    same_head & (column < (n - c * CHUNK) * heads_local), s * score_scale, MASKED
                )
                for n, s in zip(lengths, scores)
            ]
            new_top = [
                jnp.maximum(t, jnp.max(s, axis=1, keepdims=True)) for t, s in zip(top, scores)
            ]
            weights = [jnp.exp(s - t) for s, t in zip(scores, new_top)]
            fade = [jnp.exp(a - b) for a, b in zip(top, new_top)]
            total = [
                t * f + jnp.sum(w, axis=1, keepdims=True) for t, f, w in zip(total, fade, weights)
            ]
            accum = [
                a * f
                + jnp.dot(
                    w.astype(jnp.bfloat16),
                    v_s[r, pl.ds(starts[i], chunk_rows)],
                    preferred_element_type=jnp.float32,
                )
                for i, (r, a, f, w) in enumerate(zip(requests, accum, fade, weights))
            ]
            return new_top, total, accum

        top, total, accum = lax.fori_loop(
            0, (longest + CHUNK - 1) // CHUNK, step, (top, total, accum)
        )
        for r, t, a in zip(requests, total, accum):
            attended_s[r] = a / t

    attended = jnp.concatenate(
        [attended_s[:, h, :] for h in range(heads_local)], axis=1
    ).astype(jnp.bfloat16)
    for j in range(head_count):
        out_copy(j).wait()
        target = send_ref if j % 2 else keep_ref
        target[:, j // 2 * cols : (j // 2 + 1) * cols] = jnp.dot(
            attended, w_out_s[j], preferred_element_type=jnp.float32
        ).astype(jnp.bfloat16)


def attention(pieces, me, lengths, cosine, sine, w_qkv, w_out, k_cache, v_cache):
    head_count = len(pieces)
    rows, cols = pieces[0].shape
    cache_len, heads_local, head_dim = k_cache.shape[1:]
    flat = (rows, cache_len * heads_local, head_dim)
    half = jax.ShapeDtypeStruct((rows, head_count // 2 * cols), jnp.bfloat16)
    return pl.pallas_call(
        functools.partial(attention_kernel, head_count),
        out_shape=(half, half),
        in_specs=[SMEM, SMEM, VMEM, VMEM, ANY] + [VMEM] * (head_count - 1) + [ANY] * 4,
        out_specs=(VMEM, VMEM),
        scratch_shapes=[
            pltpu.VMEM((3, head_count, cols, cols), jnp.bfloat16),
            pltpu.VMEM((head_count, cols, cols), jnp.bfloat16),
            pltpu.VMEM(flat, jnp.bfloat16),
            pltpu.VMEM(flat, jnp.bfloat16),
        ]
        + [pltpu.VMEM((rows, SUBLANES, LANES), jnp.float32)] * 4
        + [
            pltpu.VMEM((rows, cols), jnp.bfloat16),
            pltpu.SemaphoreType.DMA((3, head_count)),
            pltpu.SemaphoreType.DMA((head_count,)),
            pltpu.SemaphoreType.DMA((rows,)),
            pltpu.SemaphoreType.DMA((rows,)),
            pltpu.SemaphoreType.DMA(()),
        ],
        compiler_params=pltpu.CompilerParams(vmem_limit_bytes=44 * 2**20),
        cost_estimate=pl.CostEstimate(
            flops=2 * rows * 4 * cols * head_count * cols,
            bytes_accessed=8 * cols * cols * head_count + 4 * rows * cache_len * cols // 2,
            transcendentals=0,
        ),
        name="attention",
    )(in_hbm(lengths), me, cosine, sine, in_hbm(pieces[0]), *pieces[1:], in_hbm(w_qkv), in_hbm(w_out), in_hbm(k_cache.reshape(flat)), in_hbm(v_cache.reshape(flat)))


RELAYOUT_ROWS = 128
RELAYOUT_STEP = 16

def relayout_kernel(js, me_ref, w_ref, *refs):
    out_ref, token_ref, in_s, in_sem = refs[-4:]
    token_ref[...] = jnp.zeros_like(token_ref)
    experts, _, cols, _ = out_ref.shape
    step = in_s.shape[1]
    per_block = cols // step
    copies = []
    for at, j in enumerate(js):
        base = (me_ref[0] ^ j) * cols
        for i in range(per_block):
            slot = at * per_block + i
            first = pl.multiple_of(base + i * step, step)
            copies.append(
                pltpu.make_async_copy(
                    w_ref.at[pl.ds(first, step)], in_s.at[slot], in_sem.at[slot]
                )
            )
    for copy in copies:
        copy.start()
    for slot, copy in enumerate(copies):
        j, i = js[slot // per_block], slot % per_block
        copy.wait()
        for s in range(step // RELAYOUT_STEP):
            part = in_s[slot, pl.ds(s * RELAYOUT_STEP, RELAYOUT_STEP)]
            out_ref[:, j, pl.ds(i * step + s * RELAYOUT_STEP, RELAYOUT_STEP), :] = jnp.swapaxes(
                part, 0, 1
            )


def by_expert(js, me, w_in, head_count, buffer, after):
    width, experts, columns = w_in.shape
    cols = width // head_count
    step = min(RELAYOUT_ROWS, cols)
    slots = len(js) * cols // step
    held = [] if buffer is None else [in_vmem(buffer)]
    return pl.pallas_call(
        functools.partial(relayout_kernel, js),
        out_shape=(
            pltpu.VMEM((experts, head_count, cols, columns), jnp.bfloat16),
            jax.ShapeDtypeStruct((SUBLANES, LANES), jnp.float32),
        ),
        in_specs=[SMEM, ANY] + [VMEM] * len(held) + [ANY],
        out_specs=(VMEM, VMEM),
        input_output_aliases={2: 0} if held else {},
        scratch_shapes=[
            pltpu.VMEM((slots, step, experts, columns), jnp.bfloat16),
            pltpu.SemaphoreType.DMA((slots,)),
        ],
        compiler_params=pltpu.CompilerParams(vmem_limit_bytes=16 * 2**20),
        cost_estimate=pl.CostEstimate(
            flops=0, bytes_accessed=4 * len(js) * cols * experts * columns, transcendentals=0
        ),
        name=f"by_expert_{js[0]}",
    )(me, in_hbm(w_in), *held, after)


def payload_kernel(head_count, *refs):
    blocks = head_count // 2
    pieces, (half_ref, *others), shares_ref = refs[:blocks], refs[blocks : 2 * blocks], refs[2 * blocks]
    payload_ref, resid_ref = refs[-2:]
    cols = pieces[0].shape[1]
    for t in range(blocks):
        total = pieces[t][...].astype(jnp.float32)
        for at, source in enumerate((half_ref, *others)):
            place = (t ^ at) * cols
            total += source[:, place : place + cols].astype(jnp.float32)
        payload_ref[:, t * cols : (t + 1) * cols] = total.astype(jnp.bfloat16)
        if t == 0:
            resid_ref[...] = total
    payload_ref[:, blocks * cols :] = shares_ref[...]


def payload_part(pieces, half, others, shares, after):
    blocks = len(pieces)
    rows, cols = pieces[0].shape
    return pl.pallas_call(
        functools.partial(payload_kernel, 2 * blocks),
        out_shape=(
            jax.ShapeDtypeStruct((rows, blocks * cols + shares.shape[1]), jnp.bfloat16),
            jax.ShapeDtypeStruct((rows, cols), jnp.float32),
        ),
        in_specs=[VMEM] * (2 * blocks + 1) + [ANY],
        out_specs=(VMEM, VMEM),
        name="payload",
    )(*pieces, half, *others, shares, after)


def stack_kernel(count, *refs):
    rows = refs[0].shape[0]
    for i in range(count):
        refs[-1][i * rows : (i + 1) * rows, :] = refs[i][...]


def stack_part(parts, after):
    rows, columns = parts[0].shape
    return pl.pallas_call(
        functools.partial(stack_kernel, len(parts)),
        out_shape=jax.ShapeDtypeStruct((len(parts) * rows, columns), jnp.bfloat16),
        in_specs=[VMEM] * len(parts) + [ANY],
        out_specs=VMEM,
        name="stack",
    )(*parts, after)


def down_copy(w_ref, scratch, sem, me, j, t):
    cols = scratch.shape[2]
    first = pl.multiple_of((me ^ j) * cols, cols)
    return pltpu.make_async_copy(w_ref.at[:, pl.ds(first, cols)], scratch.at[t], sem.at[t])


def experts_kernel(me_ref, mine_0, mine_1, other_0, other_1, w_ref, w_down_ref, *refs):
    units_ref, send_ref, states_s, down_s, down_sem = refs
    me = me_ref[0]
    experts, head_count, cols, columns = w_ref.shape
    blocks = head_count // 2
    for t in range(blocks):
        down_copy(w_down_ref, down_s, down_sem, me, 2 * t + 1, t).start()
    tokens = states_s.shape[0]
    square = []
    for at, pair in enumerate(((mine_0, other_0), (mine_1, other_1))):
        first = at * tokens // 2
        total = 0.0
        for j in range(head_count):
            part = pair[j % 2][:, j // 2 * cols : (j // 2 + 1) * cols]
            states_s[first : first + tokens // 2, j * cols : (j + 1) * cols] = part
            total += jnp.sum(jnp.square(part.astype(jnp.float32)), axis=1, keepdims=True)
        square.append(total)
    scale = lax.rsqrt(jnp.concatenate(square, axis=0) / (head_count * cols) + norm_eps)
    shares = jnp.concatenate([mine_0[:, blocks * cols :], mine_1[:, blocks * cols :]], axis=0)
    per_step = max(1, 2 * LANES // columns)
    first_half = lax.broadcasted_iota(jnp.int32, (tokens, LANES), 1) < LANES // 2
    source = lax.broadcasted_iota(jnp.int32, (LANES, LANES), 0)
    lane = lax.broadcasted_iota(jnp.int32, (LANES, LANES), 1)

    @pl.loop(0, experts // per_step, unroll=2)
    def _(p):
        states = states_s[...]
        products = [
            jnp.dot(
                states,
                w_ref[p * per_step + i].reshape(head_count * cols, columns),
                preferred_element_type=jnp.float32,
            )
            for i in range(per_step)
        ]
        product = products[0] if per_step == 1 else jnp.concatenate(products, axis=1)
        expert = me * experts + p * per_step + lane * per_step // LANES
        share = jnp.dot(
            shares, (source == expert).astype(jnp.bfloat16), preferred_element_type=jnp.float32
        )
        a, b = product[:, :LANES], product[:, LANES:]
        gate = jnp.where(first_half, a, pltpu.roll(b, LANES // 2, 1)) * scale
        upward = jnp.where(first_half, pltpu.roll(a, LANES // 2, 1), b) * scale
        units = share * (gate / (1.0 + jnp.exp(-gate)) * upward)
        units_ref[:, pl.ds(pl.multiple_of(p * LANES, LANES), LANES)] = units.astype(jnp.bfloat16)

    units = units_ref[...]
    for t in range(blocks):
        down_copy(w_down_ref, down_s, down_sem, me, 2 * t + 1, t).wait()
        send_ref[:, t * cols : (t + 1) * cols] = jnp.dot(
            units, down_s[t], preferred_element_type=jnp.float32
        ).astype(jnp.bfloat16)


def experts_part(me, mine, other, weights, w_down):
    experts, head_count, cols, columns = weights.shape
    tokens = 2 * mine[0].shape[0]
    total_units = w_down.shape[0]
    return pl.pallas_call(
        experts_kernel,
        out_shape=(
            jax.ShapeDtypeStruct((tokens, total_units), jnp.bfloat16),
            jax.ShapeDtypeStruct((tokens, head_count // 2 * cols), jnp.bfloat16),
        ),
        in_specs=[SMEM] + [VMEM] * 5 + [ANY],
        out_specs=(VMEM, VMEM),
        scratch_shapes=[
            pltpu.VMEM((tokens, head_count * cols), jnp.bfloat16),
            pltpu.VMEM((head_count // 2, total_units, cols), jnp.bfloat16),
            pltpu.SemaphoreType.DMA((head_count // 2,)),
        ],
        compiler_params=pltpu.CompilerParams(vmem_limit_bytes=20 * 2**20),
        cost_estimate=pl.CostEstimate(
            flops=2 * tokens * head_count * cols * experts * columns,
            bytes_accessed=2 * head_count * cols * experts * columns,
            transcendentals=0,
        ),
        name="experts",
    )(me, *mine, *other, in_vmem(weights), in_hbm(w_down))


def down_kernel(head_count, me_ref, units_ref, w_down_ref, keep_ref, down_s, down_sem):
    me = me_ref[0]
    cols = down_s.shape[2]
    blocks = head_count // 2
    for t in range(blocks):
        down_copy(w_down_ref, down_s, down_sem, me, 2 * t, t).start()
    units = units_ref[...]
    for t in range(blocks):
        down_copy(w_down_ref, down_s, down_sem, me, 2 * t, t).wait()
        keep_ref[:, t * cols : (t + 1) * cols] = jnp.dot(
            units, down_s[t], preferred_element_type=jnp.float32
        ).astype(jnp.bfloat16)


def down_part(me, units, w_down, head_count):
    tokens, total_units = units.shape
    cols = w_down.shape[1] // head_count
    return pl.pallas_call(
        functools.partial(down_kernel, head_count),
        out_shape=jax.ShapeDtypeStruct((tokens, head_count // 2 * cols), jnp.bfloat16),
        in_specs=[SMEM, VMEM, ANY],
        out_specs=VMEM,
        scratch_shapes=[
            pltpu.VMEM((head_count // 2, total_units, cols), jnp.bfloat16),
            pltpu.SemaphoreType.DMA((head_count // 2,)),
        ],
        compiler_params=pltpu.CompilerParams(vmem_limit_bytes=16 * 2**20),
        cost_estimate=pl.CostEstimate(
            flops=2 * tokens * total_units * head_count // 2 * cols,
            bytes_accessed=2 * total_units * head_count // 2 * cols,
            transcendentals=0,
        ),
        name="down",
    )(me, units, in_hbm(w_down))


def swap(value, axis, size, mask):
    return lax.ppermute(value, axis, [(i, i ^ mask) for i in range(size)])


def per_device(
    hidden, lengths, expert_ids, route_weights, w_qkv, w_out, k_cache, v_cache, w_in, w_down
):
    req_size = lax.axis_size("req")
    head_size = lax.axis_size("head")
    me = lax.axis_index("head")
    me_ref = me[None].astype(jnp.int32)
    rows, cols = hidden.shape
    experts_local, units_local, width = w_down.shape
    even = range(0, head_size, 2)

    pieces = [hidden] + [swap(hidden, "head", head_size, j) for j in range(1, head_size)]
    half_dim = k_cache.shape[3] // 2
    freqs = rope_theta ** (-jnp.arange(half_dim, dtype=jnp.float32) / half_dim)
    angles = lengths.astype(jnp.float32)[:, None] * freqs[None, :]
    cosine, sine = jnp.cos(angles), jnp.sin(angles)
    keep, send = attention(
        pieces,
        me_ref,
        lengths,
        jnp.concatenate([cosine, cosine], axis=1),
        jnp.concatenate([-sine, sine], axis=1),
        w_qkv,
        w_out,
        k_cache,
        v_cache,
    )
    half = keep.astype(jnp.float32) + swap(send, "head", head_size, 1).astype(jnp.float32)
    half = half.astype(jnp.bfloat16)
    others = [swap(half, "head", head_size, j) for j in even if j]
    buffer, token = by_expert((0,), me_ref, w_in, head_size, None, half)

    every = jnp.arange(head_size * experts_local, dtype=jnp.int32)
    matches = (expert_ids[:, :, None] == every[None, None, :]).astype(jnp.float32)
    shares = jnp.sum(route_weights[:, :, None] * matches, axis=1).astype(jnp.bfloat16)
    shares = jnp.pad(shares, ((0, 0), (0, -shares.shape[1] % LANES)))
    payload, resid = payload_part([pieces[j] for j in even], half, others, shares, token)

    steps = range(2, req_size, 2)
    line = [payload] + [swap(payload, "req", req_size, k) for k in steps]
    buffer, token = by_expert((1, 2), me_ref, w_in, head_size, buffer, payload)
    line = stack_part(line, token)
    crossed = swap(line, "req", req_size, 1)
    line_other = swap(line, "head", head_size, 1)
    rest = tuple(range(3, head_size))
    buffer, _ = by_expert(rest, me_ref, w_in, head_size, buffer, line)
    crossed_other = swap(crossed, "head", head_size, 1)
    w_down_flat = w_down.reshape(experts_local * units_local, width)
    units, send = experts_part(
        me_ref, (line, crossed), (line_other, crossed_other), buffer, w_down_flat
    )
    sent = swap(send, "head", head_size, 1)
    tokens = units.shape[0]
    summed = down_part(me_ref, units, w_down_flat, head_size)
    summed = summed.astype(jnp.float32) + sent.astype(jnp.float32)
    summed = summed.astype(jnp.bfloat16).reshape(2, tokens // 2, head_size // 2, cols)
    total = summed[0, :, 0].astype(jnp.float32)
    for j in even:
        for k in range(2):
            if j or k:
                pairs = [
                    (r * head_size + h, (r ^ k) * head_size + (h ^ j))
                    for r in range(req_size)
                    for h in range(head_size)
                ]
                got = lax.ppermute(summed[k, :, j // 2], ("req", "head"), pairs)
                total = total + got.astype(jnp.float32)
    chunks = total.astype(jnp.bfloat16).reshape(req_size // 2, rows, cols)
    out = chunks[0].astype(jnp.float32)
    for k in steps:
        out = out + swap(chunks[k // 2], "req", req_size, k).astype(jnp.float32)
    return (out + resid).astype(jnp.bfloat16)


def solution(mesh):
    in_specs = (
        P("req", "head"),
        P("req"),
        P("req", None),
        P("req", None),
        P(None, None, "head"),
        P("head", None),
        P("req", None, "head", None),
        P("req", None, "head", None),
        P(None, "head", "req"),
        P("head", "req", None),
    )
    out_specs = P("req", "head")
    return jax.shard_map(
        per_device, mesh=mesh, in_specs=in_specs, out_specs=out_specs, check_vma=False
    )
```

```python
import functools
import jax
import jax.numpy as jnp
from jax import lax
from jax.experimental import pallas as pl
from jax.experimental.pallas import tpu as pltpu
from jax.sharding import PartitionSpec as P

rope_theta = 50000.0
norm_eps = 1e-05
LANES = 128
SUBLANES = 8
CHUNK = 64
GROUP = 8
MASKED = -1e30


VMEM = pl.BlockSpec(memory_space=pltpu.VMEM)
SMEM = pl.BlockSpec(memory_space=pltpu.SMEM)
ANY = pl.BlockSpec(memory_space=pl.ANY)


def in_hbm(array):
    return pltpu.with_memory_space_constraint(array, pltpu.HBM)


def in_vmem(array):
    return pltpu.with_memory_space_constraint(array, pltpu.VMEM)


def attention_kernel(
    head_count, lengths_ref, me_ref, cos_ref, sin_ref, *refs
):
    pieces = refs[:head_count]
    (
        w_qkv_ref, w_out_ref, k_ref, v_ref, keep_ref, send_ref,
        w_qkv_s, w_out_s, k_s, v_s, query_s, key_s, value_s, attended_s,
        own_s, qkv_sem, out_sem, k_sem, v_sem, own_sem,
    ) = refs[head_count:]
    rows, cols = pieces[0].shape
    heads_local = cols // LANES
    chunk_rows = CHUNK * heads_local
    me = me_ref[0]

    def qkv_copy(c, j):
        first = pl.multiple_of((me ^ j) * cols, cols)
        return pltpu.make_async_copy(
            w_qkv_ref.at[c, pl.ds(first, cols)], w_qkv_s.at[c, j], qkv_sem.at[c, j]
        )

    def out_copy(j):
        first = pl.multiple_of((me ^ j) * cols, cols)
        return pltpu.make_async_copy(
            w_out_ref.at[:, pl.ds(first, cols)], w_out_s.at[j], out_sem.at[j]
        )

    def cache_copy(source, target, sem, r):
        used = pl.multiple_of((lengths_ref[r] + 7) // 8 * (8 * heads_local), 8 * heads_local)
        return pltpu.make_async_copy(
            source.at[r, pl.ds(0, used)], target.at[r, pl.ds(0, used)], sem.at[r]
        )

    own_copy = pltpu.make_async_copy(pieces[0], own_s, own_sem)
    own_copy.start()
    for c in range(3):
        for j in range(head_count):
            qkv_copy(c, j).start()

    @pl.loop(0, rows)
    def _(r):
        cache_copy(k_ref, k_s, k_sem, r).start()
        last = pl.multiple_of((lengths_ref[r] - 1) // CHUNK * chunk_rows, chunk_rows)
        v_s[r, pl.ds(last, chunk_rows)] = jnp.zeros((chunk_rows, LANES), jnp.bfloat16)
        cache_copy(v_ref, v_s, v_sem, r).start()

    for j in range(head_count):
        out_copy(j).start()

    own_copy.wait()
    states = [piece[...].astype(jnp.float32) for piece in (own_s, *pieces[1:])]
    square = sum(jnp.sum(state * state, axis=1, keepdims=True) for state in states)
    scale = lax.rsqrt(square / (cols * head_count) + norm_eps)
    normed = [(state * scale).astype(jnp.bfloat16) for state in states]
    cosine, sine = cos_ref[...], sin_ref[...]
    if heads_local < SUBLANES:
        query_s[...] = jnp.zeros_like(query_s)
        key_s[...] = jnp.zeros_like(key_s)
        value_s[...] = jnp.zeros_like(value_s)
    for c, target in enumerate((query_s, key_s, value_s)):
        projected = jnp.zeros((rows, cols), jnp.float32)
        for j in range(head_count):
            qkv_copy(c, j).wait()
            projected += jnp.dot(normed[j], w_qkv_s[c, j], preferred_element_type=jnp.float32)
        for h in range(heads_local):
            part = projected[:, h * LANES : (h + 1) * LANES]
            if c < 2:
                part = part * cosine + pltpu.roll(part, LANES // 2, 1) * sine
            target[:, h, :] = part.astype(jnp.bfloat16).astype(jnp.float32)

    column = lax.broadcasted_iota(jnp.int32, (SUBLANES, chunk_rows), 1)
    row = lax.broadcasted_iota(jnp.int32, (SUBLANES, chunk_rows), 0)
    same_head = column % heads_local == row
    score_scale = LANES**-0.5

    @pl.loop(0, rows // GROUP)
    def _(g):
        requests = [g * GROUP + i for i in range(GROUP)]
        lengths = [lengths_ref[r] for r in requests]
        queries = [query_s[r].astype(jnp.bfloat16) for r in requests]
        top = [
            jnp.sum(query_s[r] * key_s[r], axis=1, keepdims=True) * score_scale for r in requests
        ]
        total = [jnp.ones((SUBLANES, 1), jnp.float32)] * GROUP
        accum = [value_s[r] for r in requests]
        longest = functools.reduce(jnp.maximum, lengths)
        for r in requests:
            cache_copy(k_ref, k_s, k_sem, r).wait()
            cache_copy(v_ref, v_s, v_sem, r).wait()

        def step(c, carry):
            top, total, accum = carry
            starts = [
                pl.multiple_of(jnp.minimum(c, (n - 1) // CHUNK) * chunk_rows, chunk_rows)
                for n in lengths
            ]
            scores = [
                lax.dot_general(
                    queries[i],
                    k_s[r, pl.ds(starts[i], chunk_rows)],
                    (((1,), (1,)), ((), ())),
                    preferred_element_type=jnp.float32,
                )
                for i, r in enumerate(requests)
            ]
            scores = [
                jnp.where(
                    same_head & (column < (n - c * CHUNK) * heads_local), s * score_scale, MASKED
                )
                for n, s in zip(lengths, scores)
            ]
            new_top = [
                jnp.maximum(t, jnp.max(s, axis=1, keepdims=True)) for t, s in zip(top, scores)
            ]
            weights = [jnp.exp(s - t) for s, t in zip(scores, new_top)]
            fade = [jnp.exp(a - b) for a, b in zip(top, new_top)]
            total = [
                t * f + jnp.sum(w, axis=1, keepdims=True) for t, f, w in zip(total, fade, weights)
            ]
            accum = [
                a * f
                + jnp.dot(
                    w.astype(jnp.bfloat16),
                    v_s[r, pl.ds(starts[i], chunk_rows)],
                    preferred_element_type=jnp.float32,
                )
                for i, (r, a, f, w) in enumerate(zip(requests, accum, fade, weights))
            ]
            return new_top, total, accum

        top, total, accum = lax.fori_loop(
            0, (longest + CHUNK - 1) // CHUNK, step, (top, total, accum)
        )
        for r, t, a in zip(requests, total, accum):
            attended_s[r] = a / t

    attended = jnp.concatenate(
        [attended_s[:, h, :] for h in range(heads_local)], axis=1
    ).astype(jnp.bfloat16)
    for j in range(head_count):
        out_copy(j).wait()
        target = send_ref if j % 2 else keep_ref
        target[:, j // 2 * cols : (j // 2 + 1) * cols] = jnp.dot(
            attended, w_out_s[j], preferred_element_type=jnp.float32
        ).astype(jnp.bfloat16)


def attention(pieces, me, lengths, cosine, sine, w_qkv, w_out, k_cache, v_cache):
    head_count = len(pieces)
    rows, cols = pieces[0].shape
    cache_len, heads_local, head_dim = k_cache.shape[1:]
    flat = (rows, cache_len * heads_local, head_dim)
    half = jax.ShapeDtypeStruct((rows, head_count // 2 * cols), jnp.bfloat16)
    return pl.pallas_call(
        functools.partial(attention_kernel, head_count),
        out_shape=(half, half),
        in_specs=[SMEM, SMEM, VMEM, VMEM, ANY] + [VMEM] * (head_count - 1) + [ANY] * 4,
        out_specs=(VMEM, VMEM),
        scratch_shapes=[
            pltpu.VMEM((3, head_count, cols, cols), jnp.bfloat16),
            pltpu.VMEM((head_count, cols, cols), jnp.bfloat16),
            pltpu.VMEM(flat, jnp.bfloat16),
            pltpu.VMEM(flat, jnp.bfloat16),
        ]
        + [pltpu.VMEM((rows, SUBLANES, LANES), jnp.float32)] * 4
        + [
            pltpu.VMEM((rows, cols), jnp.bfloat16),
            pltpu.SemaphoreType.DMA((3, head_count)),
            pltpu.SemaphoreType.DMA((head_count,)),
            pltpu.SemaphoreType.DMA((rows,)),
            pltpu.SemaphoreType.DMA((rows,)),
            pltpu.SemaphoreType.DMA(()),
        ],
        compiler_params=pltpu.CompilerParams(vmem_limit_bytes=44 * 2**20),
        cost_estimate=pl.CostEstimate(
            flops=2 * rows * 4 * cols * head_count * cols,
            bytes_accessed=8 * cols * cols * head_count + 4 * rows * cache_len * cols // 2,
            transcendentals=0,
        ),
        name="attention",
    )(in_hbm(lengths), me, cosine, sine, in_hbm(pieces[0]), *pieces[1:], in_hbm(w_qkv), in_hbm(w_out), in_hbm(k_cache.reshape(flat)), in_hbm(v_cache.reshape(flat)))


RELAYOUT_ROWS = 128
RELAYOUT_STEP = 16

def relayout_kernel(js, me_ref, w_ref, *refs):
    out_ref, token_ref, in_s, in_sem = refs[-4:]
    token_ref[...] = jnp.zeros_like(token_ref)
    experts, _, cols, _ = out_ref.shape
    step = in_s.shape[1]
    per_block = cols // step
    copies = []
    for at, j in enumerate(js):
        base = (me_ref[0] ^ j) * cols
        for i in range(per_block):
            slot = at * per_block + i
            first = pl.multiple_of(base + i * step, step)
            copies.append(
                pltpu.make_async_copy(
                    w_ref.at[pl.ds(first, step)], in_s.at[slot], in_sem.at[slot]
                )
            )
    for copy in copies:
        copy.start()
    for slot, copy in enumerate(copies):
        j, i = js[slot // per_block], slot % per_block
        copy.wait()
        for s in range(step // RELAYOUT_STEP):
            part = in_s[slot, pl.ds(s * RELAYOUT_STEP, RELAYOUT_STEP)]
            out_ref[:, j, pl.ds(i * step + s * RELAYOUT_STEP, RELAYOUT_STEP), :] = jnp.swapaxes(
                part, 0, 1
            )


def by_expert(js, me, w_in, head_count, buffer, after):
    width, experts, columns = w_in.shape
    cols = width // head_count
    step = min(RELAYOUT_ROWS, cols)
    slots = len(js) * cols // step
    held = [] if buffer is None else [in_vmem(buffer)]
    return pl.pallas_call(
        functools.partial(relayout_kernel, js),
        out_shape=(
            pltpu.VMEM((experts, head_count, cols, columns), jnp.bfloat16),
            jax.ShapeDtypeStruct((SUBLANES, LANES), jnp.float32),
        ),
        in_specs=[SMEM, ANY] + [VMEM] * len(held) + [ANY],
        out_specs=(VMEM, VMEM),
        input_output_aliases={2: 0} if held else {},
        scratch_shapes=[
            pltpu.VMEM((slots, step, experts, columns), jnp.bfloat16),
            pltpu.SemaphoreType.DMA((slots,)),
        ],
        compiler_params=pltpu.CompilerParams(vmem_limit_bytes=16 * 2**20),
        cost_estimate=pl.CostEstimate(
            flops=0, bytes_accessed=4 * len(js) * cols * experts * columns, transcendentals=0
        ),
        name=f"by_expert_{js[0]}",
    )(me, in_hbm(w_in), *held, after)


def payload_kernel(head_count, *refs):
    blocks = head_count // 2
    pieces, (half_ref, *others), shares_ref = refs[:blocks], refs[blocks : 2 * blocks], refs[2 * blocks]
    payload_ref, resid_ref = refs[-2:]
    cols = pieces[0].shape[1]
    for t in range(blocks):
        total = pieces[t][...].astype(jnp.float32)
        for at, source in enumerate((half_ref, *others)):
            place = (t ^ at) * cols
            total += source[:, place : place + cols].astype(jnp.float32)
        payload_ref[:, t * cols : (t + 1) * cols] = total.astype(jnp.bfloat16)
        if t == 0:
            resid_ref[...] = total
    payload_ref[:, blocks * cols :] = shares_ref[...]


def payload_part(pieces, half, others, shares, after):
    blocks = len(pieces)
    rows, cols = pieces[0].shape
    return pl.pallas_call(
        functools.partial(payload_kernel, 2 * blocks),
        out_shape=(
            jax.ShapeDtypeStruct((rows, blocks * cols + shares.shape[1]), jnp.bfloat16),
            jax.ShapeDtypeStruct((rows, cols), jnp.float32),
        ),
        in_specs=[VMEM] * (2 * blocks + 1) + [ANY],
        out_specs=(VMEM, VMEM),
        compiler_params=pltpu.CompilerParams(vmem_limit_bytes=8 * 2**20),
        name="payload",
    )(*pieces, half, *others, shares, after)


def stack_kernel(count, *refs):
    rows = refs[0].shape[0]
    for i in range(count):
        refs[-1][i * rows : (i + 1) * rows, :] = refs[i][...]


def stack_part(parts, after):
    rows, columns = parts[0].shape
    return pl.pallas_call(
        functools.partial(stack_kernel, len(parts)),
        out_shape=jax.ShapeDtypeStruct((len(parts) * rows, columns), jnp.bfloat16),
        in_specs=[VMEM] * len(parts) + [ANY],
        out_specs=VMEM,
        compiler_params=pltpu.CompilerParams(vmem_limit_bytes=8 * 2**20),
        name="stack",
    )(*parts, after)


def down_copy(w_ref, scratch, sem, me, j, t):
    cols = scratch.shape[2]
    first = pl.multiple_of((me ^ j) * cols, cols)
    return pltpu.make_async_copy(w_ref.at[:, pl.ds(first, cols)], scratch.at[t], sem.at[t])


def experts_kernel(me_ref, mine_0, mine_1, other_0, other_1, w_ref, w_down_ref, *refs):
    units_ref, send_ref, states_s, down_s, down_sem = refs
    me = me_ref[0]
    experts, head_count, cols, columns = w_ref.shape
    blocks = head_count // 2
    for t in range(blocks):
        down_copy(w_down_ref, down_s, down_sem, me, 2 * t + 1, t).start()
    tokens = states_s.shape[0]
    square = []
    for at, pair in enumerate(((mine_0, other_0), (mine_1, other_1))):
        first = at * tokens // 2
        total = 0.0
        for j in range(head_count):
            part = pair[j % 2][:, j // 2 * cols : (j // 2 + 1) * cols]
            states_s[first : first + tokens // 2, j * cols : (j + 1) * cols] = part
            total += jnp.sum(jnp.square(part.astype(jnp.float32)), axis=1, keepdims=True)
        square.append(total)
    scale = lax.rsqrt(jnp.concatenate(square, axis=0) / (head_count * cols) + norm_eps)
    shares = jnp.concatenate([mine_0[:, blocks * cols :], mine_1[:, blocks * cols :]], axis=0)
    per_step = max(1, 2 * LANES // columns)
    first_half = lax.broadcasted_iota(jnp.int32, (tokens, LANES), 1) < LANES // 2
    source = lax.broadcasted_iota(jnp.int32, (LANES, LANES), 0)
    lane = lax.broadcasted_iota(jnp.int32, (LANES, LANES), 1)

    @pl.loop(0, experts // per_step, unroll=2)
    def _(p):
        states = states_s[...]
        products = [
            jnp.dot(
                states,
                w_ref[p * per_step + i].reshape(head_count * cols, columns),
                preferred_element_type=jnp.float32,
            )
            for i in range(per_step)
        ]
        product = products[0] if per_step == 1 else jnp.concatenate(products, axis=1)
        expert = me * experts + p * per_step + lane * per_step // LANES
        share = jnp.dot(
            shares, (source == expert).astype(jnp.bfloat16), preferred_element_type=jnp.float32
        )
        a, b = product[:, :LANES], product[:, LANES:]
        gate = jnp.where(first_half, a, pltpu.roll(b, LANES // 2, 1)) * scale
        upward = jnp.where(first_half, pltpu.roll(a, LANES // 2, 1), b) * scale
        units = share * (gate / (1.0 + jnp.exp(-gate)) * upward)
        units_ref[:, pl.ds(pl.multiple_of(p * LANES, LANES), LANES)] = units.astype(jnp.bfloat16)

    units = units_ref[...]
    for t in range(blocks):
        down_copy(w_down_ref, down_s, down_sem, me, 2 * t + 1, t).wait()
        send_ref[:, t * cols : (t + 1) * cols] = jnp.dot(
            units, down_s[t], preferred_element_type=jnp.float32
        ).astype(jnp.bfloat16)


def experts_part(me, mine, other, weights, w_down):
    experts, head_count, cols, columns = weights.shape
    tokens = 2 * mine[0].shape[0]
    total_units = w_down.shape[0]
    return pl.pallas_call(
        experts_kernel,
        out_shape=(
            jax.ShapeDtypeStruct((tokens, total_units), jnp.bfloat16),
            jax.ShapeDtypeStruct((tokens, head_count // 2 * cols), jnp.bfloat16),
        ),
        in_specs=[SMEM] + [VMEM] * 5 + [ANY],
        out_specs=(VMEM, VMEM),
        scratch_shapes=[
            pltpu.VMEM((tokens, head_count * cols), jnp.bfloat16),
            pltpu.VMEM((head_count // 2, total_units, cols), jnp.bfloat16),
            pltpu.SemaphoreType.DMA((head_count // 2,)),
        ],
        compiler_params=pltpu.CompilerParams(vmem_limit_bytes=20 * 2**20),
        cost_estimate=pl.CostEstimate(
            flops=2 * tokens * head_count * cols * experts * columns,
            bytes_accessed=2 * head_count * cols * experts * columns,
            transcendentals=0,
        ),
        name="experts",
    )(me, *mine, *other, in_vmem(weights), in_hbm(w_down))


def down_kernel(head_count, me_ref, units_ref, w_down_ref, keep_ref, down_s, down_sem):
    me = me_ref[0]
    cols = down_s.shape[2]
    blocks = head_count // 2
    for t in range(blocks):
        down_copy(w_down_ref, down_s, down_sem, me, 2 * t, t).start()
    units = units_ref[...]
    for t in range(blocks):
        down_copy(w_down_ref, down_s, down_sem, me, 2 * t, t).wait()
        keep_ref[:, t * cols : (t + 1) * cols] = jnp.dot(
            units, down_s[t], preferred_element_type=jnp.float32
        ).astype(jnp.bfloat16)


def down_part(me, units, w_down, head_count):
    tokens, total_units = units.shape
    cols = w_down.shape[1] // head_count
    return pl.pallas_call(
        functools.partial(down_kernel, head_count),
        out_shape=jax.ShapeDtypeStruct((tokens, head_count // 2 * cols), jnp.bfloat16),
        in_specs=[SMEM, VMEM, ANY],
        out_specs=VMEM,
        scratch_shapes=[
            pltpu.VMEM((head_count // 2, total_units, cols), jnp.bfloat16),
            pltpu.SemaphoreType.DMA((head_count // 2,)),
        ],
        compiler_params=pltpu.CompilerParams(vmem_limit_bytes=16 * 2**20),
        cost_estimate=pl.CostEstimate(
            flops=2 * tokens * total_units * head_count // 2 * cols,
            bytes_accessed=2 * total_units * head_count // 2 * cols,
            transcendentals=0,
        ),
        name="down",
    )(me, units, in_hbm(w_down))


def swap(value, axis, size, mask):
    return lax.ppermute(value, axis, [(i, i ^ mask) for i in range(size)])


def per_device(
    hidden, lengths, expert_ids, route_weights, w_qkv, w_out, k_cache, v_cache, w_in, w_down
):
    req_size = lax.axis_size("req")
    head_size = lax.axis_size("head")
    me = lax.axis_index("head")
    me_ref = me[None].astype(jnp.int32)
    rows, cols = hidden.shape
    experts_local, units_local, width = w_down.shape
    even = range(0, head_size, 2)

    pieces = [hidden] + [swap(hidden, "head", head_size, j) for j in range(1, head_size)]
    half_dim = k_cache.shape[3] // 2
    freqs = rope_theta ** (-jnp.arange(half_dim, dtype=jnp.float32) / half_dim)
    angles = lengths.astype(jnp.float32)[:, None] * freqs[None, :]
    cosine, sine = jnp.cos(angles), jnp.sin(angles)
    keep, send = attention(
        pieces,
        me_ref,
        lengths,
        jnp.concatenate([cosine, cosine], axis=1),
        jnp.concatenate([-sine, sine], axis=1),
        w_qkv,
        w_out,
        k_cache,
        v_cache,
    )
    half = keep.astype(jnp.float32) + swap(send, "head", head_size, 1).astype(jnp.float32)
    half = half.astype(jnp.bfloat16)
    others = [swap(half, "head", head_size, j) for j in even if j]
    buffer, token = by_expert((0,), me_ref, w_in, head_size, None, half)

    every = jnp.arange(head_size * experts_local, dtype=jnp.int32)
    matches = (expert_ids[:, :, None] == every[None, None, :]).astype(jnp.float32)
    shares = jnp.sum(route_weights[:, :, None] * matches, axis=1).astype(jnp.bfloat16)
    shares = jnp.pad(shares, ((0, 0), (0, -shares.shape[1] % LANES)))
    payload, resid = payload_part([pieces[j] for j in even], half, others, shares, token)

    steps = range(2, req_size, 2)
    line = [payload] + [swap(payload, "req", req_size, k) for k in steps]
    buffer, token = by_expert((1, 2), me_ref, w_in, head_size, buffer, payload)
    line = stack_part(line, token)
    crossed = swap(line, "req", req_size, 1)
    line_other = swap(line, "head", head_size, 1)
    rest = tuple(range(3, head_size))
    buffer, _ = by_expert(rest, me_ref, w_in, head_size, buffer, line)
    crossed_other = swap(crossed, "head", head_size, 1)
    w_down_flat = w_down.reshape(experts_local * units_local, width)
    units, send = experts_part(
        me_ref, (line, crossed), (line_other, crossed_other), buffer, w_down_flat
    )
    sent = swap(send, "head", head_size, 1)
    tokens = units.shape[0]
    summed = down_part(me_ref, units, w_down_flat, head_size)
    summed = summed.astype(jnp.float32) + sent.astype(jnp.float32)
    summed = summed.astype(jnp.bfloat16).reshape(2, tokens // 2, head_size // 2, cols)
    total = summed[0, :, 0].astype(jnp.float32)
    for j in even:
        for k in range(2):
            if j or k:
                pairs = [
                    (r * head_size + h, (r ^ k) * head_size + (h ^ j))
                    for r in range(req_size)
                    for h in range(head_size)
                ]
                got = lax.ppermute(summed[k, :, j // 2], ("req", "head"), pairs)
                total = total + got.astype(jnp.float32)
    chunks = total.astype(jnp.bfloat16).reshape(req_size // 2, rows, cols)
    out = chunks[0].astype(jnp.float32)
    for k in steps:
        out = out + swap(chunks[k // 2], "req", req_size, k).astype(jnp.float32)
    return (out + resid).astype(jnp.bfloat16)


def solution(mesh):
    in_specs = (
        P("req", "head"),
        P("req"),
        P("req", None),
        P("req", None),
        P(None, None, "head"),
        P("head", None),
        P("req", None, "head", None),
        P("req", None, "head", None),
        P(None, "head", "req"),
        P("head", "req", None),
    )
    out_specs = P("req", "head")
    return jax.shard_map(
        per_device, mesh=mesh, in_specs=in_specs, out_specs=out_specs, check_vma=False
    )
```

```python
import functools
import jax
import jax.numpy as jnp
from jax import lax
from jax.experimental import pallas as pl
from jax.experimental.pallas import tpu as pltpu
from jax.sharding import PartitionSpec as P

rope_theta = 50000.0
norm_eps = 1e-05
LANES = 128
SUBLANES = 8
CHUNK = 128
GROUP = 8
MASKED = -1e30


VMEM = pl.BlockSpec(memory_space=pltpu.VMEM)
SMEM = pl.BlockSpec(memory_space=pltpu.SMEM)
ANY = pl.BlockSpec(memory_space=pl.ANY)


def in_hbm(array):
    return pltpu.with_memory_space_constraint(array, pltpu.HBM)


def in_vmem(array):
    return pltpu.with_memory_space_constraint(array, pltpu.VMEM)


def used_rows(length, heads_local):
    return pl.multiple_of((length + 7) // 8 * (8 * heads_local), 8 * heads_local)


def fetch_kernel(lengths_ref, me_ref, own_ref, w_ref, own_out_ref, w_out_ref, blank_ref, sem, own_sem):
    head_count, cols = w_out_ref.shape[1:3]
    chunk_rows = CHUNK * cols // LANES
    me = me_ref[0]
    copies = [pltpu.make_async_copy(own_ref, own_out_ref, own_sem)]
    for c in range(w_ref.shape[0]):
        for j in range(head_count):
            first = pl.multiple_of((me ^ j) * cols, cols)
            copies.append(
                pltpu.make_async_copy(
                    w_ref.at[c, pl.ds(first, cols)], w_out_ref.at[c, j], sem.at[c, j]
                )
            )
    for copy in copies:
        copy.start()

    @pl.loop(0, blank_ref.shape[0])
    def _(r):
        last = pl.multiple_of((lengths_ref[r] - 1) // CHUNK * chunk_rows, chunk_rows)
        blank_ref[r, pl.ds(last, chunk_rows)] = jnp.zeros((chunk_rows, LANES), jnp.bfloat16)

    for copy in copies:
        copy.wait()


def fetch(me, lengths, hidden, w_qkv, v_shape, head_count):
    cols = w_qkv.shape[2]
    return pl.pallas_call(
        fetch_kernel,
        out_shape=(
            pltpu.VMEM(hidden.shape, jnp.bfloat16),
            pltpu.VMEM((w_qkv.shape[0], head_count, cols, cols), jnp.bfloat16),
            pltpu.VMEM(v_shape, jnp.bfloat16),
        ),
        in_specs=[SMEM, SMEM, ANY, ANY],
        out_specs=(VMEM, VMEM, VMEM),
        scratch_shapes=[
            pltpu.SemaphoreType.DMA((w_qkv.shape[0], head_count)),
            pltpu.SemaphoreType.DMA(()),
        ],
        compiler_params=pltpu.CompilerParams(vmem_limit_bytes=8 * 2**20),
        cost_estimate=pl.CostEstimate(
            flops=0, bytes_accessed=4 * w_qkv.size, transcendentals=0
        ),
        name="fetch",
    )(in_hbm(lengths), me, in_hbm(hidden), in_hbm(w_qkv))


def attention_kernel(head_count, lengths_ref, me_ref, cos_ref, sin_ref, *refs):
    pieces = refs[:head_count]
    (
        w_qkv_ref, _, w_out_ref, k_ref, v_ref, keep_ref, send_ref, v_s,
        w_out_s, k_s, query_s, key_s, value_s, attended_s, out_sem, k_sem, v_sem,
    ) = refs[head_count:]
    rows, cols = pieces[0].shape
    heads_local = cols // LANES
    chunk_rows = CHUNK * heads_local
    me = me_ref[0]

    def out_copy(j):
        first = pl.multiple_of((me ^ j) * cols, cols)
        return pltpu.make_async_copy(
            w_out_ref.at[:, pl.ds(first, cols)], w_out_s.at[j], out_sem.at[j]
        )

    def cache_copy(source, target, sem, r):
        used = used_rows(lengths_ref[r], heads_local)
        return pltpu.make_async_copy(
            source.at[r, pl.ds(0, used)], target.at[r, pl.ds(0, used)], sem.at[r]
        )

    @pl.loop(0, rows, unroll=4)
    def _(r):
        cache_copy(k_ref, k_s, k_sem, r).start()
        cache_copy(v_ref, v_s, v_sem, r).start()

    for j in range(head_count):
        out_copy(j).start()

    if heads_local < SUBLANES:
        query_s[...] = jnp.zeros_like(query_s)
        key_s[...] = jnp.zeros_like(key_s)
        value_s[...] = jnp.zeros_like(value_s)
    states = jnp.concatenate([piece[...] for piece in pieces], axis=1)
    square = jnp.sum(jnp.square(states.astype(jnp.float32)), axis=1, keepdims=True)
    scale = lax.rsqrt(square / (cols * head_count) + norm_eps)
    cosine, sine = cos_ref[...], sin_ref[...]
    for c, target in enumerate((query_s, key_s, value_s)):
        projected = scale * jnp.dot(
            states,
            w_qkv_ref[c].reshape(head_count * cols, cols),
            preferred_element_type=jnp.float32,
        )
        for h in range(heads_local):
            part = projected[:, h * LANES : (h + 1) * LANES]
            if c < 2:
                part = part * cosine + pltpu.roll(part, LANES // 2, 1) * sine
            target[:, h, :] = part.astype(jnp.bfloat16).astype(jnp.float32)

    column = lax.broadcasted_iota(jnp.int32, (2 * SUBLANES, chunk_rows), 1)
    row = lax.broadcasted_iota(jnp.int32, (2 * SUBLANES, chunk_rows), 0)
    same_head = column % heads_local == row % SUBLANES
    upper = row < SUBLANES
    score_scale = LANES**-0.5
    blank = jnp.zeros((SUBLANES, LANES), jnp.float32)

    def diagonal(a, b):
        return jnp.concatenate(
            [jnp.concatenate([a, blank], axis=1), jnp.concatenate([blank, b], axis=1)], axis=0
        )

    @pl.loop(0, rows // GROUP)
    def _(g):
        requests = [g * GROUP + i for i in range(GROUP)]
        pairs = list(zip(requests[::2], requests[1::2]))
        lengths = [lengths_ref[r] for r in requests]
        spans = list(zip(lengths[::2], lengths[1::2]))
        queries = [diagonal(query_s[a], query_s[b]).astype(jnp.bfloat16) for a, b in pairs]
        own = [
            jnp.sum(query_s[r] * key_s[r], axis=1, keepdims=True) * score_scale for r in requests
        ]
        own = [jnp.concatenate([a, b], axis=0) for a, b in zip(own[::2], own[1::2])]
        values = [diagonal(value_s[a], value_s[b]) for a, b in pairs]
        longest = functools.reduce(jnp.maximum, lengths)
        for r in requests:
            cache_copy(k_ref, k_s, k_sem, r).wait()
            cache_copy(v_ref, v_s, v_sem, r).wait()

        def with_chunks(count):
            def both(ref, c, pair, span):
                parts = []
                for r, length in zip(pair, span):
                    first = jnp.minimum(c, (length - 1) // CHUNK) * chunk_rows if c else 0
                    parts.append(ref[r, pl.ds(pl.multiple_of(first, chunk_rows), chunk_rows)])
                return jnp.concatenate(parts, axis=1)

            scores = [
                [
                    lax.dot_general(
                        query,
                        both(k_s, c, pair, span),
                        (((1,), (1,)), ((), ())),
                        preferred_element_type=jnp.float32,
                    )
                    for c in range(count)
                ]
                for query, pair, span in zip(queries, pairs, spans)
            ]
            limits = [
                jnp.where(upper, span[0] * heads_local, span[1] * heads_local) for span in spans
            ]
            scores = [
                [
                    jnp.where(
                        same_head & (column < limit - c * chunk_rows), score * score_scale, MASKED
                    )
                    for c, score in enumerate(parts)
                ]
                for limit, parts in zip(limits, scores)
            ]
            tops = [
                jnp.maximum(
                    mine, jnp.max(functools.reduce(jnp.maximum, parts), axis=1, keepdims=True)
                )
                for mine, parts in zip(own, scores)
            ]
            weights = [[jnp.exp(part - top) for part in parts] for top, parts in zip(tops, scores)]
            faded = [jnp.exp(mine - top) for mine, top in zip(own, tops)]
            totals = [
                fade + jnp.sum(functools.reduce(jnp.add, parts), axis=1, keepdims=True)
                for fade, parts in zip(faded, weights)
            ]
            sums = [
                fade * value
                + sum(
                    jnp.dot(
                        part.astype(jnp.bfloat16),
                        both(v_s, c, pair, span),
                        preferred_element_type=jnp.float32,
                    )
                    for c, part in enumerate(parts)
                )
                for pair, span, fade, value, parts in zip(pairs, spans, faded, values, weights)
            ]
            for (a, b), total, summed in zip(pairs, totals, sums):
                summed = summed / total
                attended_s[a] = summed[:SUBLANES, :LANES]
                attended_s[b] = summed[SUBLANES:, LANES:]

        for count in range(1, k_s.shape[1] // chunk_rows + 1):
            pl.when((longest + CHUNK - 1) // CHUNK == count)(
                functools.partial(with_chunks, count)
            )

    attended = jnp.concatenate(
        [attended_s[:, h, :] for h in range(heads_local)], axis=1
    ).astype(jnp.bfloat16)
    for j in range(head_count):
        out_copy(j).wait()
        target = send_ref if j % 2 else keep_ref
        target[:, j // 2 * cols : (j // 2 + 1) * cols] = jnp.dot(
            attended, w_out_s[j], preferred_element_type=jnp.float32
        ).astype(jnp.bfloat16)


def attention(pieces, me, lengths, cosine, sine, w_qkv, room, w_out, k_cache, v_cache):
    head_count = len(pieces)
    rows, cols = pieces[0].shape
    half = jax.ShapeDtypeStruct((rows, head_count // 2 * cols), jnp.bfloat16)
    return pl.pallas_call(
        functools.partial(attention_kernel, head_count),
        out_shape=(half, half, pltpu.VMEM(room.shape, jnp.bfloat16)),
        in_specs=[SMEM, SMEM] + [VMEM] * (head_count + 4) + [ANY] * 3,
        out_specs=(VMEM, VMEM, VMEM),
        input_output_aliases={head_count + 5: 2},
        scratch_shapes=[
            pltpu.VMEM((head_count, cols, cols), jnp.bfloat16),
            pltpu.VMEM(k_cache.shape, jnp.bfloat16),
        ]
        + [pltpu.VMEM((rows, SUBLANES, LANES), jnp.float32)] * 4
        + [
            pltpu.SemaphoreType.DMA((head_count,)),
            pltpu.SemaphoreType.DMA((rows,)),
            pltpu.SemaphoreType.DMA((rows,)),
        ],
        compiler_params=pltpu.CompilerParams(vmem_limit_bytes=20 * 2**20),
        cost_estimate=pl.CostEstimate(
            flops=2 * rows * 4 * cols * head_count * cols,
            bytes_accessed=2 * cols * cols * head_count + k_cache.size // 2,
            transcendentals=0,
        ),
        name="attention",
    )(
        in_hbm(lengths), me, cosine, sine, *map(in_vmem, pieces), in_vmem(w_qkv), in_vmem(room),
        in_hbm(w_out), in_hbm(k_cache), in_hbm(v_cache),
    )[:2]


RELAYOUT_ROWS = 128
RELAYOUT_STEP = 16

def relayout_kernel(js, me_ref, w_ref, *refs):
    out_ref, token_ref, in_s, in_sem = refs[-4:]
    token_ref[...] = jnp.zeros_like(token_ref)
    experts, _, cols, _ = out_ref.shape
    step = in_s.shape[1]
    per_block = cols // step
    copies = []
    for at, j in enumerate(js):
        base = (me_ref[0] ^ j) * cols
        for i in range(per_block):
            slot = at * per_block + i
            first = pl.multiple_of(base + i * step, step)
            copies.append(
                pltpu.make_async_copy(
                    w_ref.at[pl.ds(first, step)], in_s.at[slot], in_sem.at[slot]
                )
            )
    for copy in copies:
        copy.start()
    for slot, copy in enumerate(copies):
        j, i = js[slot // per_block], slot % per_block
        copy.wait()
        for s in range(step // RELAYOUT_STEP):
            part = in_s[slot, pl.ds(s * RELAYOUT_STEP, RELAYOUT_STEP)]
            out_ref[:, j, pl.ds(i * step + s * RELAYOUT_STEP, RELAYOUT_STEP), :] = jnp.swapaxes(
                part, 0, 1
            )


def by_expert(js, me, w_in, head_count, buffer, after):
    width, experts, columns = w_in.shape
    cols = width // head_count
    step = min(RELAYOUT_ROWS, cols)
    slots = len(js) * cols // step
    held = [] if buffer is None else [in_vmem(buffer)]
    return pl.pallas_call(
        functools.partial(relayout_kernel, js),
        out_shape=(
            pltpu.VMEM((experts, head_count, cols, columns), jnp.bfloat16),
            jax.ShapeDtypeStruct((SUBLANES, LANES), jnp.float32),
        ),
        in_specs=[SMEM, ANY] + [VMEM] * len(held) + [ANY],
        out_specs=(VMEM, VMEM),
        input_output_aliases={2: 0} if held else {},
        scratch_shapes=[
            pltpu.VMEM((slots, step, experts, columns), jnp.bfloat16),
            pltpu.SemaphoreType.DMA((slots,)),
        ],
        compiler_params=pltpu.CompilerParams(vmem_limit_bytes=16 * 2**20),
        cost_estimate=pl.CostEstimate(
            flops=0, bytes_accessed=4 * len(js) * cols * experts * columns, transcendentals=0
        ),
        name=f"by_expert_{js[0]}",
    )(me, in_hbm(w_in), *held, after)


def payload_kernel(head_count, *refs):
    blocks = head_count // 2
    pieces, (half_ref, *others), shares_ref = refs[:blocks], refs[blocks : 2 * blocks], refs[2 * blocks]
    payload_ref, resid_ref = refs[-2:]
    cols = pieces[0].shape[1]
    for t in range(blocks):
        total = pieces[t][...].astype(jnp.float32)
        for at, source in enumerate((half_ref, *others)):
            place = (t ^ at) * cols
            total += source[:, place : place + cols].astype(jnp.float32)
        payload_ref[:, t * cols : (t + 1) * cols] = total.astype(jnp.bfloat16)
        if t == 0:
            resid_ref[...] = total
    payload_ref[:, blocks * cols :] = shares_ref[...]


def payload_part(pieces, half, others, shares, after):
    blocks = len(pieces)
    rows, cols = pieces[0].shape
    return pl.pallas_call(
        functools.partial(payload_kernel, 2 * blocks),
        out_shape=(
            jax.ShapeDtypeStruct((rows, blocks * cols + shares.shape[1]), jnp.bfloat16),
            jax.ShapeDtypeStruct((rows, cols), jnp.float32),
        ),
        in_specs=[VMEM] * (2 * blocks + 1) + [ANY],
        out_specs=(VMEM, VMEM),
        compiler_params=pltpu.CompilerParams(vmem_limit_bytes=8 * 2**20),
        name="payload",
    )(*pieces, half, *others, shares, after)


def stack_kernel(count, *refs):
    rows = refs[0].shape[0]
    for i in range(count):
        refs[-1][i * rows : (i + 1) * rows, :] = refs[i][...]


def stack_part(parts, after):
    rows, columns = parts[0].shape
    return pl.pallas_call(
        functools.partial(stack_kernel, len(parts)),
        out_shape=jax.ShapeDtypeStruct((len(parts) * rows, columns), jnp.bfloat16),
        in_specs=[VMEM] * len(parts) + [ANY],
        out_specs=VMEM,
        compiler_params=pltpu.CompilerParams(vmem_limit_bytes=8 * 2**20),
        name="stack",
    )(*parts, after)


def fetch_down_kernel(me_ref, w_ref, _, out_ref, token_ref, sem):
    token_ref[...] = jnp.zeros_like(token_ref)
    head_count, _, cols = out_ref.shape
    copies = []
    for j in range(head_count):
        first = pl.multiple_of((me_ref[0] ^ j) * cols, cols)
        copies.append(
            pltpu.make_async_copy(w_ref.at[:, pl.ds(first, cols)], out_ref.at[j], sem.at[j])
        )
        copies[-1].start()
    for copy in copies:
        copy.wait()


def fetch_down(me, w_down, head_count, after):
    total_units, width = w_down.shape
    return pl.pallas_call(
        fetch_down_kernel,
        out_shape=(
            pltpu.VMEM((head_count, total_units, width // head_count), jnp.bfloat16),
            jax.ShapeDtypeStruct((SUBLANES, LANES), jnp.float32),
        ),
        in_specs=[SMEM, ANY, ANY],
        out_specs=(VMEM, VMEM),
        scratch_shapes=[pltpu.SemaphoreType.DMA((head_count,))],
        compiler_params=pltpu.CompilerParams(vmem_limit_bytes=8 * 2**20),
        cost_estimate=pl.CostEstimate(
            flops=0, bytes_accessed=4 * w_down.size, transcendentals=0
        ),
        name="fetch_down",
    )(me, in_hbm(w_down), after)


def down_blocks(units, w_ref, first, out_ref):
    cols = w_ref.shape[2]
    for t in range(w_ref.shape[0] // 2):
        out_ref[:, t * cols : (t + 1) * cols] = jnp.dot(
            units, w_ref[2 * t + first], preferred_element_type=jnp.float32
        ).astype(jnp.bfloat16)


def experts_kernel(me_ref, mine_ref, other_ref, w_ref, w_down_ref, _, units_ref, send_ref, states_s):
    me = me_ref[0]
    experts, head_count, cols, columns = w_ref.shape
    blocks = head_count // 2
    tokens = states_s.shape[0]
    square = 0.0
    for j in range(head_count):
        part = (mine_ref, other_ref)[j % 2][:, j // 2 * cols : (j // 2 + 1) * cols]
        states_s[:, j * cols : (j + 1) * cols] = part
        square += jnp.sum(jnp.square(part.astype(jnp.float32)), axis=1, keepdims=True)
    scale = lax.rsqrt(square / (head_count * cols) + norm_eps)
    shares = mine_ref[:, blocks * cols :]
    per_step = max(1, 2 * LANES // columns)
    first_half = lax.broadcasted_iota(jnp.int32, (tokens, LANES), 1) < LANES // 2
    source = lax.broadcasted_iota(jnp.int32, (LANES, LANES), 0)
    lane = lax.broadcasted_iota(jnp.int32, (LANES, LANES), 1)

    @pl.loop(0, experts // per_step, unroll=4)
    def _(p):
        states = states_s[...]
        products = [
            jnp.dot(
                states,
                w_ref[p * per_step + i].reshape(head_count * cols, columns),
                preferred_element_type=jnp.float32,
            )
            for i in range(per_step)
        ]
        product = products[0] if per_step == 1 else jnp.concatenate(products, axis=1)
        expert = me * experts + p * per_step + lane * per_step // LANES
        share = jnp.dot(
            shares, (source == expert).astype(jnp.bfloat16), preferred_element_type=jnp.float32
        )
        a, b = product[:, :LANES], product[:, LANES:]
        gate = jnp.where(first_half, a, pltpu.roll(b, LANES // 2, 1)) * scale
        upward = jnp.where(first_half, pltpu.roll(a, LANES // 2, 1), b) * scale
        units = share * (gate / (1.0 + jnp.exp(-gate)) * upward)
        units_ref[:, pl.ds(pl.multiple_of(p * LANES, LANES), LANES)] = units.astype(jnp.bfloat16)

    down_blocks(units_ref[...], w_down_ref, 1, send_ref)


def experts_part(me, mine, other, weights, w_down, after):
    experts, head_count, cols, columns = weights.shape
    tokens = mine.shape[0]
    total_units = w_down.shape[1]
    return pl.pallas_call(
        experts_kernel,
        out_shape=(
            jax.ShapeDtypeStruct((tokens, total_units), jnp.bfloat16),
            jax.ShapeDtypeStruct((tokens, head_count // 2 * cols), jnp.bfloat16),
        ),
        in_specs=[SMEM] + [VMEM] * 4 + [ANY],
        out_specs=(VMEM, VMEM),
        scratch_shapes=[pltpu.VMEM((tokens, head_count * cols), jnp.bfloat16)],
        compiler_params=pltpu.CompilerParams(vmem_limit_bytes=16 * 2**20),
        cost_estimate=pl.CostEstimate(
            flops=2 * tokens * head_count * cols * experts * columns,
            bytes_accessed=2 * head_count * cols * experts * columns,
            transcendentals=0,
        ),
        name="experts",
    )(me, mine, other, in_vmem(weights), in_vmem(w_down), after)


def down_kernel(units_ref, w_ref, keep_ref):
    down_blocks(units_ref[...], w_ref, 0, keep_ref)


def down_part(units, w_down):
    head_count, total_units, cols = w_down.shape
    tokens = units.shape[0]
    return pl.pallas_call(
        down_kernel,
        out_shape=jax.ShapeDtypeStruct((tokens, head_count // 2 * cols), jnp.bfloat16),
        in_specs=[VMEM, VMEM],
        out_specs=VMEM,
        compiler_params=pltpu.CompilerParams(vmem_limit_bytes=16 * 2**20),
        cost_estimate=pl.CostEstimate(
            flops=2 * tokens * total_units * head_count // 2 * cols,
            bytes_accessed=2 * total_units * head_count // 2 * cols,
            transcendentals=0,
        ),
        name="down",
    )(units, in_vmem(w_down))


def hold_kernel(value_ref, after_ref, out_ref):
    pass


def hold(value, after):
    return pl.pallas_call(
        hold_kernel,
        out_shape=jax.ShapeDtypeStruct(value.shape, value.dtype),
        in_specs=[ANY, ANY],
        out_specs=ANY,
        input_output_aliases={0: 0},
        compiler_params=pltpu.CompilerParams(vmem_limit_bytes=2**20),
        name="hold",
    )(value, after)


def sum_kernel(keep_ref, sent_ref, *outs):
    cols = outs[0].shape[1]
    for t, out in enumerate(outs):
        part = slice(t * cols, (t + 1) * cols)
        total = keep_ref[:, part].astype(jnp.float32) + sent_ref[:, part].astype(jnp.float32)
        out[...] = total.astype(out.dtype)


def sum_part(keep, sent, cols, first_type):
    tokens, columns = keep.shape
    blocks = columns // cols
    return pl.pallas_call(
        sum_kernel,
        out_shape=[
            jax.ShapeDtypeStruct((tokens, cols), jnp.bfloat16 if t else first_type)
            for t in range(blocks)
        ],
        in_specs=[VMEM, VMEM],
        out_specs=[VMEM] * blocks,
        compiler_params=pltpu.CompilerParams(vmem_limit_bytes=8 * 2**20),
        name="sum",
    )(keep, sent)


def swap(value, axis, size, mask):
    return lax.ppermute(value, axis, [(i, i ^ mask) for i in range(size)])


def per_device(
    hidden, lengths, expert_ids, route_weights, w_qkv, w_out, k_cache, v_cache, w_in, w_down
):
    req_size = lax.axis_size("req")
    head_size = lax.axis_size("head")
    me = lax.axis_index("head")
    me_ref = me[None].astype(jnp.int32)
    rows, cols = hidden.shape
    experts_local, units_local, width = w_down.shape
    even = range(0, head_size, 2)

    pieces = [hidden] + [swap(hidden, "head", head_size, j) for j in range(1, head_size)]
    half_dim = k_cache.shape[3] // 2
    freqs = rope_theta ** (-jnp.arange(half_dim, dtype=jnp.float32) / half_dim)
    angles = lengths.astype(jnp.float32)[:, None] * freqs[None, :]
    cosine, sine = jnp.cos(angles), jnp.sin(angles)
    flat = (rows, k_cache.shape[1] * k_cache.shape[2], k_cache.shape[3])
    own, w_near, room = fetch(me_ref, lengths, hidden, w_qkv, flat, head_size)
    keep, send = attention(
        [own] + pieces[1:],
        me_ref,
        lengths,
        jnp.concatenate([cosine, cosine], axis=1),
        jnp.concatenate([-sine, sine], axis=1),
        w_near,
        room,
        w_out,
        k_cache.reshape(flat),
        v_cache.reshape(flat),
    )
    half = keep.astype(jnp.float32) + swap(send, "head", head_size, 1).astype(jnp.float32)
    half = half.astype(jnp.bfloat16)
    others = [swap(half, "head", head_size, j) for j in even if j]
    early, late = range(head_size // 2), range(head_size // 2, head_size)
    buffer, token = by_expert(tuple(early), me_ref, w_in, head_size, None, half)

    every = jnp.arange(head_size * experts_local, dtype=jnp.int32)
    matches = (expert_ids[:, :, None] == every[None, None, :]).astype(jnp.float32)
    shares = jnp.sum(route_weights[:, :, None] * matches, axis=1).astype(jnp.bfloat16)
    shares = jnp.pad(shares, ((0, 0), (0, -shares.shape[1] % LANES)))
    payload, resid = payload_part([pieces[j] for j in even], half, others, shares, token)

    steps = range(2, req_size, 2)
    line = [payload] + [swap(payload, "req", req_size, k) for k in steps]
    w_down_flat = w_down.reshape(experts_local * units_local, width)
    buffer, token = by_expert(tuple(late), me_ref, w_in, head_size, buffer, payload)
    w_down_near, token = fetch_down(me_ref, w_down_flat, head_size, token)
    line = stack_part(line, token)
    crossed = swap(line, "req", req_size, 1)
    line_other = swap(line, "head", head_size, 1)
    units, send = experts_part(me_ref, line, line_other, buffer, w_down_near, token)
    crossed = hold(crossed, send)
    crossed_other = swap(crossed, "head", head_size, 1)
    keep = down_part(units, w_down_near)
    line_sums = sum_part(keep, swap(send, "head", head_size, 1), cols, jnp.float32)
    total = line_sums[0]
    got = [swap(line_sums[j // 2], "head", head_size, j) for j in even if j]
    units, send = experts_part(me_ref, crossed, crossed_other, buffer, w_down_near, line_sums[-1])
    keep = down_part(units, w_down_near)
    crossed_sums = sum_part(keep, swap(send, "head", head_size, 1), cols, jnp.bfloat16)
    for j in even:
        pairs = [
            (r * head_size + h, (r ^ 1) * head_size + (h ^ j))
            for r in range(req_size)
            for h in range(head_size)
        ]
        got.append(lax.ppermute(crossed_sums[j // 2], ("req", "head"), pairs))
    for part in got:
        total = total + part.astype(jnp.float32)
    chunks = total.astype(jnp.bfloat16).reshape(req_size // 2, rows, cols)
    out = chunks[0].astype(jnp.float32)
    for k in steps:
        out = out + swap(chunks[k // 2], "req", req_size, k).astype(jnp.float32)
    return (out + resid).astype(jnp.bfloat16)


def solution(mesh):
    in_specs = (
        P("req", "head"),
        P("req"),
        P("req", None),
        P("req", None),
        P(None, None, "head"),
        P("head", None),
        P("req", None, "head", None),
        P("req", None, "head", None),
        P(None, "head", "req"),
        P("head", "req", None),
    )
    out_specs = P("req", "head")
    return jax.shard_map(
        per_device, mesh=mesh, in_specs=in_specs, out_specs=out_specs, check_vma=False
    )
```

```python
import functools
import jax
import jax.numpy as jnp
from jax import lax
from jax.experimental import pallas as pl
from jax.experimental.pallas import tpu as pltpu
from jax.sharding import PartitionSpec as P

rope_theta = 50000.0
norm_eps = 1e-05
LANES = 128
SUBLANES = 8
CHUNK = 128
GROUP = 8
MASKED = -1e30


VMEM = pl.BlockSpec(memory_space=pltpu.VMEM)
SMEM = pl.BlockSpec(memory_space=pltpu.SMEM)
ANY = pl.BlockSpec(memory_space=pl.ANY)


def in_hbm(array):
    return pltpu.with_memory_space_constraint(array, pltpu.HBM)


def in_vmem(array):
    return pltpu.with_memory_space_constraint(array, pltpu.VMEM)


def used_rows(length, heads_local):
    return pl.multiple_of((length + 7) // 8 * (8 * heads_local), 8 * heads_local)


def fetch_kernel(
    lengths_ref, me_ref, freqs_ref, own_ref, w_ref,
    own_out_ref, w_out_ref, blank_ref, cos_ref, sin_ref, angle_s, sem, own_sem,
):
    head_count, cols = w_out_ref.shape[1:3]
    chunk_rows = CHUNK * cols // LANES
    me = me_ref[0]
    copies = [pltpu.make_async_copy(own_ref, own_out_ref, own_sem)]
    for c in range(w_ref.shape[0]):
        for j in range(head_count):
            first = pl.multiple_of((me ^ j) * cols, cols)
            copies.append(
                pltpu.make_async_copy(
                    w_ref.at[c, pl.ds(first, cols)], w_out_ref.at[c, j], sem.at[c, j]
                )
            )
    for copy in copies:
        copy.start()

    @pl.loop(0, blank_ref.shape[0])
    def _(r):
        last = pl.multiple_of((lengths_ref[r] - 1) // CHUNK * chunk_rows, chunk_rows)
        blank_ref[r, pl.ds(last, chunk_rows)] = jnp.zeros((chunk_rows, LANES), jnp.bfloat16)
        angle_s[pl.ds(r, 1), :] = lengths_ref[r].astype(jnp.float32) * freqs_ref[...]

    cos_ref[...] = jnp.cos(angle_s[...])
    lane = lax.broadcasted_iota(jnp.int32, sin_ref.shape, 1)
    sine = jnp.sin(angle_s[...])
    sin_ref[...] = jnp.where(lane < LANES // 2, -sine, sine)
    for copy in copies:
        copy.wait()


def fetch(me, lengths, hidden, w_qkv, v_shape, head_count):
    cols = w_qkv.shape[2]
    rows = hidden.shape[0]
    exponents = jnp.arange(LANES, dtype=jnp.float32) % (LANES // 2) / (LANES // 2)
    freqs = (rope_theta**-exponents)[None, :]
    return pl.pallas_call(
        fetch_kernel,
        out_shape=(
            pltpu.VMEM(hidden.shape, jnp.bfloat16),
            pltpu.VMEM((w_qkv.shape[0], head_count, cols, cols), jnp.bfloat16),
            pltpu.VMEM(v_shape, jnp.bfloat16),
            pltpu.VMEM((rows, LANES), jnp.float32),
            pltpu.VMEM((rows, LANES), jnp.float32),
        ),
        in_specs=[SMEM, SMEM, VMEM, ANY, ANY],
        out_specs=[VMEM] * 5,
        scratch_shapes=[
            pltpu.VMEM((rows, LANES), jnp.float32),
            pltpu.SemaphoreType.DMA((w_qkv.shape[0], head_count)),
            pltpu.SemaphoreType.DMA(()),
        ],
        compiler_params=pltpu.CompilerParams(vmem_limit_bytes=8 * 2**20),
        cost_estimate=pl.CostEstimate(
            flops=0, bytes_accessed=4 * w_qkv.size, transcendentals=0
        ),
        name="fetch",
    )(in_hbm(lengths), me, freqs, in_hbm(hidden), in_hbm(w_qkv))


def attention_kernel(head_count, lengths_ref, me_ref, cos_ref, sin_ref, *refs):
    pieces = refs[:head_count]
    (
        w_qkv_ref, _, w_out_ref, k_ref, v_ref, keep_ref, send_ref, v_s,
        w_out_s, k_s, query_s, key_s, value_s, attended_s, out_sem, k_sem, v_sem,
    ) = refs[head_count:]
    rows, cols = pieces[0].shape
    heads_local = cols // LANES
    chunk_rows = CHUNK * heads_local
    me = me_ref[0]

    def out_copy(j):
        first = pl.multiple_of((me ^ j) * cols, cols)
        return pltpu.make_async_copy(
            w_out_ref.at[:, pl.ds(first, cols)], w_out_s.at[j], out_sem.at[j]
        )

    def cache_copy(source, target, sem, r):
        used = used_rows(lengths_ref[r], heads_local)
        return pltpu.make_async_copy(
            source.at[r, pl.ds(0, used)], target.at[r, pl.ds(0, used)], sem.at[r]
        )

    @pl.loop(0, rows, unroll=4)
    def _(r):
        cache_copy(k_ref, k_s, k_sem, r).start()
        cache_copy(v_ref, v_s, v_sem, r).start()

    for j in range(head_count):
        out_copy(j).start()

    if heads_local < SUBLANES:
        query_s[...] = jnp.zeros_like(query_s)
        key_s[...] = jnp.zeros_like(key_s)
        value_s[...] = jnp.zeros_like(value_s)
    states = jnp.concatenate([piece[...] for piece in pieces], axis=1)
    square = jnp.sum(jnp.square(states.astype(jnp.float32)), axis=1, keepdims=True)
    scale = lax.rsqrt(square / (cols * head_count) + norm_eps)
    cosine, sine = cos_ref[...], sin_ref[...]
    for c, target in enumerate((query_s, key_s, value_s)):
        projected = scale * jnp.dot(
            states,
            w_qkv_ref[c].reshape(head_count * cols, cols),
            preferred_element_type=jnp.float32,
        )
        for h in range(heads_local):
            part = projected[:, h * LANES : (h + 1) * LANES]
            if c < 2:
                part = part * cosine + pltpu.roll(part, LANES // 2, 1) * sine
            target[:, h, :] = part.astype(jnp.bfloat16).astype(jnp.float32)

    column = lax.broadcasted_iota(jnp.int32, (2 * SUBLANES, chunk_rows), 1)
    row = lax.broadcasted_iota(jnp.int32, (2 * SUBLANES, chunk_rows), 0)
    same_head = column % heads_local == row % SUBLANES
    upper = row < SUBLANES
    score_scale = LANES**-0.5
    blank = jnp.zeros((SUBLANES, LANES), jnp.float32)

    def diagonal(a, b):
        return jnp.concatenate(
            [jnp.concatenate([a, blank], axis=1), jnp.concatenate([blank, b], axis=1)], axis=0
        )

    @pl.loop(0, rows // GROUP)
    def _(g):
        requests = [g * GROUP + i for i in range(GROUP)]
        pairs = list(zip(requests[::2], requests[1::2]))
        lengths = [lengths_ref[r] for r in requests]
        spans = list(zip(lengths[::2], lengths[1::2]))
        queries = [diagonal(query_s[a], query_s[b]).astype(jnp.bfloat16) for a, b in pairs]
        own = [
            jnp.sum(query_s[r] * key_s[r], axis=1, keepdims=True) * score_scale for r in requests
        ]
        own = [jnp.concatenate([a, b], axis=0) for a, b in zip(own[::2], own[1::2])]
        values = [diagonal(value_s[a], value_s[b]) for a, b in pairs]
        longest = functools.reduce(jnp.maximum, lengths)
        for r in requests:
            cache_copy(k_ref, k_s, k_sem, r).wait()
            cache_copy(v_ref, v_s, v_sem, r).wait()

        def with_chunks(count):
            def both(ref, c, pair, span):
                parts = []
                for r, length in zip(pair, span):
                    first = jnp.minimum(c, (length - 1) // CHUNK) * chunk_rows if c else 0
                    parts.append(ref[r, pl.ds(pl.multiple_of(first, chunk_rows), chunk_rows)])
                return jnp.concatenate(parts, axis=1)

            scores = [
                [
                    lax.dot_general(
                        query,
                        both(k_s, c, pair, span),
                        (((1,), (1,)), ((), ())),
                        preferred_element_type=jnp.float32,
                    )
                    for c in range(count)
                ]
                for query, pair, span in zip(queries, pairs, spans)
            ]
            limits = [
                jnp.where(upper, span[0] * heads_local, span[1] * heads_local) for span in spans
            ]
            scores = [
                [
                    jnp.where(
                        same_head & (column < limit - c * chunk_rows), score * score_scale, MASKED
                    )
                    for c, score in enumerate(parts)
                ]
                for limit, parts in zip(limits, scores)
            ]
            tops = [
                jnp.maximum(
                    mine, jnp.max(functools.reduce(jnp.maximum, parts), axis=1, keepdims=True)
                )
                for mine, parts in zip(own, scores)
            ]
            weights = [[jnp.exp(part - top) for part in parts] for top, parts in zip(tops, scores)]
            faded = [jnp.exp(mine - top) for mine, top in zip(own, tops)]
            totals = [
                fade + jnp.sum(functools.reduce(jnp.add, parts), axis=1, keepdims=True)
                for fade, parts in zip(faded, weights)
            ]
            sums = [
                fade * value
                + sum(
                    jnp.dot(
                        part.astype(jnp.bfloat16),
                        both(v_s, c, pair, span),
                        preferred_element_type=jnp.float32,
                    )
                    for c, part in enumerate(parts)
                )
                for pair, span, fade, value, parts in zip(pairs, spans, faded, values, weights)
            ]
            for (a, b), total, summed in zip(pairs, totals, sums):
                summed = summed / total
                attended_s[a] = summed[:SUBLANES, :LANES]
                attended_s[b] = summed[SUBLANES:, LANES:]

        for count in range(1, k_s.shape[1] // chunk_rows + 1):
            pl.when((longest + CHUNK - 1) // CHUNK == count)(
                functools.partial(with_chunks, count)
            )

    attended = jnp.concatenate(
        [attended_s[:, h, :] for h in range(heads_local)], axis=1
    ).astype(jnp.bfloat16)
    for j in range(head_count):
        out_copy(j).wait()
        target = send_ref if j % 2 else keep_ref
        target[:, j // 2 * cols : (j // 2 + 1) * cols] = jnp.dot(
            attended, w_out_s[j], preferred_element_type=jnp.float32
        ).astype(jnp.bfloat16)


def attention(pieces, me, lengths, cosine, sine, w_qkv, room, w_out, k_cache, v_cache):
    head_count = len(pieces)
    rows, cols = pieces[0].shape
    half = jax.ShapeDtypeStruct((rows, head_count // 2 * cols), jnp.bfloat16)
    return pl.pallas_call(
        functools.partial(attention_kernel, head_count),
        out_shape=(half, half, pltpu.VMEM(room.shape, jnp.bfloat16)),
        in_specs=[SMEM, SMEM] + [VMEM] * (head_count + 4) + [ANY] * 3,
        out_specs=(VMEM, VMEM, VMEM),
        input_output_aliases={head_count + 5: 2},
        scratch_shapes=[
            pltpu.VMEM((head_count, cols, cols), jnp.bfloat16),
            pltpu.VMEM(k_cache.shape, jnp.bfloat16),
        ]
        + [pltpu.VMEM((rows, SUBLANES, LANES), jnp.float32)] * 4
        + [
            pltpu.SemaphoreType.DMA((head_count,)),
            pltpu.SemaphoreType.DMA((rows,)),
            pltpu.SemaphoreType.DMA((rows,)),
        ],
        compiler_params=pltpu.CompilerParams(vmem_limit_bytes=20 * 2**20),
        cost_estimate=pl.CostEstimate(
            flops=2 * rows * 4 * cols * head_count * cols,
            bytes_accessed=2 * cols * cols * head_count + k_cache.size // 2,
            transcendentals=0,
        ),
        name="attention",
    )(
        in_hbm(lengths), me, cosine, sine, *map(in_vmem, pieces), in_vmem(w_qkv), in_vmem(room),
        in_hbm(w_out), in_hbm(k_cache), in_hbm(v_cache),
    )[:2]


RELAYOUT_ROWS = 128
RELAYOUT_STEP = 16

def slot_of(j, head_count):
    return j // 2 + j % 2 * (head_count // 2)


def relayout_kernel(js, me_ref, w_ref, *refs):
    out_ref, token_ref, in_s, in_sem = refs[-4:]
    token_ref[...] = jnp.zeros_like(token_ref)
    experts, head_count, cols, _ = out_ref.shape
    step = in_s.shape[1]
    per_block = cols // step
    copies = []
    for at, j in enumerate(js):
        base = (me_ref[0] ^ j) * cols
        for i in range(per_block):
            slot = at * per_block + i
            first = pl.multiple_of(base + i * step, step)
            copies.append(
                pltpu.make_async_copy(
                    w_ref.at[pl.ds(first, step)], in_s.at[slot], in_sem.at[slot]
                )
            )
    for copy in copies:
        copy.start()
    for slot, copy in enumerate(copies):
        j, i = js[slot // per_block], slot % per_block
        copy.wait()
        for s in range(step // RELAYOUT_STEP):
            part = in_s[slot, pl.ds(s * RELAYOUT_STEP, RELAYOUT_STEP)]
            out_ref[:, slot_of(j, head_count), pl.ds(i * step + s * RELAYOUT_STEP, RELAYOUT_STEP), :] = jnp.swapaxes(
                part, 0, 1
            )


def by_expert(js, me, w_in, head_count, buffer, after):
    width, experts, columns = w_in.shape
    cols = width // head_count
    step = min(RELAYOUT_ROWS, cols)
    slots = len(js) * cols // step
    held = [] if buffer is None else [in_vmem(buffer)]
    return pl.pallas_call(
        functools.partial(relayout_kernel, js),
        out_shape=(
            pltpu.VMEM((experts, head_count, cols, columns), jnp.bfloat16),
            jax.ShapeDtypeStruct((SUBLANES, LANES), jnp.float32),
        ),
        in_specs=[SMEM, ANY] + [VMEM] * len(held) + [ANY],
        out_specs=(VMEM, VMEM),
        input_output_aliases={2: 0} if held else {},
        scratch_shapes=[
            pltpu.VMEM((slots, step, experts, columns), jnp.bfloat16),
            pltpu.SemaphoreType.DMA((slots,)),
        ],
        compiler_params=pltpu.CompilerParams(vmem_limit_bytes=16 * 2**20),
        cost_estimate=pl.CostEstimate(
            flops=0, bytes_accessed=4 * len(js) * cols * experts * columns, transcendentals=0
        ),
        name=f"by_expert_{js[0]}",
    )(me, in_hbm(w_in), *held, after)


def payload_kernel(head_count, *refs):
    blocks = head_count // 2
    pieces, (half_ref, *others), shares_ref = refs[:blocks], refs[blocks : 2 * blocks], refs[2 * blocks]
    payload_ref, resid_ref = refs[-2:]
    cols = pieces[0].shape[1]
    for t in range(blocks):
        total = pieces[t][...].astype(jnp.float32)
        for at, source in enumerate((half_ref, *others)):
            place = (t ^ at) * cols
            total += source[:, place : place + cols].astype(jnp.float32)
        payload_ref[:, t * cols : (t + 1) * cols] = total.astype(jnp.bfloat16)
        if t == 0:
            resid_ref[...] = total
    payload_ref[:, blocks * cols :] = shares_ref[...]


def payload_part(pieces, half, others, shares, after):
    blocks = len(pieces)
    rows, cols = pieces[0].shape
    return pl.pallas_call(
        functools.partial(payload_kernel, 2 * blocks),
        out_shape=(
            jax.ShapeDtypeStruct((rows, blocks * cols + shares.shape[1]), jnp.bfloat16),
            jax.ShapeDtypeStruct((rows, cols), jnp.float32),
        ),
        in_specs=[VMEM] * (2 * blocks + 1) + [ANY],
        out_specs=(VMEM, VMEM),
        compiler_params=pltpu.CompilerParams(vmem_limit_bytes=8 * 2**20),
        name="payload",
    )(*pieces, half, *others, shares, after)


def stack_kernel(count, *refs):
    rows = refs[0].shape[0]
    for i in range(count):
        refs[-1][i * rows : (i + 1) * rows, :] = refs[i][...]


def stack_part(parts, after):
    rows, columns = parts[0].shape
    return pl.pallas_call(
        functools.partial(stack_kernel, len(parts)),
        out_shape=jax.ShapeDtypeStruct((len(parts) * rows, columns), jnp.bfloat16),
        in_specs=[VMEM] * len(parts) + [ANY],
        out_specs=VMEM,
        compiler_params=pltpu.CompilerParams(vmem_limit_bytes=8 * 2**20),
        name="stack",
    )(*parts, after)


def fetch_down_kernel(me_ref, w_ref, _, out_ref, token_ref, sem):
    token_ref[...] = jnp.zeros_like(token_ref)
    head_count, _, cols = out_ref.shape
    copies = []
    for j in range(head_count):
        first = pl.multiple_of((me_ref[0] ^ j) * cols, cols)
        copies.append(
            pltpu.make_async_copy(w_ref.at[:, pl.ds(first, cols)], out_ref.at[j], sem.at[j])
        )
        copies[-1].start()
    for copy in copies:
        copy.wait()


def fetch_down(me, w_down, head_count, after):
    total_units, width = w_down.shape
    return pl.pallas_call(
        fetch_down_kernel,
        out_shape=(
            pltpu.VMEM((head_count, total_units, width // head_count), jnp.bfloat16),
            jax.ShapeDtypeStruct((SUBLANES, LANES), jnp.float32),
        ),
        in_specs=[SMEM, ANY, ANY],
        out_specs=(VMEM, VMEM),
        scratch_shapes=[pltpu.SemaphoreType.DMA((head_count,))],
        compiler_params=pltpu.CompilerParams(vmem_limit_bytes=8 * 2**20),
        cost_estimate=pl.CostEstimate(
            flops=0, bytes_accessed=4 * w_down.size, transcendentals=0
        ),
        name="fetch_down",
    )(me, in_hbm(w_down), after)


def expert_products(states, w_ref, first, p, per_step):
    columns = w_ref.shape[3]
    depth = states.shape[1]
    taken = pl.ds(first, depth // w_ref.shape[2])
    products = [
        jnp.dot(
            states,
            w_ref[p * per_step + i, taken].reshape(depth, columns),
            preferred_element_type=jnp.float32,
        )
        for i in range(per_step)
    ]
    return products[0] if per_step == 1 else jnp.concatenate(products, axis=1)


def steps_of(w_shape):
    per_step = max(1, 2 * LANES // w_shape[3])
    return w_shape[0] // per_step, per_step


def square_sum(ref, depth):
    return jnp.sum(jnp.square(ref[:, :depth].astype(jnp.float32)), axis=1, keepdims=True)


def units_step(me, p, per_step, experts, product, scale, shares):
    tokens = product.shape[0]
    first_half = lax.broadcasted_iota(jnp.int32, (tokens, LANES), 1) < LANES // 2
    source = lax.broadcasted_iota(jnp.int32, (LANES, LANES), 0)
    lane = lax.broadcasted_iota(jnp.int32, (LANES, LANES), 1)
    expert = me * experts + p * per_step + lane * per_step // LANES
    share = jnp.dot(
        shares, (source == expert).astype(jnp.bfloat16), preferred_element_type=jnp.float32
    )
    a, b = product[:, :LANES], product[:, LANES:]
    gate = jnp.where(first_half, a, pltpu.roll(b, LANES // 2, 1)) * scale
    upward = jnp.where(first_half, pltpu.roll(a, LANES // 2, 1), b) * scale
    return (share * (gate / (1.0 + jnp.exp(-gate)) * upward)).astype(jnp.bfloat16)


def part_of(p):
    return pl.ds(pl.multiple_of(p * LANES, LANES), LANES)


def whole_kernel(me_ref, mine_ref, other_ref, w_ref, _, units_ref, states_s):
    experts, head_count, cols, _ = w_ref.shape
    depth = head_count // 2 * cols
    states_s[:, :depth] = mine_ref[:, :depth]
    states_s[:, depth:] = other_ref[:, :depth]
    square = square_sum(mine_ref, depth) + square_sum(other_ref, depth)
    scale = lax.rsqrt(square / (2 * depth) + norm_eps)
    shares = mine_ref[:, depth:]
    steps, per_step = steps_of(w_ref.shape)

    @pl.loop(0, steps, unroll=4)
    def _(p):
        product = expert_products(states_s[...], w_ref, 0, p, per_step)
        units_ref[:, part_of(p)] = units_step(
            me_ref[0], p, per_step, experts, product, scale, shares
        )


def first_kernel(mine_ref, w_ref, _, product_ref):
    _, head_count, cols, _ = w_ref.shape
    steps, per_step = steps_of(w_ref.shape)

    @pl.loop(0, steps, unroll=4)
    def _(p):
        states = mine_ref[:, : head_count // 2 * cols]
        product_ref[p] = expert_products(states, w_ref, 0, p, per_step)


def second_kernel(me_ref, mine_ref, other_ref, product_ref, w_ref, w_down_ref, units_ref, send_ref):
    experts, head_count, cols, _ = w_ref.shape
    depth = head_count // 2 * cols
    square = square_sum(mine_ref, depth) + square_sum(other_ref, depth)
    scale = lax.rsqrt(square / (2 * depth) + norm_eps)
    shares = mine_ref[:, depth:]
    steps, per_step = steps_of(w_ref.shape)

    @pl.loop(0, steps, unroll=4)
    def _(p):
        product = product_ref[p] + expert_products(
            other_ref[:, :depth], w_ref, head_count // 2, p, per_step
        )
        units_ref[:, part_of(p)] = units_step(
            me_ref[0], p, per_step, experts, product, scale, shares
        )

    down_blocks(units_ref[...], w_down_ref, 1, send_ref)


def experts_whole(me, mine, other, weights, after, total_units):
    experts, head_count, cols, columns = weights.shape
    tokens = mine.shape[0]
    return pl.pallas_call(
        whole_kernel,
        out_shape=jax.ShapeDtypeStruct((tokens, total_units), jnp.bfloat16),
        in_specs=[SMEM] + [VMEM] * 3 + [ANY],
        out_specs=VMEM,
        scratch_shapes=[pltpu.VMEM((tokens, head_count * cols), jnp.bfloat16)],
        compiler_params=pltpu.CompilerParams(vmem_limit_bytes=12 * 2**20),
        cost_estimate=pl.CostEstimate(
            flops=2 * tokens * head_count * cols * experts * columns,
            bytes_accessed=2 * head_count * cols * experts * columns,
            transcendentals=0,
        ),
        name="experts_whole",
    )(me, mine, other, in_vmem(weights), after)


def experts_first(mine, weights, after):
    experts, head_count, cols, columns = weights.shape
    tokens = mine.shape[0]
    steps, per_step = steps_of(weights.shape)
    return pl.pallas_call(
        first_kernel,
        out_shape=jax.ShapeDtypeStruct((steps, tokens, per_step * columns), jnp.float32),
        in_specs=[VMEM] * 2 + [ANY],
        out_specs=VMEM,
        compiler_params=pltpu.CompilerParams(vmem_limit_bytes=12 * 2**20),
        cost_estimate=pl.CostEstimate(
            flops=tokens * head_count * cols * experts * columns,
            bytes_accessed=head_count * cols * experts * columns,
            transcendentals=0,
        ),
        name="experts_first",
    )(mine, in_vmem(weights), after)


def experts_second(me, mine, other, products, weights, w_down):
    experts, head_count, cols, columns = weights.shape
    tokens = mine.shape[0]
    return pl.pallas_call(
        second_kernel,
        out_shape=(
            jax.ShapeDtypeStruct((tokens, w_down.shape[1]), jnp.bfloat16),
            jax.ShapeDtypeStruct((tokens, head_count // 2 * cols), jnp.bfloat16),
        ),
        in_specs=[SMEM] + [VMEM] * 5,
        out_specs=(VMEM, VMEM),
        compiler_params=pltpu.CompilerParams(vmem_limit_bytes=12 * 2**20),
        cost_estimate=pl.CostEstimate(
            flops=tokens * head_count * cols * experts * columns,
            bytes_accessed=head_count * cols * experts * columns,
            transcendentals=0,
        ),
        name="experts_second",
    )(me, mine, other, products, in_vmem(weights), in_vmem(w_down))


def down_blocks(units, w_ref, first, out_ref):
    cols = w_ref.shape[2]
    for t in range(w_ref.shape[0] // 2):
        out_ref[:, t * cols : (t + 1) * cols] = jnp.dot(
            units, w_ref[2 * t + first], preferred_element_type=jnp.float32
        ).astype(jnp.bfloat16)


def down_kernel(firsts, units_ref, w_ref, *outs):
    for first, out_ref in zip(firsts, outs):
        down_blocks(units_ref[...], w_ref, first, out_ref)


def down_part(units, w_down, firsts):
    head_count, total_units, cols = w_down.shape
    tokens = units.shape[0]
    half = jax.ShapeDtypeStruct((tokens, head_count // 2 * cols), jnp.bfloat16)
    return pl.pallas_call(
        functools.partial(down_kernel, firsts),
        out_shape=[half] * len(firsts),
        in_specs=[VMEM, VMEM],
        out_specs=[VMEM] * len(firsts),
        compiler_params=pltpu.CompilerParams(vmem_limit_bytes=12 * 2**20),
        cost_estimate=pl.CostEstimate(
            flops=len(firsts) * tokens * total_units * head_count * cols,
            bytes_accessed=len(firsts) * total_units * head_count * cols,
            transcendentals=0,
        ),
        name="down",
    )(units, in_vmem(w_down))


def hold_kernel(value_ref, after_ref, out_ref):
    pass


def hold(value, after):
    return pl.pallas_call(
        hold_kernel,
        out_shape=jax.ShapeDtypeStruct(value.shape, value.dtype),
        in_specs=[ANY, ANY],
        out_specs=ANY,
        input_output_aliases={0: 0},
        compiler_params=pltpu.CompilerParams(vmem_limit_bytes=2**20),
        name="hold",
    )(value, after)


def sum_kernel(keep_ref, sent_ref, *outs):
    cols = outs[0].shape[1]
    for t, out in enumerate(outs):
        part = slice(t * cols, (t + 1) * cols)
        total = keep_ref[:, part].astype(jnp.float32) + sent_ref[:, part].astype(jnp.float32)
        out[...] = total.astype(out.dtype)


def sum_part(keep, sent, cols, first_type):
    tokens, columns = keep.shape
    blocks = columns // cols
    return pl.pallas_call(
        sum_kernel,
        out_shape=[
            jax.ShapeDtypeStruct((tokens, cols), jnp.bfloat16 if t else first_type)
            for t in range(blocks)
        ],
        in_specs=[VMEM, VMEM],
        out_specs=[VMEM] * blocks,
        compiler_params=pltpu.CompilerParams(vmem_limit_bytes=8 * 2**20),
        name="sum",
    )(keep, sent)


def swap(value, axis, size, mask):
    return lax.ppermute(value, axis, [(i, i ^ mask) for i in range(size)])


def per_device(
    hidden, lengths, expert_ids, route_weights, w_qkv, w_out, k_cache, v_cache, w_in, w_down
):
    req_size = lax.axis_size("req")
    head_size = lax.axis_size("head")
    me = lax.axis_index("head")
    me_ref = me[None].astype(jnp.int32)
    rows, cols = hidden.shape
    experts_local, units_local, width = w_down.shape
    even = range(0, head_size, 2)

    pieces = [hidden] + [swap(hidden, "head", head_size, j) for j in range(1, head_size)]
    flat = (rows, k_cache.shape[1] * k_cache.shape[2], k_cache.shape[3])
    own, w_near, room, cosine, sine = fetch(me_ref, lengths, hidden, w_qkv, flat, head_size)
    keep, send = attention(
        [own] + pieces[1:],
        me_ref,
        lengths,
        cosine,
        sine,
        w_near,
        room,
        w_out,
        k_cache.reshape(flat),
        v_cache.reshape(flat),
    )
    half = keep.astype(jnp.float32) + swap(send, "head", head_size, 1).astype(jnp.float32)
    half = half.astype(jnp.bfloat16)
    others = [swap(half, "head", head_size, j) for j in even if j]
    early, late = range(head_size // 2), range(head_size // 2, head_size)
    buffer, token = by_expert(tuple(early), me_ref, w_in, head_size, None, half)

    every = jnp.arange(head_size * experts_local, dtype=jnp.int32)
    matches = (expert_ids[:, :, None] == every[None, None, :]).astype(jnp.float32)
    shares = jnp.sum(route_weights[:, :, None] * matches, axis=1).astype(jnp.bfloat16)
    shares = jnp.pad(shares, ((0, 0), (0, -shares.shape[1] % LANES)))
    payload, resid = payload_part([pieces[j] for j in even], half, others, shares, token)

    steps = range(2, req_size, 2)
    line = [payload] + [swap(payload, "req", req_size, k) for k in steps]
    w_down_flat = w_down.reshape(experts_local * units_local, width)
    buffer, token = by_expert(tuple(late), me_ref, w_in, head_size, buffer, payload)
    line = stack_part(line, token)
    crossed = swap(line, "req", req_size, 1)
    line_other = swap(line, "head", head_size, 1)
    units = experts_whole(me_ref, line, line_other, buffer, token, w_down_flat.shape[0])
    w_down_near, _ = fetch_down(me_ref, w_down_flat, head_size, units)
    keep, send = down_part(units, w_down_near, (0, 1))
    crossed = hold(crossed, send)
    crossed_other = swap(crossed, "head", head_size, 1)
    line_sums = sum_part(keep, swap(send, "head", head_size, 1), cols, jnp.float32)
    total = line_sums[0]
    got = [swap(line_sums[j // 2], "head", head_size, j) for j in even if j]
    products = experts_first(crossed, buffer, line_sums[-1])
    units, send = experts_second(me_ref, crossed, crossed_other, products, buffer, w_down_near)
    (keep,) = down_part(units, w_down_near, (0,))
    crossed_sums = sum_part(keep, swap(send, "head", head_size, 1), cols, jnp.bfloat16)
    for j in even:
        pairs = [
            (r * head_size + h, (r ^ 1) * head_size + (h ^ j))
            for r in range(req_size)
            for h in range(head_size)
        ]
        got.append(lax.ppermute(crossed_sums[j // 2], ("req", "head"), pairs))
    for part in got:
        total = total + part.astype(jnp.float32)
    chunks = total.astype(jnp.bfloat16).reshape(req_size // 2, rows, cols)
    out = chunks[0].astype(jnp.float32)
    for k in steps:
        out = out + swap(chunks[k // 2], "req", req_size, k).astype(jnp.float32)
    return (out + resid).astype(jnp.bfloat16)


def solution(mesh):
    in_specs = (
        P("req", "head"),
        P("req"),
        P("req", None),
        P("req", None),
        P(None, None, "head"),
        P("head", None),
        P("req", None, "head", None),
        P("req", None, "head", None),
        P(None, "head", "req"),
        P("head", "req", None),
    )
    out_specs = P("req", "head")
    return jax.shard_map(
        per_device, mesh=mesh, in_specs=in_specs, out_specs=out_specs, check_vma=False
    )
```

```python
import functools
import jax
import jax.numpy as jnp
from jax import lax
from jax.experimental import pallas as pl
from jax.experimental.pallas import tpu as pltpu
from jax.sharding import PartitionSpec as P

rope_theta = 50000.0
norm_eps = 1e-05
LANES = 128
SUBLANES = 8
CHUNK = 128
GROUP = 8
MASKED = -1e30


VMEM = pl.BlockSpec(memory_space=pltpu.VMEM)
SMEM = pl.BlockSpec(memory_space=pltpu.SMEM)
ANY = pl.BlockSpec(memory_space=pl.ANY)


def in_hbm(array):
    return pltpu.with_memory_space_constraint(array, pltpu.HBM)


def in_vmem(array):
    return pltpu.with_memory_space_constraint(array, pltpu.VMEM)


def used_rows(length, heads_local):
    return pl.multiple_of((length + 7) // 8 * (8 * heads_local), 8 * heads_local)


def fetch_kernel(
    lengths_hbm, me_ref, freqs_ref, own_ref, w_ref,
    own_out_ref, w_out_ref, blank_ref, cos_ref, sin_ref, lengths_ref, angle_s, sem, own_sem, len_sem,
):
    head_count, cols = w_out_ref.shape[1:3]
    chunk_rows = CHUNK * cols // LANES
    me = me_ref[0]
    copies = [pltpu.make_async_copy(own_ref, own_out_ref, own_sem)]
    for c in range(w_ref.shape[0]):
        for j in range(head_count):
            first = pl.multiple_of((me ^ j) * cols, cols)
            copies.append(
                pltpu.make_async_copy(
                    w_ref.at[c, pl.ds(first, cols)], w_out_ref.at[c, j], sem.at[c, j]
                )
            )
    lengths_copy = pltpu.make_async_copy(lengths_hbm, lengths_ref, len_sem)
    lengths_copy.start()
    for copy in copies:
        copy.start()
    lengths_copy.wait()

    rows = angle_s.shape[0]
    cache_rows = blank_ref.shape[0] // rows

    @pl.loop(0, rows)
    def _(r):
        last = r * cache_rows + (lengths_ref[r] - 1) // CHUNK * chunk_rows
        blank_ref[pl.ds(pl.multiple_of(last, chunk_rows), chunk_rows)] = jnp.zeros(
            (chunk_rows, LANES), jnp.bfloat16
        )
        angle_s[pl.ds(r, 1), :] = lengths_ref[r].astype(jnp.float32) * freqs_ref[...]

    cos_ref[...] = jnp.cos(angle_s[...])
    lane = lax.broadcasted_iota(jnp.int32, sin_ref.shape, 1)
    sine = jnp.sin(angle_s[...])
    sin_ref[...] = jnp.where(lane < LANES // 2, -sine, sine)
    for copy in copies:
        copy.wait()


def fetch(me, lengths, hidden, w_qkv, v_shape, head_count):
    cols = w_qkv.shape[2]
    rows = hidden.shape[0]
    exponents = jnp.arange(LANES, dtype=jnp.float32) % (LANES // 2) / (LANES // 2)
    freqs = (rope_theta**-exponents)[None, :]
    return pl.pallas_call(
        fetch_kernel,
        out_shape=(
            pltpu.VMEM(hidden.shape, jnp.bfloat16),
            pltpu.VMEM((w_qkv.shape[0], head_count, cols, cols), jnp.bfloat16),
            pltpu.VMEM(v_shape, jnp.bfloat16),
            pltpu.VMEM((rows, LANES), jnp.float32),
            pltpu.VMEM((rows, LANES), jnp.float32),
            pltpu.SMEM(lengths.shape, lengths.dtype),
        ),
        in_specs=[ANY, SMEM, VMEM, ANY, ANY],
        out_specs=[VMEM] * 5 + [SMEM],
        scratch_shapes=[
            pltpu.VMEM((rows, LANES), jnp.float32),
            pltpu.SemaphoreType.DMA((w_qkv.shape[0], head_count)),
            pltpu.SemaphoreType.DMA(()),
            pltpu.SemaphoreType.DMA(()),
        ],
        compiler_params=pltpu.CompilerParams(vmem_limit_bytes=8 * 2**20),
        cost_estimate=pl.CostEstimate(
            flops=0, bytes_accessed=4 * w_qkv.size, transcendentals=0
        ),
        name="fetch",
    )(in_hbm(lengths), me, freqs, in_hbm(hidden), in_hbm(w_qkv))


def attention_kernel(head_count, lengths_ref, me_ref, cos_ref, sin_ref, *refs):
    pieces = refs[:head_count]
    (
        w_qkv_ref, _, w_out_ref, k_ref, v_ref, w_down_ref, keep_ref, send_ref, v_s, down_ref,
        w_out_s, k_s, query_s, key_s, value_s, attended_s, out_sem, k_sem, v_sem, down_sem,
    ) = refs[head_count:]
    rows, cols = pieces[0].shape
    heads_local = cols // LANES
    chunk_rows = CHUNK * heads_local
    me = me_ref[0]

    def out_copy(j):
        first = pl.multiple_of((me ^ j) * cols, cols)
        return pltpu.make_async_copy(
            w_out_ref.at[:, pl.ds(first, cols)], w_out_s.at[j], out_sem.at[j]
        )

    cache_rows = k_s.shape[0] // rows

    def cache_copy(source, target, sem, r, used):
        taken = pl.ds(pl.multiple_of(r * cache_rows, cache_rows), used)
        return pltpu.make_async_copy(
            source.at[taken], target.at[taken], sem.at[r // GROUP]
        )

    @pl.loop(0, rows, unroll=4)
    def _(r):
        used = used_rows(lengths_ref[r], heads_local)
        cache_copy(k_ref, k_s, k_sem, r, used).start()
        cache_copy(v_ref, v_s, v_sem, r, used).start()

    def down_copy(j):
        first = pl.multiple_of((me ^ j) * cols, cols)
        return pltpu.make_async_copy(
            w_down_ref.at[:, pl.ds(first, cols)], down_ref.at[j], down_sem.at[j]
        )

    for j in range(head_count):
        out_copy(j).start()
    for j in range(head_count):
        down_copy(j).start()

    if heads_local < SUBLANES:
        query_s[...] = jnp.zeros_like(query_s)
        key_s[...] = jnp.zeros_like(key_s)
        value_s[...] = jnp.zeros_like(value_s)
    states = jnp.concatenate([piece[...] for piece in pieces], axis=1)
    square = jnp.sum(jnp.square(states.astype(jnp.float32)), axis=1, keepdims=True)
    scale = lax.rsqrt(square / (cols * head_count) + norm_eps)
    cosine, sine = cos_ref[...], sin_ref[...]
    for c, target in enumerate((query_s, key_s, value_s)):
        projected = scale * jnp.dot(
            states,
            w_qkv_ref[c].reshape(head_count * cols, cols),
            preferred_element_type=jnp.float32,
        )
        for h in range(heads_local):
            part = projected[:, h * LANES : (h + 1) * LANES]
            if c < 2:
                part = part * cosine + pltpu.roll(part, LANES // 2, 1) * sine
            target[:, h, :] = part.astype(jnp.bfloat16).astype(jnp.float32)

    column = lax.broadcasted_iota(jnp.int32, (2 * SUBLANES, chunk_rows), 1)
    row = lax.broadcasted_iota(jnp.int32, (2 * SUBLANES, chunk_rows), 0)
    same_head = column % heads_local == row % SUBLANES
    upper = row < SUBLANES
    score_scale = LANES**-0.5
    blank = jnp.zeros((SUBLANES, LANES), jnp.float32)

    def diagonal(a, b):
        return jnp.concatenate(
            [jnp.concatenate([a, blank], axis=1), jnp.concatenate([blank, b], axis=1)], axis=0
        )

    @pl.loop(0, rows // GROUP)
    def _(g):
        requests = [g * GROUP + i for i in range(GROUP)]
        pairs = list(zip(requests[::2], requests[1::2]))
        lengths = [lengths_ref[r] for r in requests]
        spans = list(zip(lengths[::2], lengths[1::2]))
        queries = [diagonal(query_s[a], query_s[b]).astype(jnp.bfloat16) for a, b in pairs]
        own = [
            jnp.sum(query_s[r] * key_s[r], axis=1, keepdims=True) * score_scale for r in requests
        ]
        own = [jnp.concatenate([a, b], axis=0) for a, b in zip(own[::2], own[1::2])]
        values = [diagonal(value_s[a], value_s[b]) for a, b in pairs]
        longest = functools.reduce(jnp.maximum, lengths)
        used = used_rows(sum((length + 7) // 8 * 8 for length in lengths), heads_local)
        cache_copy(k_ref, k_s, k_sem, g * GROUP, used).wait()
        cache_copy(v_ref, v_s, v_sem, g * GROUP, used).wait()

        def with_chunks(count):
            def both(ref, c, pair, span):
                parts = []
                for r, length in zip(pair, span):
                    first = jnp.minimum(c, (length - 1) // CHUNK) * chunk_rows if c else 0
                    first = pl.multiple_of(r * cache_rows + first, chunk_rows)
                    parts.append(ref[pl.ds(first, chunk_rows)])
                return jnp.concatenate(parts, axis=1)

            scores = [
                [
                    lax.dot_general(
                        query,
                        both(k_s, c, pair, span),
                        (((1,), (1,)), ((), ())),
                        preferred_element_type=jnp.float32,
                    )
                    for c in range(count)
                ]
                for query, pair, span in zip(queries, pairs, spans)
            ]
            limits = [
                jnp.where(upper, span[0] * heads_local, span[1] * heads_local) for span in spans
            ]
            scores = [
                [
                    jnp.where(
                        same_head & (column < limit - c * chunk_rows), score * score_scale, MASKED
                    )
                    for c, score in enumerate(parts)
                ]
                for limit, parts in zip(limits, scores)
            ]
            tops = [
                jnp.maximum(
                    mine, jnp.max(functools.reduce(jnp.maximum, parts), axis=1, keepdims=True)
                )
                for mine, parts in zip(own, scores)
            ]
            weights = [[jnp.exp(part - top) for part in parts] for top, parts in zip(tops, scores)]
            faded = [jnp.exp(mine - top) for mine, top in zip(own, tops)]
            totals = [
                fade + jnp.sum(functools.reduce(jnp.add, parts), axis=1, keepdims=True)
                for fade, parts in zip(faded, weights)
            ]
            sums = [
                fade * value
                + sum(
                    jnp.dot(
                        part.astype(jnp.bfloat16),
                        both(v_s, c, pair, span),
                        preferred_element_type=jnp.float32,
                    )
                    for c, part in enumerate(parts)
                )
                for pair, span, fade, value, parts in zip(pairs, spans, faded, values, weights)
            ]
            for (a, b), total, summed in zip(pairs, totals, sums):
                summed = summed / total
                attended_s[a] = summed[:SUBLANES, :LANES]
                attended_s[b] = summed[SUBLANES:, LANES:]

        for count in range(1, cache_rows // chunk_rows + 1):
            pl.when((longest + CHUNK - 1) // CHUNK == count)(
                functools.partial(with_chunks, count)
            )

    attended = jnp.concatenate(
        [attended_s[:, h, :] for h in range(heads_local)], axis=1
    ).astype(jnp.bfloat16)
    for j in range(head_count):
        out_copy(j).wait()
        target = send_ref if j % 2 else keep_ref
        target[:, j // 2 * cols : (j // 2 + 1) * cols] = jnp.dot(
            attended, w_out_s[j], preferred_element_type=jnp.float32
        ).astype(jnp.bfloat16)
    for j in range(head_count):
        down_copy(j).wait()


def attention(pieces, me, lengths, cosine, sine, w_qkv, room, w_out, k_cache, v_cache, w_down):
    head_count = len(pieces)
    rows, cols = pieces[0].shape
    half = jax.ShapeDtypeStruct((rows, head_count // 2 * cols), jnp.bfloat16)
    return pl.pallas_call(
        functools.partial(attention_kernel, head_count),
        out_shape=(
            half,
            half,
            pltpu.VMEM(room.shape, jnp.bfloat16),
            pltpu.VMEM((head_count, w_down.shape[0], cols), jnp.bfloat16),
        ),
        in_specs=[SMEM, SMEM] + [VMEM] * (head_count + 4) + [ANY] * 4,
        out_specs=(VMEM, VMEM, VMEM, VMEM),
        input_output_aliases={head_count + 5: 2},
        scratch_shapes=[
            pltpu.VMEM((head_count, cols, cols), jnp.bfloat16),
            pltpu.VMEM(k_cache.shape, jnp.bfloat16),
        ]
        + [pltpu.VMEM((rows, SUBLANES, LANES), jnp.float32)] * 4
        + [
            pltpu.SemaphoreType.DMA((head_count,)),
            pltpu.SemaphoreType.DMA((rows // GROUP,)),
            pltpu.SemaphoreType.DMA((rows // GROUP,)),
            pltpu.SemaphoreType.DMA((head_count,)),
        ],
        compiler_params=pltpu.CompilerParams(vmem_limit_bytes=20 * 2**20),
        cost_estimate=pl.CostEstimate(
            flops=2 * rows * 4 * cols * head_count * cols,
            bytes_accessed=2 * w_down.size + k_cache.size // 2,
            transcendentals=0,
        ),
        name="attention",
    )(
        pltpu.with_memory_space_constraint(lengths, pltpu.SMEM), me, in_vmem(cosine), in_vmem(sine), *map(in_vmem, pieces), in_vmem(w_qkv), in_vmem(room),
        in_hbm(w_out), in_hbm(k_cache), in_hbm(v_cache), in_hbm(w_down),
    )


RELAYOUT_ROWS = 128
RELAYOUT_STEP = 16

def slot_of(j, head_count):
    return j // 2 + j % 2 * (head_count // 2)


def relayout_kernel(js, me_ref, w_ref, *refs):
    out_ref, token_ref, in_s, in_sem = refs[-4:]
    token_ref[...] = jnp.zeros_like(token_ref)
    experts, head_count, cols, _ = out_ref.shape
    step = in_s.shape[1]
    per_block = cols // step
    copies = []
    for at, j in enumerate(js):
        base = (me_ref[0] ^ j) * cols
        for i in range(per_block):
            slot = at * per_block + i
            first = pl.multiple_of(base + i * step, step)
            copies.append(
                pltpu.make_async_copy(
                    w_ref.at[pl.ds(first, step)], in_s.at[slot], in_sem.at[slot]
                )
            )
    for copy in copies:
        copy.start()
    for slot, copy in enumerate(copies):
        j, i = js[slot // per_block], slot % per_block
        copy.wait()
        for s in range(step // RELAYOUT_STEP):
            part = in_s[slot, pl.ds(s * RELAYOUT_STEP, RELAYOUT_STEP)]
            out_ref[:, slot_of(j, head_count), pl.ds(i * step + s * RELAYOUT_STEP, RELAYOUT_STEP), :] = jnp.swapaxes(
                part, 0, 1
            )


def by_expert(js, me, w_in, head_count, buffer, after):
    width, experts, columns = w_in.shape
    cols = width // head_count
    step = min(RELAYOUT_ROWS, cols)
    slots = len(js) * cols // step
    held = [] if buffer is None else [in_vmem(buffer)]
    return pl.pallas_call(
        functools.partial(relayout_kernel, js),
        out_shape=(
            pltpu.VMEM((experts, head_count, cols, columns), jnp.bfloat16),
            jax.ShapeDtypeStruct((SUBLANES, LANES), jnp.float32),
        ),
        in_specs=[SMEM, ANY] + [VMEM] * len(held) + [ANY],
        out_specs=(VMEM, VMEM),
        input_output_aliases={2: 0} if held else {},
        scratch_shapes=[
            pltpu.VMEM((slots, step, experts, columns), jnp.bfloat16),
            pltpu.SemaphoreType.DMA((slots,)),
        ],
        compiler_params=pltpu.CompilerParams(vmem_limit_bytes=16 * 2**20),
        cost_estimate=pl.CostEstimate(
            flops=0, bytes_accessed=4 * len(js) * cols * experts * columns, transcendentals=0
        ),
        name=f"by_expert_{js[0]}",
    )(me, in_hbm(w_in), *held, after)


def payload_kernel(head_count, *refs):
    blocks = head_count // 2
    pieces, (half_ref, *others), shares_ref = refs[:blocks], refs[blocks : 2 * blocks], refs[2 * blocks]
    payload_ref, resid_ref = refs[-2:]
    cols = pieces[0].shape[1]
    for t in range(blocks):
        total = pieces[t][...].astype(jnp.float32)
        for at, source in enumerate((half_ref, *others)):
            place = (t ^ at) * cols
            total += source[:, place : place + cols].astype(jnp.float32)
        payload_ref[:, t * cols : (t + 1) * cols] = total.astype(jnp.bfloat16)
        if t == 0:
            resid_ref[...] = total
    payload_ref[:, blocks * cols :] = shares_ref[...]


def payload_part(pieces, half, others, shares, after):
    blocks = len(pieces)
    rows, cols = pieces[0].shape
    return pl.pallas_call(
        functools.partial(payload_kernel, 2 * blocks),
        out_shape=(
            jax.ShapeDtypeStruct((rows, blocks * cols + shares.shape[1]), jnp.bfloat16),
            jax.ShapeDtypeStruct((rows, cols), jnp.float32),
        ),
        in_specs=[VMEM] * (2 * blocks + 1) + [ANY],
        out_specs=(VMEM, VMEM),
        compiler_params=pltpu.CompilerParams(vmem_limit_bytes=8 * 2**20),
        name="payload",
    )(*pieces, half, *others, shares, after)


def stack_kernel(count, *refs):
    rows = refs[0].shape[0]
    for i in range(count):
        refs[-1][i * rows : (i + 1) * rows, :] = refs[i][...]


def stack_part(parts, after):
    rows, columns = parts[0].shape
    return pl.pallas_call(
        functools.partial(stack_kernel, len(parts)),
        out_shape=jax.ShapeDtypeStruct((len(parts) * rows, columns), jnp.bfloat16),
        in_specs=[VMEM] * len(parts) + [ANY],
        out_specs=VMEM,
        compiler_params=pltpu.CompilerParams(vmem_limit_bytes=8 * 2**20),
        name="stack",
    )(*parts, after)


def expert_products(states, w_ref, first, p, per_step):
    columns = w_ref.shape[3]
    depth = states.shape[1]
    taken = pl.ds(first, depth // w_ref.shape[2])
    products = [
        jnp.dot(
            states,
            w_ref[p * per_step + i, taken].reshape(depth, columns),
            preferred_element_type=jnp.float32,
        )
        for i in range(per_step)
    ]
    return products[0] if per_step == 1 else jnp.concatenate(products, axis=1)


def steps_of(w_shape):
    per_step = max(1, 2 * LANES // w_shape[3])
    return w_shape[0] // per_step, per_step


def square_sum(ref, depth):
    return jnp.sum(jnp.square(ref[:, :depth].astype(jnp.float32)), axis=1, keepdims=True)


def units_step(me, p, per_step, experts, product, scale, shares):
    tokens = product.shape[0]
    first_half = lax.broadcasted_iota(jnp.int32, (tokens, LANES), 1) < LANES // 2
    source = lax.broadcasted_iota(jnp.int32, (LANES, LANES), 0)
    lane = lax.broadcasted_iota(jnp.int32, (LANES, LANES), 1)
    expert = me * experts + p * per_step + lane * per_step // LANES
    share = jnp.dot(
        shares, (source == expert).astype(jnp.bfloat16), preferred_element_type=jnp.float32
    )
    a, b = product[:, :LANES], product[:, LANES:]
    gate = jnp.where(first_half, a, pltpu.roll(b, LANES // 2, 1)) * scale
    upward = jnp.where(first_half, pltpu.roll(a, LANES // 2, 1), b) * scale
    return (share * (gate / (1.0 + jnp.exp(-gate)) * upward)).astype(jnp.bfloat16)


def part_of(p):
    return pl.ds(pl.multiple_of(p * LANES, LANES), LANES)


def whole_kernel(me_ref, mine_ref, other_ref, w_ref, _, units_ref, states_s):
    experts, head_count, cols, _ = w_ref.shape
    depth = head_count // 2 * cols
    states_s[:, :depth] = mine_ref[:, :depth]
    states_s[:, depth:] = other_ref[:, :depth]
    square = square_sum(mine_ref, depth) + square_sum(other_ref, depth)
    scale = lax.rsqrt(square / (2 * depth) + norm_eps)
    shares = mine_ref[:, depth:]
    steps, per_step = steps_of(w_ref.shape)

    @pl.loop(0, steps, unroll=4)
    def _(p):
        product = expert_products(states_s[...], w_ref, 0, p, per_step)
        units_ref[:, part_of(p)] = units_step(
            me_ref[0], p, per_step, experts, product, scale, shares
        )


def first_kernel(mine_ref, w_ref, _, product_ref):
    _, head_count, cols, _ = w_ref.shape
    steps, per_step = steps_of(w_ref.shape)

    @pl.loop(0, steps, unroll=4)
    def _(p):
        states = mine_ref[:, : head_count // 2 * cols]
        product_ref[p] = expert_products(states, w_ref, 0, p, per_step)


def second_kernel(me_ref, mine_ref, other_ref, product_ref, w_ref, w_down_ref, units_ref, send_ref):
    experts, head_count, cols, _ = w_ref.shape
    depth = head_count // 2 * cols
    square = square_sum(mine_ref, depth) + square_sum(other_ref, depth)
    scale = lax.rsqrt(square / (2 * depth) + norm_eps)
    shares = mine_ref[:, depth:]
    steps, per_step = steps_of(w_ref.shape)

    @pl.loop(0, steps, unroll=4)
    def _(p):
        product = product_ref[p] + expert_products(
            other_ref[:, :depth], w_ref, head_count // 2, p, per_step
        )
        units_ref[:, part_of(p)] = units_step(
            me_ref[0], p, per_step, experts, product, scale, shares
        )

    down_blocks(units_ref[...], w_down_ref, 1, send_ref)


def experts_whole(me, mine, other, weights, after, total_units):
    experts, head_count, cols, columns = weights.shape
    tokens = mine.shape[0]
    return pl.pallas_call(
        whole_kernel,
        out_shape=jax.ShapeDtypeStruct((tokens, total_units), jnp.bfloat16),
        in_specs=[SMEM] + [VMEM] * 3 + [ANY],
        out_specs=VMEM,
        scratch_shapes=[pltpu.VMEM((tokens, head_count * cols), jnp.bfloat16)],
        compiler_params=pltpu.CompilerParams(vmem_limit_bytes=12 * 2**20),
        cost_estimate=pl.CostEstimate(
            flops=2 * tokens * head_count * cols * experts * columns,
            bytes_accessed=2 * head_count * cols * experts * columns,
            transcendentals=0,
        ),
        name="experts_whole",
    )(me, mine, other, in_vmem(weights), after)


def experts_first(mine, weights, after):
    experts, head_count, cols, columns = weights.shape
    tokens = mine.shape[0]
    steps, per_step = steps_of(weights.shape)
    return pl.pallas_call(
        first_kernel,
        out_shape=jax.ShapeDtypeStruct((steps, tokens, per_step * columns), jnp.float32),
        in_specs=[VMEM] * 2 + [ANY],
        out_specs=VMEM,
        compiler_params=pltpu.CompilerParams(vmem_limit_bytes=12 * 2**20),
        cost_estimate=pl.CostEstimate(
            flops=tokens * head_count * cols * experts * columns,
            bytes_accessed=head_count * cols * experts * columns,
            transcendentals=0,
        ),
        name="experts_first",
    )(mine, in_vmem(weights), after)


def experts_second(me, mine, other, products, weights, w_down):
    experts, head_count, cols, columns = weights.shape
    tokens = mine.shape[0]
    return pl.pallas_call(
        second_kernel,
        out_shape=(
            jax.ShapeDtypeStruct((tokens, w_down.shape[1]), jnp.bfloat16),
            jax.ShapeDtypeStruct((tokens, head_count // 2 * cols), jnp.bfloat16),
        ),
        in_specs=[SMEM] + [VMEM] * 5,
        out_specs=(VMEM, VMEM),
        compiler_params=pltpu.CompilerParams(vmem_limit_bytes=12 * 2**20),
        cost_estimate=pl.CostEstimate(
            flops=tokens * head_count * cols * experts * columns,
            bytes_accessed=head_count * cols * experts * columns,
            transcendentals=0,
        ),
        name="experts_second",
    )(me, mine, other, products, in_vmem(weights), in_vmem(w_down))


def down_blocks(units, w_ref, first, out_ref):
    cols = w_ref.shape[2]
    for t in range(w_ref.shape[0] // 2):
        out_ref[:, t * cols : (t + 1) * cols] = jnp.dot(
            units, w_ref[2 * t + first], preferred_element_type=jnp.float32
        ).astype(jnp.bfloat16)


def down_kernel(firsts, units_ref, w_ref, *outs):
    for first, out_ref in zip(firsts, outs):
        down_blocks(units_ref[...], w_ref, first, out_ref)


def down_part(units, w_down, firsts):
    head_count, total_units, cols = w_down.shape
    tokens = units.shape[0]
    half = jax.ShapeDtypeStruct((tokens, head_count // 2 * cols), jnp.bfloat16)
    return pl.pallas_call(
        functools.partial(down_kernel, firsts),
        out_shape=[half] * len(firsts),
        in_specs=[VMEM, VMEM],
        out_specs=[VMEM] * len(firsts),
        compiler_params=pltpu.CompilerParams(vmem_limit_bytes=12 * 2**20),
        cost_estimate=pl.CostEstimate(
            flops=len(firsts) * tokens * total_units * head_count * cols,
            bytes_accessed=len(firsts) * total_units * head_count * cols,
            transcendentals=0,
        ),
        name="down",
    )(units, in_vmem(w_down))


def hold_kernel(value_ref, after_ref, out_ref):
    pass


def hold(value, after):
    return pl.pallas_call(
        hold_kernel,
        out_shape=jax.ShapeDtypeStruct(value.shape, value.dtype),
        in_specs=[ANY, ANY],
        out_specs=ANY,
        input_output_aliases={0: 0},
        compiler_params=pltpu.CompilerParams(vmem_limit_bytes=2**20),
        name="hold",
    )(value, after)


def sum_kernel(keep_ref, sent_ref, *outs):
    cols = outs[0].shape[1]
    for t, out in enumerate(outs):
        part = slice(t * cols, (t + 1) * cols)
        total = keep_ref[:, part].astype(jnp.float32) + sent_ref[:, part].astype(jnp.float32)
        out[...] = total.astype(out.dtype)


def sum_part(keep, sent, cols, first_type):
    tokens, columns = keep.shape
    blocks = columns // cols
    return pl.pallas_call(
        sum_kernel,
        out_shape=[
            jax.ShapeDtypeStruct((tokens, cols), jnp.bfloat16 if t else first_type)
            for t in range(blocks)
        ],
        in_specs=[VMEM, VMEM],
        out_specs=[VMEM] * blocks,
        compiler_params=pltpu.CompilerParams(vmem_limit_bytes=8 * 2**20),
        name="sum",
    )(keep, sent)


def swap(value, axis, size, mask):
    return lax.ppermute(value, axis, [(i, i ^ mask) for i in range(size)])


def per_device(
    hidden, lengths, expert_ids, route_weights, w_qkv, w_out, k_cache, v_cache, w_in, w_down
):
    req_size = lax.axis_size("req")
    head_size = lax.axis_size("head")
    me = lax.axis_index("head")
    me_ref = me[None].astype(jnp.int32)
    rows, cols = hidden.shape
    experts_local, units_local, width = w_down.shape
    even = range(0, head_size, 2)

    pieces = [hidden] + [swap(hidden, "head", head_size, j) for j in range(1, head_size)]
    flat = (rows * k_cache.shape[1] * k_cache.shape[2], k_cache.shape[3])
    own, w_near, room, cosine, sine, lengths_near = fetch(me_ref, lengths, hidden, w_qkv, flat, head_size)
    keep, send, _, w_down_near = attention(
        [own] + pieces[1:],
        me_ref,
        lengths_near,
        cosine,
        sine,
        w_near,
        room,
        w_out,
        k_cache.reshape(flat),
        v_cache.reshape(flat),
        w_down.reshape(experts_local * units_local, width),
    )
    half = keep.astype(jnp.float32) + swap(send, "head", head_size, 1).astype(jnp.float32)
    half = half.astype(jnp.bfloat16)
    others = [swap(half, "head", head_size, j) for j in even if j]
    early, late = range(head_size // 2), range(head_size // 2, head_size)
    buffer, token = by_expert(tuple(early), me_ref, w_in, head_size, None, half)

    every = jnp.arange(head_size * experts_local, dtype=jnp.int32)
    matches = (expert_ids[:, :, None] == every[None, None, :]).astype(jnp.float32)
    shares = jnp.sum(route_weights[:, :, None] * matches, axis=1).astype(jnp.bfloat16)
    shares = jnp.pad(shares, ((0, 0), (0, -shares.shape[1] % LANES)))
    payload, resid = payload_part([pieces[j] for j in even], half, others, shares, token)

    steps = range(2, req_size, 2)
    line = [payload] + [swap(payload, "req", req_size, k) for k in steps]
    buffer, token = by_expert(tuple(late), me_ref, w_in, head_size, buffer, payload)
    line = stack_part(line, token)
    crossed = swap(line, "req", req_size, 1)
    line_other = swap(line, "head", head_size, 1)
    units = experts_whole(me_ref, line, line_other, buffer, token, w_down_near.shape[1])
    keep, send = down_part(units, w_down_near, (0, 1))
    crossed = hold(crossed, send)
    crossed_other = swap(crossed, "head", head_size, 1)
    line_sums = sum_part(keep, swap(send, "head", head_size, 1), cols, jnp.float32)
    total = line_sums[0]
    products = experts_first(crossed, buffer, line_sums[-1])
    units, send = experts_second(me_ref, crossed, crossed_other, products, buffer, w_down_near)
    (keep,) = down_part(units, w_down_near, (0,))
    crossed_sums = sum_part(keep, swap(send, "head", head_size, 1), cols, jnp.bfloat16)
    got = [
        swap(hold(line_sums[j // 2], crossed_sums[0]), "head", head_size, j) for j in even if j
    ]
    for j in even:
        pairs = [
            (r * head_size + h, (r ^ 1) * head_size + (h ^ j))
            for r in range(req_size)
            for h in range(head_size)
        ]
        got.append(lax.ppermute(crossed_sums[j // 2], ("req", "head"), pairs))
    for part in got:
        total = total + part.astype(jnp.float32)
    chunks = total.astype(jnp.bfloat16).reshape(req_size // 2, rows, cols)
    out = chunks[0].astype(jnp.float32)
    for k in steps:
        out = out + swap(chunks[k // 2], "req", req_size, k).astype(jnp.float32)
    return (out + resid).astype(jnp.bfloat16)


def solution(mesh):
    in_specs = (
        P("req", "head"),
        P("req"),
        P("req", None),
        P("req", None),
        P(None, None, "head"),
        P("head", None),
        P("req", None, "head", None),
        P("req", None, "head", None),
        P(None, "head", "req"),
        P("head", "req", None),
    )
    out_specs = P("req", "head")
    return jax.shard_map(
        per_device, mesh=mesh, in_specs=in_specs, out_specs=out_specs, check_vma=False
    )
```

```python
import functools
import jax
import jax.numpy as jnp
from jax import lax
from jax.experimental import pallas as pl
from jax.experimental.pallas import tpu as pltpu
from jax.sharding import PartitionSpec as P

rope_theta = 50000.0
norm_eps = 1e-05
LANES = 128
SUBLANES = 8
CHUNK = 128
GROUP = 8
MASKED = -1e30


VMEM = pl.BlockSpec(memory_space=pltpu.VMEM)
SMEM = pl.BlockSpec(memory_space=pltpu.SMEM)
ANY = pl.BlockSpec(memory_space=pl.ANY)


def in_hbm(array):
    return pltpu.with_memory_space_constraint(array, pltpu.HBM)


def in_vmem(array):
    return pltpu.with_memory_space_constraint(array, pltpu.VMEM)


def used_rows(length, heads_local):
    return pl.multiple_of((length + 7) // 8 * (8 * heads_local), 8 * heads_local)


def fetch_kernel(
    lengths_hbm, me_ref, freqs_ref, own_ref, w_ref, ids_ref, route_ref,
    own_out_ref, w_out_ref, blank_ref, cos_ref, sin_ref, lengths_ref, shares_ref,
    angle_s, ids_s, route_s, sem, small_sem,
):
    head_count, cols = w_out_ref.shape[1:3]
    chunk_rows = CHUNK * cols // LANES
    me = me_ref[0]
    lengths_copy, *copies = [
        pltpu.make_async_copy(source, target, small_sem.at[i])
        for i, (source, target) in enumerate(
            (
                (lengths_hbm, lengths_ref),
                (ids_ref, ids_s),
                (route_ref, route_s),
                (own_ref, own_out_ref),
            )
        )
    ]
    small = copies[:2]
    for c in range(w_ref.shape[0]):
        for j in range(head_count):
            first = pl.multiple_of((me ^ j) * cols, cols)
            copies.append(
                pltpu.make_async_copy(
                    w_ref.at[c, pl.ds(first, cols)], w_out_ref.at[c, j], sem.at[c, j]
                )
            )
    lengths_copy.start()
    for copy in copies:
        copy.start()
    lengths_copy.wait()

    rows = angle_s.shape[0]
    cache_rows = blank_ref.shape[0] // rows

    @pl.loop(0, rows)
    def _(r):
        last = r * cache_rows + (lengths_ref[r] - 1) // CHUNK * chunk_rows
        blank_ref[pl.ds(pl.multiple_of(last, chunk_rows), chunk_rows)] = jnp.zeros(
            (chunk_rows, LANES), jnp.bfloat16
        )
        angle_s[pl.ds(r, 1), :] = lengths_ref[r].astype(jnp.float32) * freqs_ref[...]

    cos_ref[...] = jnp.cos(angle_s[...])
    lane = lax.broadcasted_iota(jnp.int32, sin_ref.shape, 1)
    sine = jnp.sin(angle_s[...])
    sin_ref[...] = jnp.where(lane < LANES // 2, -sine, sine)
    for copy in small:
        copy.wait()
    expert = lax.broadcasted_iota(jnp.int32, (shares_ref.shape[1], rows), 0)
    shares = jnp.zeros(expert.shape, jnp.float32)
    for k in range(ids_s.shape[0]):
        shares += jnp.where(expert == ids_s[k : k + 1, :], route_s[k : k + 1, :], 0.0)
    shares_ref[...] = jnp.transpose(shares, (1, 0)).astype(jnp.bfloat16)
    for copy in copies[2:]:
        copy.wait()


def fetch(me, lengths, hidden, w_qkv, v_shape, head_count, expert_ids, route_weights, experts):
    cols = w_qkv.shape[2]
    rows = hidden.shape[0]
    exponents = jnp.arange(LANES, dtype=jnp.float32) % (LANES // 2) / (LANES // 2)
    freqs = (rope_theta**-exponents)[None, :]
    return pl.pallas_call(
        fetch_kernel,
        out_shape=(
            pltpu.VMEM(hidden.shape, jnp.bfloat16),
            pltpu.VMEM((w_qkv.shape[0], head_count, cols, cols), jnp.bfloat16),
            pltpu.VMEM(v_shape, jnp.bfloat16),
            pltpu.VMEM((rows, LANES), jnp.float32),
            pltpu.VMEM((rows, LANES), jnp.float32),
            pltpu.SMEM(lengths.shape, lengths.dtype),
            pltpu.VMEM((rows, -(-experts // LANES) * LANES), jnp.bfloat16),
        ),
        in_specs=[ANY, SMEM, VMEM] + [ANY] * 4,
        out_specs=[VMEM] * 5 + [SMEM, VMEM],
        scratch_shapes=[
            pltpu.VMEM((rows, LANES), jnp.float32),
            pltpu.VMEM(expert_ids.shape[::-1], expert_ids.dtype),
            pltpu.VMEM(route_weights.shape[::-1], route_weights.dtype),
            pltpu.SemaphoreType.DMA((w_qkv.shape[0], head_count)),
            pltpu.SemaphoreType.DMA((4,)),
        ],
        compiler_params=pltpu.CompilerParams(vmem_limit_bytes=8 * 2**20),
        cost_estimate=pl.CostEstimate(
            flops=0, bytes_accessed=4 * w_qkv.size, transcendentals=0
        ),
        name="fetch",
    )(
        in_hbm(lengths), me, freqs, in_hbm(hidden), in_hbm(w_qkv), in_hbm(expert_ids.T),
        in_hbm(route_weights.T),
    )


def attention_kernel(head_count, lengths_ref, me_ref, cos_ref, sin_ref, *refs):
    pieces = refs[:head_count]
    (
        w_qkv_ref, _, w_out_ref, k_ref, v_ref, w_down_ref, keep_ref, send_ref, v_s, down_ref,
        w_out_s, k_s, query_s, key_s, value_s, attended_s, out_sem, k_sem, v_sem, down_sem,
    ) = refs[head_count:]
    rows, cols = pieces[0].shape
    heads_local = cols // LANES
    chunk_rows = CHUNK * heads_local
    me = me_ref[0]

    def out_copy(j):
        first = pl.multiple_of((me ^ j) * cols, cols)
        return pltpu.make_async_copy(
            w_out_ref.at[:, pl.ds(first, cols)], w_out_s.at[j], out_sem.at[j]
        )

    cache_rows = k_s.shape[0] // rows

    def cache_copy(source, target, sem, r, used):
        taken = pl.ds(pl.multiple_of(r * cache_rows, cache_rows), used)
        return pltpu.make_async_copy(
            source.at[taken], target.at[taken], sem.at[r // GROUP]
        )

    @pl.loop(0, rows, unroll=4)
    def _(r):
        used = used_rows(lengths_ref[r], heads_local)
        cache_copy(k_ref, k_s, k_sem, r, used).start()
        cache_copy(v_ref, v_s, v_sem, r, used).start()

    def down_copy(j):
        first = pl.multiple_of((me ^ j) * cols, cols)
        return pltpu.make_async_copy(
            w_down_ref.at[:, pl.ds(first, cols)], down_ref.at[j], down_sem.at[j]
        )

    for j in range(head_count):
        out_copy(j).start()
    for j in range(head_count):
        down_copy(j).start()

    if heads_local < SUBLANES:
        query_s[...] = jnp.zeros_like(query_s)
        key_s[...] = jnp.zeros_like(key_s)
        value_s[...] = jnp.zeros_like(value_s)
    states = jnp.concatenate([piece[...] for piece in pieces], axis=1)
    square = jnp.sum(jnp.square(states.astype(jnp.float32)), axis=1, keepdims=True)
    scale = lax.rsqrt(square / (cols * head_count) + norm_eps)
    cosine, sine = cos_ref[...], sin_ref[...]
    for c, target in enumerate((query_s, key_s, value_s)):
        projected = scale * jnp.dot(
            states,
            w_qkv_ref[c].reshape(head_count * cols, cols),
            preferred_element_type=jnp.float32,
        )
        for h in range(heads_local):
            part = projected[:, h * LANES : (h + 1) * LANES]
            if c < 2:
                part = part * cosine + pltpu.roll(part, LANES // 2, 1) * sine
            target[:, h, :] = part.astype(jnp.bfloat16).astype(jnp.float32)

    column = lax.broadcasted_iota(jnp.int32, (2 * SUBLANES, chunk_rows), 1)
    row = lax.broadcasted_iota(jnp.int32, (2 * SUBLANES, chunk_rows), 0)
    same_head = column % heads_local == row % SUBLANES
    upper = row < SUBLANES
    score_scale = LANES**-0.5
    blank = jnp.zeros((SUBLANES, LANES), jnp.float32)

    def diagonal(a, b):
        return jnp.concatenate(
            [jnp.concatenate([a, blank], axis=1), jnp.concatenate([blank, b], axis=1)], axis=0
        )

    @pl.loop(0, rows // GROUP)
    def _(g):
        requests = [g * GROUP + i for i in range(GROUP)]
        pairs = list(zip(requests[::2], requests[1::2]))
        lengths = [lengths_ref[r] for r in requests]
        spans = list(zip(lengths[::2], lengths[1::2]))
        queries = [diagonal(query_s[a], query_s[b]).astype(jnp.bfloat16) for a, b in pairs]
        own = [
            jnp.sum(query_s[r] * key_s[r], axis=1, keepdims=True) * score_scale for r in requests
        ]
        own = [jnp.concatenate([a, b], axis=0) for a, b in zip(own[::2], own[1::2])]
        values = [diagonal(value_s[a], value_s[b]) for a, b in pairs]
        longest = functools.reduce(jnp.maximum, lengths)
        used = used_rows(sum((length + 7) // 8 * 8 for length in lengths), heads_local)
        cache_copy(k_ref, k_s, k_sem, g * GROUP, used).wait()
        cache_copy(v_ref, v_s, v_sem, g * GROUP, used).wait()

        def with_chunks(count):
            def both(ref, c, pair, span):
                parts = []
                for r, length in zip(pair, span):
                    first = jnp.minimum(c, (length - 1) // CHUNK) * chunk_rows if c else 0
                    first = pl.multiple_of(r * cache_rows + first, chunk_rows)
                    parts.append(ref[pl.ds(first, chunk_rows)])
                return jnp.concatenate(parts, axis=1)

            scores = [
                [
                    lax.dot_general(
                        query,
                        both(k_s, c, pair, span),
                        (((1,), (1,)), ((), ())),
                        preferred_element_type=jnp.float32,
                    )
                    for c in range(count)
                ]
                for query, pair, span in zip(queries, pairs, spans)
            ]
            limits = [
                jnp.where(upper, span[0] * heads_local, span[1] * heads_local) for span in spans
            ]
            scores = [
                [
                    jnp.where(
                        same_head & (column < limit - c * chunk_rows), score * score_scale, MASKED
                    )
                    for c, score in enumerate(parts)
                ]
                for limit, parts in zip(limits, scores)
            ]
            tops = [
                jnp.maximum(
                    mine, jnp.max(functools.reduce(jnp.maximum, parts), axis=1, keepdims=True)
                )
                for mine, parts in zip(own, scores)
            ]
            weights = [[jnp.exp(part - top) for part in parts] for top, parts in zip(tops, scores)]
            faded = [jnp.exp(mine - top) for mine, top in zip(own, tops)]
            totals = [
                fade + jnp.sum(functools.reduce(jnp.add, parts), axis=1, keepdims=True)
                for fade, parts in zip(faded, weights)
            ]
            sums = [
                fade * value
                + sum(
                    jnp.dot(
                        part.astype(jnp.bfloat16),
                        both(v_s, c, pair, span),
                        preferred_element_type=jnp.float32,
                    )
                    for c, part in enumerate(parts)
                )
                for pair, span, fade, value, parts in zip(pairs, spans, faded, values, weights)
            ]
            for (a, b), total, summed in zip(pairs, totals, sums):
                summed = summed / total
                attended_s[a] = summed[:SUBLANES, :LANES]
                attended_s[b] = summed[SUBLANES:, LANES:]

        for count in range(1, cache_rows // chunk_rows + 1):
            pl.when((longest + CHUNK - 1) // CHUNK == count)(
                functools.partial(with_chunks, count)
            )

    attended = jnp.concatenate(
        [attended_s[:, h, :] for h in range(heads_local)], axis=1
    ).astype(jnp.bfloat16)
    for j in range(head_count):
        out_copy(j).wait()
        target = send_ref if j % 2 else keep_ref
        target[:, j // 2 * cols : (j // 2 + 1) * cols] = jnp.dot(
            attended, w_out_s[j], preferred_element_type=jnp.float32
        ).astype(jnp.bfloat16)
    for j in range(head_count):
        down_copy(j).wait()


def attention(pieces, me, lengths, cosine, sine, w_qkv, room, w_out, k_cache, v_cache, w_down):
    head_count = len(pieces)
    rows, cols = pieces[0].shape
    half = jax.ShapeDtypeStruct((rows, head_count // 2 * cols), jnp.bfloat16)
    return pl.pallas_call(
        functools.partial(attention_kernel, head_count),
        out_shape=(
            half,
            half,
            pltpu.VMEM(room.shape, jnp.bfloat16),
            pltpu.VMEM((head_count, w_down.shape[0], cols), jnp.bfloat16),
        ),
        in_specs=[SMEM, SMEM] + [VMEM] * (head_count + 4) + [ANY] * 4,
        out_specs=(VMEM, VMEM, VMEM, VMEM),
        input_output_aliases={head_count + 5: 2},
        scratch_shapes=[
            pltpu.VMEM((head_count, cols, cols), jnp.bfloat16),
            pltpu.VMEM(k_cache.shape, jnp.bfloat16),
        ]
        + [pltpu.VMEM((rows, SUBLANES, LANES), jnp.float32)] * 4
        + [
            pltpu.SemaphoreType.DMA((head_count,)),
            pltpu.SemaphoreType.DMA((rows // GROUP,)),
            pltpu.SemaphoreType.DMA((rows // GROUP,)),
            pltpu.SemaphoreType.DMA((head_count,)),
        ],
        compiler_params=pltpu.CompilerParams(vmem_limit_bytes=20 * 2**20),
        cost_estimate=pl.CostEstimate(
            flops=2 * rows * 4 * cols * head_count * cols,
            bytes_accessed=2 * w_down.size + k_cache.size // 2,
            transcendentals=0,
        ),
        name="attention",
    )(
        pltpu.with_memory_space_constraint(lengths, pltpu.SMEM), me, in_vmem(cosine), in_vmem(sine), *map(in_vmem, pieces), in_vmem(w_qkv), in_vmem(room),
        in_hbm(w_out), in_hbm(k_cache), in_hbm(v_cache), in_hbm(w_down),
    )


RELAYOUT_ROWS = 128
RELAYOUT_STEP = 16

def slot_of(j, head_count):
    return j // 2 + j % 2 * (head_count // 2)


def relayout_kernel(js, me_ref, w_ref, *refs):
    out_ref, token_ref, in_s, in_sem = refs[-4:]
    token_ref[...] = jnp.zeros_like(token_ref)
    experts, head_count, cols, _ = out_ref.shape
    step = in_s.shape[1]
    per_block = cols // step
    copies = []
    for at, j in enumerate(js):
        base = (me_ref[0] ^ j) * cols
        for i in range(per_block):
            slot = at * per_block + i
            first = pl.multiple_of(base + i * step, step)
            copies.append(
                pltpu.make_async_copy(
                    w_ref.at[pl.ds(first, step)], in_s.at[slot], in_sem.at[slot]
                )
            )
    for copy in copies:
        copy.start()
    for slot, copy in enumerate(copies):
        j, i = js[slot // per_block], slot % per_block
        copy.wait()
        for s in range(step // RELAYOUT_STEP):
            part = in_s[slot, pl.ds(s * RELAYOUT_STEP, RELAYOUT_STEP)]
            out_ref[:, slot_of(j, head_count), pl.ds(i * step + s * RELAYOUT_STEP, RELAYOUT_STEP), :] = jnp.swapaxes(
                part, 0, 1
            )


def by_expert(js, me, w_in, head_count, buffer, after):
    width, experts, columns = w_in.shape
    cols = width // head_count
    step = min(RELAYOUT_ROWS, cols)
    slots = len(js) * cols // step
    held = [] if buffer is None else [in_vmem(buffer)]
    return pl.pallas_call(
        functools.partial(relayout_kernel, js),
        out_shape=(
            pltpu.VMEM((experts, head_count, cols, columns), jnp.bfloat16),
            jax.ShapeDtypeStruct((SUBLANES, LANES), jnp.float32),
        ),
        in_specs=[SMEM, ANY] + [VMEM] * len(held) + [ANY],
        out_specs=(VMEM, VMEM),
        input_output_aliases={2: 0} if held else {},
        scratch_shapes=[
            pltpu.VMEM((slots, step, experts, columns), jnp.bfloat16),
            pltpu.SemaphoreType.DMA((slots,)),
        ],
        compiler_params=pltpu.CompilerParams(vmem_limit_bytes=16 * 2**20),
        cost_estimate=pl.CostEstimate(
            flops=0, bytes_accessed=4 * len(js) * cols * experts * columns, transcendentals=0
        ),
        name=f"by_expert_{js[0]}",
    )(me, in_hbm(w_in), *held, after)


def payload_kernel(head_count, *refs):
    blocks = head_count // 2
    pieces, (half_ref, *others), shares_ref = refs[:blocks], refs[blocks : 2 * blocks], refs[2 * blocks]
    payload_ref, resid_ref = refs[-2:]
    cols = pieces[0].shape[1]
    for t in range(blocks):
        total = pieces[t][...].astype(jnp.float32)
        for at, source in enumerate((half_ref, *others)):
            place = (t ^ at) * cols
            total += source[:, place : place + cols].astype(jnp.float32)
        payload_ref[:, t * cols : (t + 1) * cols] = total.astype(jnp.bfloat16)
        if t == 0:
            resid_ref[...] = total
    payload_ref[:, blocks * cols :] = shares_ref[...]


def payload_part(pieces, half, others, shares, after):
    blocks = len(pieces)
    rows, cols = pieces[0].shape
    return pl.pallas_call(
        functools.partial(payload_kernel, 2 * blocks),
        out_shape=(
            jax.ShapeDtypeStruct((rows, blocks * cols + shares.shape[1]), jnp.bfloat16),
            jax.ShapeDtypeStruct((rows, cols), jnp.float32),
        ),
        in_specs=[VMEM] * (2 * blocks + 1) + [ANY],
        out_specs=(VMEM, VMEM),
        compiler_params=pltpu.CompilerParams(vmem_limit_bytes=8 * 2**20),
        name="payload",
    )(*pieces, half, *others, shares, after)


def stack_kernel(count, *refs):
    rows = refs[0].shape[0]
    for i in range(count):
        refs[-1][i * rows : (i + 1) * rows, :] = refs[i][...]


def stack_part(parts, after):
    rows, columns = parts[0].shape
    return pl.pallas_call(
        functools.partial(stack_kernel, len(parts)),
        out_shape=jax.ShapeDtypeStruct((len(parts) * rows, columns), jnp.bfloat16),
        in_specs=[VMEM] * len(parts) + [ANY],
        out_specs=VMEM,
        compiler_params=pltpu.CompilerParams(vmem_limit_bytes=8 * 2**20),
        name="stack",
    )(*parts, after)


def expert_products(states, w_ref, first, p, per_step):
    columns = w_ref.shape[3]
    depth = states.shape[1]
    taken = pl.ds(first, depth // w_ref.shape[2])
    products = [
        jnp.dot(
            states,
            w_ref[p * per_step + i, taken].reshape(depth, columns),
            preferred_element_type=jnp.float32,
        )
        for i in range(per_step)
    ]
    return products[0] if per_step == 1 else jnp.concatenate(products, axis=1)


def steps_of(w_shape):
    per_step = max(1, 2 * LANES // w_shape[3])
    return w_shape[0] // per_step, per_step


def square_sum(ref, depth):
    return jnp.sum(jnp.square(ref[:, :depth].astype(jnp.float32)), axis=1, keepdims=True)


def local_shares(me, shares, experts):
    lanes = shares.shape[1]
    return pltpu.roll(shares.astype(jnp.float32), lax.rem(lanes - me * experts, lanes), 1)


def units_step(p, per_step, product, scale, shares):
    tokens = product.shape[0]
    first_half = lax.broadcasted_iota(jnp.int32, (tokens, LANES), 1) < LANES // 2
    expert = p * per_step
    share = shares[:, expert : expert + 1]
    if per_step == 2:
        share = jnp.where(first_half, share, shares[:, expert + 1 : expert + 2])
    a, b = product[:, :LANES], product[:, LANES:]
    gate = jnp.where(first_half, a, pltpu.roll(b, LANES // 2, 1)) * scale
    upward = jnp.where(first_half, pltpu.roll(a, LANES // 2, 1), b) * (scale * 0.5)
    return (share * (gate * (1.0 + jnp.tanh(gate * 0.5)) * upward)).astype(jnp.bfloat16)


def whole_kernel(me_ref, mine_ref, other_ref, w_ref, _, units_ref, states_s):
    experts, head_count, cols, _ = w_ref.shape
    depth = head_count // 2 * cols
    states_s[:, :depth] = mine_ref[:, :depth]
    states_s[:, depth:] = other_ref[:, :depth]
    square = square_sum(mine_ref, depth) + square_sum(other_ref, depth)
    scale = lax.rsqrt(square / (2 * depth) + norm_eps)
    shares = local_shares(me_ref[0], mine_ref[:, depth:], experts)
    steps, per_step = steps_of(w_ref.shape)
    for p in range(steps):
        product = expert_products(states_s[...], w_ref, 0, p, per_step)
        units_ref[:, p * LANES : (p + 1) * LANES] = units_step(
            p, per_step, product, scale, shares
        )


def first_kernel(mine_ref, w_ref, _, product_ref):
    _, head_count, cols, _ = w_ref.shape
    steps, per_step = steps_of(w_ref.shape)

    @pl.loop(0, steps, unroll=4)
    def _(p):
        states = mine_ref[:, : head_count // 2 * cols]
        product_ref[p] = expert_products(states, w_ref, 0, p, per_step)


def second_kernel(me_ref, mine_ref, other_ref, product_ref, w_ref, w_down_ref, units_ref, send_ref):
    experts, head_count, cols, _ = w_ref.shape
    depth = head_count // 2 * cols
    square = square_sum(mine_ref, depth) + square_sum(other_ref, depth)
    scale = lax.rsqrt(square / (2 * depth) + norm_eps)
    shares = local_shares(me_ref[0], mine_ref[:, depth:], experts)
    steps, per_step = steps_of(w_ref.shape)
    for p in range(steps):
        product = product_ref[p] + expert_products(
            other_ref[:, :depth], w_ref, head_count // 2, p, per_step
        )
        units_ref[:, p * LANES : (p + 1) * LANES] = units_step(
            p, per_step, product, scale, shares
        )

    down_blocks(units_ref[...], w_down_ref, 1, send_ref)


def experts_whole(me, mine, other, weights, after, total_units):
    experts, head_count, cols, columns = weights.shape
    tokens = mine.shape[0]
    return pl.pallas_call(
        whole_kernel,
        out_shape=jax.ShapeDtypeStruct((tokens, total_units), jnp.bfloat16),
        in_specs=[SMEM] + [VMEM] * 3 + [ANY],
        out_specs=VMEM,
        scratch_shapes=[pltpu.VMEM((tokens, head_count * cols), jnp.bfloat16)],
        compiler_params=pltpu.CompilerParams(vmem_limit_bytes=12 * 2**20),
        cost_estimate=pl.CostEstimate(
            flops=2 * tokens * head_count * cols * experts * columns,
            bytes_accessed=2 * head_count * cols * experts * columns,
            transcendentals=0,
        ),
        name="experts_whole",
    )(me, mine, other, in_vmem(weights), after)


def experts_first(mine, weights, after):
    experts, head_count, cols, columns = weights.shape
    tokens = mine.shape[0]
    steps, per_step = steps_of(weights.shape)
    return pl.pallas_call(
        first_kernel,
        out_shape=jax.ShapeDtypeStruct((steps, tokens, per_step * columns), jnp.float32),
        in_specs=[VMEM] * 2 + [ANY],
        out_specs=VMEM,
        compiler_params=pltpu.CompilerParams(vmem_limit_bytes=12 * 2**20),
        cost_estimate=pl.CostEstimate(
            flops=tokens * head_count * cols * experts * columns,
            bytes_accessed=head_count * cols * experts * columns,
            transcendentals=0,
        ),
        name="experts_first",
    )(mine, in_vmem(weights), after)


def experts_second(me, mine, other, products, weights, w_down):
    experts, head_count, cols, columns = weights.shape
    tokens = mine.shape[0]
    return pl.pallas_call(
        second_kernel,
        out_shape=(
            jax.ShapeDtypeStruct((tokens, w_down.shape[1]), jnp.bfloat16),
            jax.ShapeDtypeStruct((tokens, head_count // 2 * cols), jnp.bfloat16),
        ),
        in_specs=[SMEM] + [VMEM] * 5,
        out_specs=(VMEM, VMEM),
        compiler_params=pltpu.CompilerParams(vmem_limit_bytes=12 * 2**20),
        cost_estimate=pl.CostEstimate(
            flops=tokens * head_count * cols * experts * columns,
            bytes_accessed=head_count * cols * experts * columns,
            transcendentals=0,
        ),
        name="experts_second",
    )(me, mine, other, products, in_vmem(weights), in_vmem(w_down))


def down_blocks(units, w_ref, first, out_ref):
    cols = w_ref.shape[2]
    for t in range(w_ref.shape[0] // 2):
        out_ref[:, t * cols : (t + 1) * cols] = jnp.dot(
            units, w_ref[2 * t + first], preferred_element_type=jnp.float32
        ).astype(jnp.bfloat16)


def down_kernel(firsts, units_ref, w_ref, *outs):
    for first, out_ref in zip(firsts, outs):
        down_blocks(units_ref[...], w_ref, first, out_ref)


def down_part(units, w_down, firsts):
    head_count, total_units, cols = w_down.shape
    tokens = units.shape[0]
    half = jax.ShapeDtypeStruct((tokens, head_count // 2 * cols), jnp.bfloat16)
    return pl.pallas_call(
        functools.partial(down_kernel, firsts),
        out_shape=[half] * len(firsts),
        in_specs=[VMEM, VMEM],
        out_specs=[VMEM] * len(firsts),
        compiler_params=pltpu.CompilerParams(vmem_limit_bytes=12 * 2**20),
        cost_estimate=pl.CostEstimate(
            flops=len(firsts) * tokens * total_units * head_count * cols,
            bytes_accessed=len(firsts) * total_units * head_count * cols,
            transcendentals=0,
        ),
        name="down",
    )(units, in_vmem(w_down))


def hold_kernel(value_ref, after_ref, out_ref):
    pass


def hold(value, after):
    return pl.pallas_call(
        hold_kernel,
        out_shape=jax.ShapeDtypeStruct(value.shape, value.dtype),
        in_specs=[ANY, ANY],
        out_specs=ANY,
        input_output_aliases={0: 0},
        compiler_params=pltpu.CompilerParams(vmem_limit_bytes=2**20),
        name="hold",
    )(value, after)


def sum_kernel(keep_ref, sent_ref, *outs):
    cols = outs[0].shape[1]
    for t, out in enumerate(outs):
        part = slice(t * cols, (t + 1) * cols)
        total = keep_ref[:, part].astype(jnp.float32) + sent_ref[:, part].astype(jnp.float32)
        out[...] = total.astype(out.dtype)


def sum_part(keep, sent, cols, first_type):
    tokens, columns = keep.shape
    blocks = columns // cols
    return pl.pallas_call(
        sum_kernel,
        out_shape=[
            jax.ShapeDtypeStruct((tokens, cols), jnp.bfloat16 if t else first_type)
            for t in range(blocks)
        ],
        in_specs=[VMEM, VMEM],
        out_specs=[VMEM] * blocks,
        compiler_params=pltpu.CompilerParams(vmem_limit_bytes=8 * 2**20),
        name="sum",
    )(keep, sent)


def swap(value, axis, size, mask):
    return lax.ppermute(value, axis, [(i, i ^ mask) for i in range(size)])


def per_device(
    hidden, lengths, expert_ids, route_weights, w_qkv, w_out, k_cache, v_cache, w_in, w_down
):
    req_size = lax.axis_size("req")
    head_size = lax.axis_size("head")
    me = lax.axis_index("head")
    me_ref = me[None].astype(jnp.int32)
    rows, cols = hidden.shape
    experts_local, units_local, width = w_down.shape
    even = range(0, head_size, 2)

    pieces = [hidden] + [swap(hidden, "head", head_size, j) for j in range(1, head_size)]
    flat = (rows * k_cache.shape[1] * k_cache.shape[2], k_cache.shape[3])
    own, w_near, room, cosine, sine, lengths_near, shares = fetch(
        me_ref, lengths, hidden, w_qkv, flat, head_size, expert_ids, route_weights,
        head_size * experts_local,
    )
    pieces[0] = own
    keep, send, _, w_down_near = attention(
        pieces,
        me_ref,
        lengths_near,
        cosine,
        sine,
        w_near,
        room,
        w_out,
        k_cache.reshape(flat),
        v_cache.reshape(flat),
        w_down.reshape(experts_local * units_local, width),
    )
    (half,) = sum_part(keep, swap(send, "head", head_size, 1), keep.shape[1], jnp.bfloat16)
    others = [swap(half, "head", head_size, j) for j in even if j]
    early, late = range(head_size // 2), range(head_size // 2, head_size)
    buffer, token = by_expert(tuple(early), me_ref, w_in, head_size, None, half)

    payload, resid = payload_part(
        [pieces[j] for j in even], half, others, shares, token
    )

    steps = range(2, req_size, 2)
    line = [payload] + [swap(payload, "req", req_size, k) for k in steps]
    buffer, token = by_expert(tuple(late), me_ref, w_in, head_size, buffer, payload)
    line = stack_part(line, token)
    line_other = swap(line, "head", head_size, 1)
    crossed = swap(line, "req", req_size, 1)
    units = experts_whole(me_ref, line, line_other, buffer, token, w_down_near.shape[1])
    keep, send = down_part(units, w_down_near, (0, 1))
    crossed = hold(crossed, send)
    crossed_other = swap(crossed, "head", head_size, 1)
    line_sums = sum_part(keep, swap(send, "head", head_size, 1), cols, jnp.float32)
    total = line_sums[0]
    products = experts_first(crossed, buffer, line_sums[-1])
    units, send = experts_second(me_ref, crossed, crossed_other, products, buffer, w_down_near)
    (keep,) = down_part(units, w_down_near, (0,))
    crossed_sums = sum_part(keep, swap(send, "head", head_size, 1), cols, jnp.bfloat16)
    got = [
        swap(hold(line_sums[j // 2], crossed_sums[0]), "head", head_size, j) for j in even if j
    ]
    for j in even:
        pairs = [
            (r * head_size + h, (r ^ 1) * head_size + (h ^ j))
            for r in range(req_size)
            for h in range(head_size)
        ]
        got.append(lax.ppermute(crossed_sums[j // 2], ("req", "head"), pairs))
    for part in got:
        total = total + part.astype(jnp.float32)
    chunks = total.astype(jnp.bfloat16).reshape(req_size // 2, rows, cols)
    out = chunks[0].astype(jnp.float32)
    for k in steps:
        out = out + swap(chunks[k // 2], "req", req_size, k).astype(jnp.float32)
    return (out + resid).astype(jnp.bfloat16)


def solution(mesh):
    in_specs = (
        P("req", "head"),
        P("req"),
        P("req", None),
        P("req", None),
        P(None, None, "head"),
        P("head", None),
        P("req", None, "head", None),
        P("req", None, "head", None),
        P(None, "head", "req"),
        P("head", "req", None),
    )
    out_specs = P("req", "head")
    return jax.shard_map(
        per_device, mesh=mesh, in_specs=in_specs, out_specs=out_specs, check_vma=False
    )
```

```python
import functools
import itertools
import jax
import jax.numpy as jnp
from jax import lax
from jax.experimental import pallas as pl
from jax.experimental.pallas import tpu as pltpu
from jax.sharding import PartitionSpec as P

rope_theta = 50000.0
norm_eps = 1e-05
LANES = 128
SUBLANES = 8
CHUNK = 96
GROUP = 8
TOGETHER = 1
MASKED = -1e30


VMEM = pl.BlockSpec(memory_space=pltpu.VMEM)
SMEM = pl.BlockSpec(memory_space=pltpu.SMEM)
ANY = pl.BlockSpec(memory_space=pl.ANY)


def in_hbm(array):
    return pltpu.with_memory_space_constraint(array, pltpu.HBM)


def in_vmem(array):
    return pltpu.with_memory_space_constraint(array, pltpu.VMEM)


def used_rows(length, heads_local):
    return pl.multiple_of((length + 7) // 8 * (8 * heads_local), 8 * heads_local)


def fetch_kernel(
    lengths_hbm, me_ref, freqs_ref, own_ref, w_ref, ids_ref, route_ref,
    own_out_ref, w_out_ref, blank_ref, cos_ref, sin_ref, lengths_ref, shares_ref,
    angle_s, ids_s, route_s, sem, small_sem,
):
    head_count, cols = w_out_ref.shape[1:3]
    chunk_rows = CHUNK * cols // LANES
    me = me_ref[0]
    lengths_copy, *copies = [
        pltpu.make_async_copy(source, target, small_sem.at[i])
        for i, (source, target) in enumerate(
            (
                (lengths_hbm, lengths_ref),
                (ids_ref, ids_s),
                (route_ref, route_s),
                (own_ref, own_out_ref),
            )
        )
    ]
    small = copies[:2]
    for c in range(w_ref.shape[0]):
        for j in range(head_count):
            first = pl.multiple_of((me ^ j) * cols, cols)
            copies.append(
                pltpu.make_async_copy(
                    w_ref.at[c, pl.ds(first, cols)], w_out_ref.at[c, j], sem.at[c, j]
                )
            )
    lengths_copy.start()
    for copy in copies:
        copy.start()
    lengths_copy.wait()

    rows = angle_s.shape[0]
    cache_rows = blank_ref.shape[0] // rows

    @pl.loop(0, rows)
    def _(r):
        last = r * cache_rows + (lengths_ref[r] - 1) // CHUNK * chunk_rows
        blank_ref[pl.ds(pl.multiple_of(last, chunk_rows), chunk_rows)] = jnp.zeros(
            (chunk_rows, LANES), jnp.bfloat16
        )
        angle_s[pl.ds(r, 1), :] = lengths_ref[r].astype(jnp.float32) * freqs_ref[...]

    cos_ref[...] = jnp.cos(angle_s[...])
    lane = lax.broadcasted_iota(jnp.int32, sin_ref.shape, 1)
    sine = jnp.sin(angle_s[...])
    sin_ref[...] = jnp.where(lane < LANES // 2, -sine, sine)
    for copy in small:
        copy.wait()
    expert = lax.broadcasted_iota(jnp.int32, (shares_ref.shape[1], rows), 0)
    shares = jnp.zeros(expert.shape, jnp.float32)
    for k in range(ids_s.shape[0]):
        shares += jnp.where(expert == ids_s[k : k + 1, :], route_s[k : k + 1, :], 0.0)
    shares_ref[...] = jnp.transpose(shares, (1, 0)).astype(jnp.bfloat16)
    for copy in copies[2:]:
        copy.wait()


def fetch(me, lengths, hidden, w_qkv, v_shape, head_count, expert_ids, route_weights, experts):
    cols = w_qkv.shape[2]
    rows = hidden.shape[0]
    exponents = jnp.arange(LANES, dtype=jnp.float32) % (LANES // 2) / (LANES // 2)
    freqs = (rope_theta**-exponents)[None, :]
    return pl.pallas_call(
        fetch_kernel,
        out_shape=(
            pltpu.VMEM(hidden.shape, jnp.bfloat16),
            pltpu.VMEM((w_qkv.shape[0], head_count, cols, cols), jnp.bfloat16),
            pltpu.VMEM(v_shape, jnp.bfloat16),
            pltpu.VMEM((rows, LANES), jnp.float32),
            pltpu.VMEM((rows, LANES), jnp.float32),
            pltpu.SMEM(lengths.shape, lengths.dtype),
            pltpu.VMEM((rows, -(-experts // LANES) * LANES), jnp.bfloat16),
        ),
        in_specs=[ANY, SMEM, VMEM] + [ANY] * 4,
        out_specs=[VMEM] * 5 + [SMEM, VMEM],
        scratch_shapes=[
            pltpu.VMEM((rows, LANES), jnp.float32),
            pltpu.VMEM(expert_ids.shape[::-1], expert_ids.dtype),
            pltpu.VMEM(route_weights.shape[::-1], route_weights.dtype),
            pltpu.SemaphoreType.DMA((w_qkv.shape[0], head_count)),
            pltpu.SemaphoreType.DMA((4,)),
        ],
        compiler_params=pltpu.CompilerParams(vmem_limit_bytes=8 * 2**20),
        cost_estimate=pl.CostEstimate(
            flops=0, bytes_accessed=4 * w_qkv.size, transcendentals=0
        ),
        name="fetch",
    )(
        in_hbm(lengths), me, freqs, in_hbm(hidden), in_hbm(w_qkv), in_hbm(expert_ids.T),
        in_hbm(route_weights.T),
    )


def attention_kernel(head_count, lengths_ref, me_ref, cos_ref, sin_ref, *refs):
    pieces = refs[:head_count]
    (
        w_qkv_ref, _, w_out_ref, k_ref, v_ref, w_down_ref, keep_ref, send_ref, v_s, down_ref,
        w_out_s, k_s, query_s, key_s, value_s, attended_s, out_sem, k_sem, v_sem, down_sem,
    ) = refs[head_count:]
    rows, cols = pieces[0].shape
    heads_local = cols // LANES
    chunk_rows = CHUNK * heads_local
    me = me_ref[0]

    def out_copy(j):
        first = pl.multiple_of((me ^ j) * cols, cols)
        return pltpu.make_async_copy(
            w_out_ref.at[:, pl.ds(first, cols)], w_out_s.at[j], out_sem.at[j]
        )

    cache_rows = k_s.shape[0] // rows

    def cache_copy(source, target, sem, r, used):
        taken = pl.ds(pl.multiple_of(r * cache_rows, cache_rows), used)
        return pltpu.make_async_copy(
            source.at[taken], target.at[taken], sem.at[r // GROUP]
        )

    @pl.loop(0, rows, unroll=4)
    def _(r):
        used = used_rows(lengths_ref[r], heads_local)
        cache_copy(k_ref, k_s, k_sem, r, used).start()
        cache_copy(v_ref, v_s, v_sem, r, used).start()

    def down_copy(j):
        first = pl.multiple_of((me ^ j) * cols, cols)
        return pltpu.make_async_copy(
            w_down_ref.at[:, pl.ds(first, cols)], down_ref.at[j], down_sem.at[j]
        )

    for j in range(head_count):
        out_copy(j).start()
    for j in range(head_count):
        down_copy(j).start()

    if heads_local < SUBLANES:
        query_s[...] = jnp.zeros_like(query_s)
        key_s[...] = jnp.zeros_like(key_s)
        value_s[...] = jnp.zeros_like(value_s)
    states = jnp.concatenate([piece[...] for piece in pieces], axis=1)
    square = jnp.sum(jnp.square(states.astype(jnp.float32)), axis=1, keepdims=True)
    scale = lax.rsqrt(square / (cols * head_count) + norm_eps)
    cosine, sine = cos_ref[...], sin_ref[...]
    for c, target in enumerate((query_s, key_s, value_s)):
        projected = scale * jnp.dot(
            states,
            w_qkv_ref[c].reshape(head_count * cols, cols),
            preferred_element_type=jnp.float32,
        )
        for h in range(heads_local):
            part = projected[:, h * LANES : (h + 1) * LANES]
            if c < 2:
                part = part * cosine + pltpu.roll(part, LANES // 2, 1) * sine
            target[:, h, :] = part.astype(jnp.bfloat16).astype(jnp.float32)

    column = lax.broadcasted_iota(jnp.int32, (2 * SUBLANES, chunk_rows), 1)
    row = lax.broadcasted_iota(jnp.int32, (2 * SUBLANES, chunk_rows), 0)
    same_head = column % heads_local == row % SUBLANES
    upper = row < SUBLANES
    score_scale = LANES**-0.5
    blank = jnp.zeros((SUBLANES, LANES), jnp.float32)

    def diagonal(a, b):
        return jnp.concatenate(
            [jnp.concatenate([a, blank], axis=1), jnp.concatenate([blank, b], axis=1)], axis=0
        )

    @pl.loop(0, rows // (GROUP * TOGETHER))
    def _(step):
        requests = [step * GROUP * TOGETHER + i for i in range(GROUP * TOGETHER)]
        pairs = list(zip(requests[::2], requests[1::2]))
        lengths = [lengths_ref[r] for r in requests]
        spans = list(zip(lengths[::2], lengths[1::2]))
        queries = [diagonal(query_s[a], query_s[b]).astype(jnp.bfloat16) for a, b in pairs]
        own = [
            jnp.sum(query_s[r] * key_s[r], axis=1, keepdims=True) * score_scale for r in requests
        ]
        own = [jnp.concatenate([a, b], axis=0) for a, b in zip(own[::2], own[1::2])]
        values = [diagonal(value_s[a], value_s[b]) for a, b in pairs]
        needed = []
        for i in range(TOGETHER):
            part = lengths[i * GROUP : (i + 1) * GROUP]
            needed.append((functools.reduce(jnp.maximum, part) + CHUNK - 1) // CHUNK)
            used = used_rows(sum((length + 7) // 8 * 8 for length in part), heads_local)
            first = requests[i * GROUP]
            cache_copy(k_ref, k_s, k_sem, first, used).wait()
            cache_copy(v_ref, v_s, v_sem, first, used).wait()

        def with_chunks(counts):
            counts = [count for count in counts for _ in range(GROUP // 2)]

            def both(ref, c, pair, span):
                parts = []
                for r, length in zip(pair, span):
                    first = jnp.minimum(c, (length - 1) // CHUNK) * chunk_rows if c else 0
                    first = pl.multiple_of(r * cache_rows + first, chunk_rows)
                    parts.append(ref[pl.ds(first, chunk_rows)])
                return jnp.concatenate(parts, axis=1)

            scores = [
                [
                    lax.dot_general(
                        query,
                        both(k_s, c, pair, span),
                        (((1,), (1,)), ((), ())),
                        preferred_element_type=jnp.float32,
                    )
                    for c in range(count)
                ]
                for count, query, pair, span in zip(counts, queries, pairs, spans)
            ]
            limits = [
                jnp.where(upper, span[0] * heads_local, span[1] * heads_local) for span in spans
            ]
            scores = [
                [
                    jnp.where(
                        same_head & (column < limit - c * chunk_rows), score * score_scale, MASKED
                    )
                    for c, score in enumerate(parts)
                ]
                for limit, parts in zip(limits, scores)
            ]
            tops = [
                jnp.maximum(
                    mine, jnp.max(functools.reduce(jnp.maximum, parts), axis=1, keepdims=True)
                )
                for mine, parts in zip(own, scores)
            ]
            weights = [[jnp.exp(part - top) for part in parts] for top, parts in zip(tops, scores)]
            faded = [jnp.exp(mine - top) for mine, top in zip(own, tops)]
            totals = [
                fade + jnp.sum(functools.reduce(jnp.add, parts), axis=1, keepdims=True)
                for fade, parts in zip(faded, weights)
            ]
            sums = [
                fade * value
                + sum(
                    jnp.dot(
                        part.astype(jnp.bfloat16),
                        both(v_s, c, pair, span),
                        preferred_element_type=jnp.float32,
                    )
                    for c, part in enumerate(parts)
                )
                for pair, span, fade, value, parts in zip(pairs, spans, faded, values, weights)
            ]
            for (a, b), total, summed in zip(pairs, totals, sums):
                summed = summed / total
                attended_s[a] = summed[:SUBLANES, :LANES]
                attended_s[b] = summed[SUBLANES:, LANES:]

        most = cache_rows // chunk_rows
        for counts in itertools.product(range(1, most + 1), repeat=TOGETHER):
            chosen = functools.reduce(
                jnp.logical_and, [have == count for have, count in zip(needed, counts)]
            )
            pl.when(chosen)(functools.partial(with_chunks, counts))

    attended = jnp.concatenate(
        [attended_s[:, h, :] for h in range(heads_local)], axis=1
    ).astype(jnp.bfloat16)
    for j in range(head_count):
        out_copy(j).wait()
        target = send_ref if j % 2 else keep_ref
        target[:, j // 2 * cols : (j // 2 + 1) * cols] = jnp.dot(
            attended, w_out_s[j], preferred_element_type=jnp.float32
        ).astype(jnp.bfloat16)
    for j in range(head_count):
        down_copy(j).wait()


def attention(pieces, me, lengths, cosine, sine, w_qkv, room, w_out, k_cache, v_cache, w_down):
    head_count = len(pieces)
    rows, cols = pieces[0].shape
    half = jax.ShapeDtypeStruct((rows, head_count // 2 * cols), jnp.bfloat16)
    return pl.pallas_call(
        functools.partial(attention_kernel, head_count),
        out_shape=(
            half,
            half,
            pltpu.VMEM(room.shape, jnp.bfloat16),
            pltpu.VMEM((head_count, w_down.shape[0], cols), jnp.bfloat16),
        ),
        in_specs=[SMEM, SMEM] + [VMEM] * (head_count + 4) + [ANY] * 4,
        out_specs=(VMEM, VMEM, VMEM, VMEM),
        input_output_aliases={head_count + 5: 2},
        scratch_shapes=[
            pltpu.VMEM((head_count, cols, cols), jnp.bfloat16),
            pltpu.VMEM(k_cache.shape, jnp.bfloat16),
        ]
        + [pltpu.VMEM((rows, SUBLANES, LANES), jnp.float32)] * 4
        + [
            pltpu.SemaphoreType.DMA((head_count,)),
            pltpu.SemaphoreType.DMA((rows // GROUP,)),
            pltpu.SemaphoreType.DMA((rows // GROUP,)),
            pltpu.SemaphoreType.DMA((head_count,)),
        ],
        compiler_params=pltpu.CompilerParams(vmem_limit_bytes=20 * 2**20),
        cost_estimate=pl.CostEstimate(
            flops=2 * rows * 4 * cols * head_count * cols,
            bytes_accessed=2 * w_down.size + k_cache.size // 2,
            transcendentals=0,
        ),
        name="attention",
    )(
        pltpu.with_memory_space_constraint(lengths, pltpu.SMEM), me, in_vmem(cosine), in_vmem(sine), *map(in_vmem, pieces), in_vmem(w_qkv), in_vmem(room),
        in_hbm(w_out), in_hbm(k_cache), in_hbm(v_cache), in_hbm(w_down),
    )


RELAYOUT_ROWS = 128
RELAYOUT_STEP = 16

def slot_of(j, head_count):
    return j // 2 + j % 2 * (head_count // 2)


def relayout_kernel(js, me_ref, w_ref, *refs):
    out_ref, token_ref, in_s, in_sem = refs[-4:]
    token_ref[...] = jnp.zeros_like(token_ref)
    experts, head_count, cols, _ = out_ref.shape
    step = in_s.shape[1]
    per_block = cols // step
    copies = []
    for at, j in enumerate(js):
        base = (me_ref[0] ^ j) * cols
        for i in range(per_block):
            slot = at * per_block + i
            first = pl.multiple_of(base + i * step, step)
            copies.append(
                pltpu.make_async_copy(
                    w_ref.at[pl.ds(first, step)], in_s.at[slot], in_sem.at[slot]
                )
            )
    for copy in copies:
        copy.start()
    for slot, copy in enumerate(copies):
        j, i = js[slot // per_block], slot % per_block
        copy.wait()
        for s in range(step // RELAYOUT_STEP):
            part = in_s[slot, pl.ds(s * RELAYOUT_STEP, RELAYOUT_STEP)]
            out_ref[:, slot_of(j, head_count), pl.ds(i * step + s * RELAYOUT_STEP, RELAYOUT_STEP), :] = jnp.swapaxes(
                part, 0, 1
            )


def by_expert(js, me, w_in, head_count, buffer, after):
    width, experts, columns = w_in.shape
    cols = width // head_count
    step = min(RELAYOUT_ROWS, cols)
    slots = len(js) * cols // step
    held = [] if buffer is None else [in_vmem(buffer)]
    return pl.pallas_call(
        functools.partial(relayout_kernel, js),
        out_shape=(
            pltpu.VMEM((experts, head_count, cols, columns), jnp.bfloat16),
            jax.ShapeDtypeStruct((SUBLANES, LANES), jnp.float32),
        ),
        in_specs=[SMEM, ANY] + [VMEM] * len(held) + [ANY],
        out_specs=(VMEM, VMEM),
        input_output_aliases={2: 0} if held else {},
        scratch_shapes=[
            pltpu.VMEM((slots, step, experts, columns), jnp.bfloat16),
            pltpu.SemaphoreType.DMA((slots,)),
        ],
        compiler_params=pltpu.CompilerParams(vmem_limit_bytes=16 * 2**20),
        cost_estimate=pl.CostEstimate(
            flops=0, bytes_accessed=4 * len(js) * cols * experts * columns, transcendentals=0
        ),
        name=f"by_expert_{js[0]}",
    )(me, in_hbm(w_in), *held, after)


def payload_kernel(head_count, *refs):
    blocks = head_count // 2
    pieces, (half_ref, *others), shares_ref = refs[:blocks], refs[blocks : 2 * blocks], refs[2 * blocks]
    payload_ref, resid_ref = refs[-2:]
    cols = pieces[0].shape[1]
    for t in range(blocks):
        total = pieces[t][...].astype(jnp.float32)
        for at, source in enumerate((half_ref, *others)):
            place = (t ^ at) * cols
            total += source[:, place : place + cols].astype(jnp.float32)
        payload_ref[:, t * cols : (t + 1) * cols] = total.astype(jnp.bfloat16)
        if t == 0:
            resid_ref[...] = total
    payload_ref[:, blocks * cols :] = shares_ref[...]


def payload_part(pieces, half, others, shares, after):
    blocks = len(pieces)
    rows, cols = pieces[0].shape
    return pl.pallas_call(
        functools.partial(payload_kernel, 2 * blocks),
        out_shape=(
            jax.ShapeDtypeStruct((rows, blocks * cols + shares.shape[1]), jnp.bfloat16),
            jax.ShapeDtypeStruct((rows, cols), jnp.float32),
        ),
        in_specs=[VMEM] * (2 * blocks + 1) + [ANY],
        out_specs=(VMEM, VMEM),
        compiler_params=pltpu.CompilerParams(vmem_limit_bytes=8 * 2**20),
        name="payload",
    )(*pieces, half, *others, shares, after)


def stack_kernel(count, *refs):
    rows = refs[0].shape[0]
    for i in range(count):
        refs[-1][i * rows : (i + 1) * rows, :] = refs[i][...]


def stack_part(parts, after):
    rows, columns = parts[0].shape
    return pl.pallas_call(
        functools.partial(stack_kernel, len(parts)),
        out_shape=jax.ShapeDtypeStruct((len(parts) * rows, columns), jnp.bfloat16),
        in_specs=[VMEM] * len(parts) + [ANY],
        out_specs=VMEM,
        compiler_params=pltpu.CompilerParams(vmem_limit_bytes=8 * 2**20),
        name="stack",
    )(*parts, after)


def expert_products(states, w_ref, first, p, per_step):
    columns = w_ref.shape[3]
    depth = states.shape[1]
    taken = pl.ds(first, depth // w_ref.shape[2])
    products = [
        jnp.dot(
            states,
            w_ref[p * per_step + i, taken].reshape(depth, columns),
            preferred_element_type=jnp.float32,
        )
        for i in range(per_step)
    ]
    return products[0] if per_step == 1 else jnp.concatenate(products, axis=1)


def steps_of(w_shape):
    per_step = max(1, 2 * LANES // w_shape[3])
    return w_shape[0] // per_step, per_step


def square_sum(ref, depth):
    return jnp.sum(jnp.square(ref[:, :depth].astype(jnp.float32)), axis=1, keepdims=True)


def local_shares(me, shares, experts):
    lanes = shares.shape[1]
    return pltpu.roll(shares.astype(jnp.float32), lax.rem(lanes - me * experts, lanes), 1)


def units_step(p, per_step, product, scale, shares):
    tokens = product.shape[0]
    first_half = lax.broadcasted_iota(jnp.int32, (tokens, LANES), 1) < LANES // 2
    expert = p * per_step
    share = shares[:, expert : expert + 1]
    if per_step == 2:
        share = jnp.where(first_half, share, shares[:, expert + 1 : expert + 2])
    a, b = product[:, :LANES], product[:, LANES:]
    gate = jnp.where(first_half, a, pltpu.roll(b, LANES // 2, 1)) * scale
    upward = jnp.where(first_half, pltpu.roll(a, LANES // 2, 1), b) * (scale * 0.5)
    return (share * (gate * (1.0 + jnp.tanh(gate * 0.5)) * upward)).astype(jnp.bfloat16)


def whole_kernel(me_ref, mine_ref, other_ref, w_ref, _, units_ref, states_s):
    experts, head_count, cols, _ = w_ref.shape
    depth = head_count // 2 * cols
    states_s[:, :depth] = mine_ref[:, :depth]
    states_s[:, depth:] = other_ref[:, :depth]
    square = square_sum(mine_ref, depth) + square_sum(other_ref, depth)
    scale = lax.rsqrt(square / (2 * depth) + norm_eps)
    shares = local_shares(me_ref[0], mine_ref[:, depth:], experts)
    steps, per_step = steps_of(w_ref.shape)
    for p in range(steps):
        product = expert_products(states_s[...], w_ref, 0, p, per_step)
        units_ref[:, p * LANES : (p + 1) * LANES] = units_step(
            p, per_step, product, scale, shares
        )


def first_kernel(mine_ref, w_ref, _, product_ref):
    _, head_count, cols, _ = w_ref.shape
    steps, per_step = steps_of(w_ref.shape)
    for p in range(steps):
        states = mine_ref[:, : head_count // 2 * cols]
        product_ref[p] = expert_products(states, w_ref, 0, p, per_step)


def second_kernel(me_ref, mine_ref, other_ref, product_ref, w_ref, w_down_ref, units_ref, send_ref):
    experts, head_count, cols, _ = w_ref.shape
    depth = head_count // 2 * cols
    square = square_sum(mine_ref, depth) + square_sum(other_ref, depth)
    scale = lax.rsqrt(square / (2 * depth) + norm_eps)
    shares = local_shares(me_ref[0], mine_ref[:, depth:], experts)
    steps, per_step = steps_of(w_ref.shape)
    for p in range(steps):
        product = product_ref[p] + expert_products(
            other_ref[:, :depth], w_ref, head_count // 2, p, per_step
        )
        units_ref[:, p * LANES : (p + 1) * LANES] = units_step(
            p, per_step, product, scale, shares
        )

    down_blocks(units_ref[...], w_down_ref, 1, send_ref)


def experts_whole(me, mine, other, weights, after, total_units):
    experts, head_count, cols, columns = weights.shape
    tokens = mine.shape[0]
    return pl.pallas_call(
        whole_kernel,
        out_shape=jax.ShapeDtypeStruct((tokens, total_units), jnp.bfloat16),
        in_specs=[SMEM] + [VMEM] * 3 + [ANY],
        out_specs=VMEM,
        scratch_shapes=[pltpu.VMEM((tokens, head_count * cols), jnp.bfloat16)],
        compiler_params=pltpu.CompilerParams(vmem_limit_bytes=12 * 2**20),
        cost_estimate=pl.CostEstimate(
            flops=2 * tokens * head_count * cols * experts * columns,
            bytes_accessed=2 * head_count * cols * experts * columns,
            transcendentals=0,
        ),
        name="experts_whole",
    )(me, mine, other, in_vmem(weights), after)


def experts_first(mine, weights, after):
    experts, head_count, cols, columns = weights.shape
    tokens = mine.shape[0]
    steps, per_step = steps_of(weights.shape)
    return pl.pallas_call(
        first_kernel,
        out_shape=jax.ShapeDtypeStruct((steps, tokens, per_step * columns), jnp.float32),
        in_specs=[VMEM] * 2 + [ANY],
        out_specs=VMEM,
        compiler_params=pltpu.CompilerParams(vmem_limit_bytes=12 * 2**20),
        cost_estimate=pl.CostEstimate(
            flops=tokens * head_count * cols * experts * columns,
            bytes_accessed=head_count * cols * experts * columns,
            transcendentals=0,
        ),
        name="experts_first",
    )(mine, in_vmem(weights), after)


def experts_second(me, mine, other, products, weights, w_down):
    experts, head_count, cols, columns = weights.shape
    tokens = mine.shape[0]
    return pl.pallas_call(
        second_kernel,
        out_shape=(
            jax.ShapeDtypeStruct((tokens, w_down.shape[1]), jnp.bfloat16),
            jax.ShapeDtypeStruct((tokens, head_count // 2 * cols), jnp.bfloat16),
        ),
        in_specs=[SMEM] + [VMEM] * 5,
        out_specs=(VMEM, VMEM),
        compiler_params=pltpu.CompilerParams(vmem_limit_bytes=12 * 2**20),
        cost_estimate=pl.CostEstimate(
            flops=tokens * head_count * cols * experts * columns,
            bytes_accessed=head_count * cols * experts * columns,
            transcendentals=0,
        ),
        name="experts_second",
    )(me, mine, other, products, in_vmem(weights), in_vmem(w_down))


def down_blocks(units, w_ref, first, out_ref):
    cols = w_ref.shape[2]
    for t in range(w_ref.shape[0] // 2):
        out_ref[:, t * cols : (t + 1) * cols] = jnp.dot(
            units, w_ref[2 * t + first], preferred_element_type=jnp.float32
        ).astype(jnp.bfloat16)


def down_kernel(firsts, units_ref, w_ref, _, *outs):
    for first, out_ref in zip(firsts, outs):
        down_blocks(units_ref[...], w_ref, first, out_ref)


def down_part(units, w_down, firsts, after):
    head_count, total_units, cols = w_down.shape
    tokens = units.shape[0]
    half = jax.ShapeDtypeStruct((tokens, head_count // 2 * cols), jnp.bfloat16)
    return pl.pallas_call(
        functools.partial(down_kernel, firsts),
        out_shape=[half] * len(firsts),
        in_specs=[VMEM, VMEM, ANY],
        out_specs=[VMEM] * len(firsts),
        compiler_params=pltpu.CompilerParams(vmem_limit_bytes=12 * 2**20),
        cost_estimate=pl.CostEstimate(
            flops=len(firsts) * tokens * total_units * head_count * cols,
            bytes_accessed=len(firsts) * total_units * head_count * cols,
            transcendentals=0,
        ),
        name="down",
    )(units, in_vmem(w_down), after)


def hold_kernel(value_ref, after_ref, out_ref):
    pass


def hold(value, after):
    return pl.pallas_call(
        hold_kernel,
        out_shape=jax.ShapeDtypeStruct(value.shape, value.dtype),
        in_specs=[ANY, ANY],
        out_specs=ANY,
        input_output_aliases={0: 0},
        compiler_params=pltpu.CompilerParams(vmem_limit_bytes=2**20),
        name="hold",
    )(value, after)


def sum_kernel(keep_ref, sent_ref, *outs):
    cols = outs[0].shape[1]
    for t, out in enumerate(outs):
        part = slice(t * cols, (t + 1) * cols)
        total = keep_ref[:, part].astype(jnp.float32) + sent_ref[:, part].astype(jnp.float32)
        out[...] = total.astype(out.dtype)


def sum_part(keep, sent, cols, first_type):
    tokens, columns = keep.shape
    blocks = columns // cols
    return pl.pallas_call(
        sum_kernel,
        out_shape=[
            jax.ShapeDtypeStruct((tokens, cols), jnp.bfloat16 if t else first_type)
            for t in range(blocks)
        ],
        in_specs=[VMEM, VMEM],
        out_specs=[VMEM] * blocks,
        compiler_params=pltpu.CompilerParams(vmem_limit_bytes=8 * 2**20),
        name="sum",
    )(keep, sent)


def swap(value, axis, size, mask):
    return lax.ppermute(value, axis, [(i, i ^ mask) for i in range(size)])


def per_device(
    hidden, lengths, expert_ids, route_weights, w_qkv, w_out, k_cache, v_cache, w_in, w_down
):
    req_size = lax.axis_size("req")
    head_size = lax.axis_size("head")
    me = lax.axis_index("head")
    me_ref = me[None].astype(jnp.int32)
    rows, cols = hidden.shape
    experts_local, units_local, width = w_down.shape
    even = range(0, head_size, 2)

    pieces = [hidden] + [swap(hidden, "head", head_size, j) for j in range(1, head_size)]
    flat = (rows * k_cache.shape[1] * k_cache.shape[2], k_cache.shape[3])
    own, w_near, room, cosine, sine, lengths_near, shares = fetch(
        me_ref, lengths, hidden, w_qkv, flat, head_size, expert_ids, route_weights,
        head_size * experts_local,
    )
    pieces[0] = own
    keep, send, _, w_down_near = attention(
        pieces,
        me_ref,
        lengths_near,
        cosine,
        sine,
        w_near,
        room,
        w_out,
        k_cache.reshape(flat),
        v_cache.reshape(flat),
        w_down.reshape(experts_local * units_local, width),
    )
    (half,) = sum_part(keep, swap(send, "head", head_size, 1), keep.shape[1], jnp.bfloat16)
    others = [swap(half, "head", head_size, j) for j in even if j]
    early, late = range(head_size // 2), range(head_size // 2, head_size)
    buffer, token = by_expert(tuple(early), me_ref, w_in, head_size, None, half)

    payload, resid = payload_part(
        [pieces[j] for j in even], half, others, shares, token
    )

    steps = range(2, req_size, 2)
    line = [payload] + [swap(payload, "req", req_size, k) for k in steps]
    buffer, token = by_expert(tuple(late), me_ref, w_in, head_size, buffer, payload)
    line = stack_part(line, token)
    line_other = swap(line, "head", head_size, 1)
    crossed = swap(line, "req", req_size, 1)
    units = experts_whole(me_ref, line, line_other, buffer, token, w_down_near.shape[1])
    keep, send = down_part(units, w_down_near, (0, 1), token)
    line_sums = sum_part(keep, swap(send, "head", head_size, 1), cols, jnp.float32)
    crossed = hold(crossed, send)
    crossed_other = swap(crossed, "head", head_size, 1)
    products = experts_first(crossed, buffer, line_sums[-1])
    units, send = experts_second(me_ref, crossed, crossed_other, products, buffer, w_down_near)
    (keep,) = down_part(units, w_down_near, (0,), send)
    crossed_sums = sum_part(keep, swap(send, "head", head_size, 1), cols, jnp.bfloat16)
    total = line_sums[0]
    got = [swap(hold(line_sums[j // 2], keep), "head", head_size, j) for j in even if j]
    for j in even:
        pairs = [
            (r * head_size + h, (r ^ 1) * head_size + (h ^ j))
            for r in range(req_size)
            for h in range(head_size)
        ]
        got.append(lax.ppermute(crossed_sums[j // 2], ("req", "head"), pairs))
    for part in got:
        total = total + part.astype(jnp.float32)
    chunks = total.astype(jnp.bfloat16).reshape(req_size // 2, rows, cols)
    out = chunks[0].astype(jnp.float32)
    for k in steps:
        out = out + swap(chunks[k // 2], "req", req_size, k).astype(jnp.float32)
    return (out + resid).astype(jnp.bfloat16)


def solution(mesh):
    in_specs = (
        P("req", "head"),
        P("req"),
        P("req", None),
        P("req", None),
        P(None, None, "head"),
        P("head", None),
        P("req", None, "head", None),
        P("req", None, "head", None),
        P(None, "head", "req"),
        P("head", "req", None),
    )
    out_specs = P("req", "head")
    return jax.shard_map(
        per_device, mesh=mesh, in_specs=in_specs, out_specs=out_specs, check_vma=False
    )
```

```python
import functools
import itertools
import jax
import jax.numpy as jnp
from jax import lax
from jax.experimental import pallas as pl
from jax.experimental.pallas import tpu as pltpu
from jax.sharding import PartitionSpec as P

rope_theta = 50000.0
norm_eps = 1e-05
LANES = 128
SUBLANES = 8
CHUNK = 96
GROUP = 8
TOGETHER = 1
MASKED = -1e30


VMEM = pl.BlockSpec(memory_space=pltpu.VMEM)
SMEM = pl.BlockSpec(memory_space=pltpu.SMEM)
ANY = pl.BlockSpec(memory_space=pl.ANY)


def in_hbm(array):
    return pltpu.with_memory_space_constraint(array, pltpu.HBM)


def in_vmem(array):
    return pltpu.with_memory_space_constraint(array, pltpu.VMEM)


def used_rows(length, heads_local):
    return pl.multiple_of((length + 7) // 8 * (8 * heads_local), 8 * heads_local)


def fetch_kernel(
    lengths_hbm, me_ref, freqs_ref, own_ref, w_ref, ids_ref, route_ref,
    own_out_ref, w_out_ref, blank_ref, cos_ref, sin_ref, lengths_ref, shares_ref,
    angle_s, ids_s, route_s, sem, small_sem,
):
    head_count, cols = w_out_ref.shape[1:3]
    chunk_rows = CHUNK * cols // LANES
    me = me_ref[0]
    lengths_copy, *copies = [
        pltpu.make_async_copy(source, target, small_sem.at[i])
        for i, (source, target) in enumerate(
            (
                (lengths_hbm, lengths_ref),
                (ids_ref, ids_s),
                (route_ref, route_s),
                (own_ref, own_out_ref),
            )
        )
    ]
    small = copies[:2]
    for c in range(w_ref.shape[0]):
        for j in range(head_count):
            first = pl.multiple_of((me ^ j) * cols, cols)
            copies.append(
                pltpu.make_async_copy(
                    w_ref.at[c, pl.ds(first, cols)], w_out_ref.at[c, j], sem.at[c, j]
                )
            )
    lengths_copy.start()
    for copy in copies:
        copy.start()
    lengths_copy.wait()

    rows = angle_s.shape[0]
    cache_rows = blank_ref.shape[0] // rows

    @pl.loop(0, rows)
    def _(r):
        last = r * cache_rows + (lengths_ref[r] - 1) // CHUNK * chunk_rows
        blank_ref[pl.ds(pl.multiple_of(last, chunk_rows), chunk_rows)] = jnp.zeros(
            (chunk_rows, LANES), jnp.bfloat16
        )
        angle_s[pl.ds(r, 1), :] = lengths_ref[r].astype(jnp.float32) * freqs_ref[...]

    cos_ref[...] = jnp.cos(angle_s[...])
    lane = lax.broadcasted_iota(jnp.int32, sin_ref.shape, 1)
    sine = jnp.sin(angle_s[...])
    sin_ref[...] = jnp.where(lane < LANES // 2, -sine, sine)
    for copy in small:
        copy.wait()
    expert = lax.broadcasted_iota(jnp.int32, (shares_ref.shape[1], rows), 0)
    shares = jnp.zeros(expert.shape, jnp.float32)
    for k in range(ids_s.shape[0]):
        shares += jnp.where(expert == ids_s[k : k + 1, :], route_s[k : k + 1, :], 0.0)
    shares_ref[...] = jnp.transpose(shares, (1, 0)).astype(jnp.bfloat16)
    for copy in copies[2:]:
        copy.wait()


def fetch(me, lengths, hidden, w_qkv, v_shape, head_count, expert_ids, route_weights, experts):
    cols = w_qkv.shape[2]
    rows = hidden.shape[0]
    exponents = jnp.arange(LANES, dtype=jnp.float32) % (LANES // 2) / (LANES // 2)
    freqs = (rope_theta**-exponents)[None, :]
    return pl.pallas_call(
        fetch_kernel,
        out_shape=(
            pltpu.VMEM(hidden.shape, jnp.bfloat16),
            pltpu.VMEM((w_qkv.shape[0], head_count, cols, cols), jnp.bfloat16),
            pltpu.VMEM(v_shape, jnp.bfloat16),
            pltpu.VMEM((rows, LANES), jnp.float32),
            pltpu.VMEM((rows, LANES), jnp.float32),
            pltpu.SMEM(lengths.shape, lengths.dtype),
            pltpu.VMEM((rows, -(-experts // LANES) * LANES), jnp.bfloat16),
        ),
        in_specs=[ANY, SMEM, VMEM] + [ANY] * 4,
        out_specs=[VMEM] * 5 + [SMEM, VMEM],
        scratch_shapes=[
            pltpu.VMEM((rows, LANES), jnp.float32),
            pltpu.VMEM(expert_ids.shape[::-1], expert_ids.dtype),
            pltpu.VMEM(route_weights.shape[::-1], route_weights.dtype),
            pltpu.SemaphoreType.DMA((w_qkv.shape[0], head_count)),
            pltpu.SemaphoreType.DMA((4,)),
        ],
        compiler_params=pltpu.CompilerParams(vmem_limit_bytes=8 * 2**20),
        cost_estimate=pl.CostEstimate(
            flops=0, bytes_accessed=4 * w_qkv.size, transcendentals=0
        ),
        name="fetch",
    )(
        in_hbm(lengths), me, freqs, in_hbm(hidden), in_hbm(w_qkv), in_hbm(expert_ids.T),
        in_hbm(route_weights.T),
    )


def attention_kernel(head_count, lengths_ref, me_ref, cos_ref, sin_ref, *refs):
    pieces = refs[:head_count]
    (
        w_qkv_ref, _, w_out_ref, k_ref, v_ref, w_down_ref, keep_ref, send_ref, v_s, down_ref,
        w_out_s, k_s, query_s, key_s, value_s, attended_s, out_sem, k_sem, v_sem, down_sem,
    ) = refs[head_count:]
    rows, cols = pieces[0].shape
    heads_local = cols // LANES
    chunk_rows = CHUNK * heads_local
    me = me_ref[0]

    def out_copy(j):
        first = pl.multiple_of((me ^ j) * cols, cols)
        return pltpu.make_async_copy(
            w_out_ref.at[:, pl.ds(first, cols)], w_out_s.at[j], out_sem.at[j]
        )

    cache_rows = k_s.shape[0] // rows

    def cache_copy(source, target, sem, r, used):
        taken = pl.ds(pl.multiple_of(r * cache_rows, cache_rows), used)
        return pltpu.make_async_copy(
            source.at[taken], target.at[taken], sem.at[r // GROUP]
        )

    @pl.loop(0, rows, unroll=4)
    def _(r):
        used = used_rows(lengths_ref[r], heads_local)
        cache_copy(k_ref, k_s, k_sem, r, used).start()
        cache_copy(v_ref, v_s, v_sem, r, used).start()

    def down_copy(j):
        first = pl.multiple_of((me ^ j) * cols, cols)
        return pltpu.make_async_copy(
            w_down_ref.at[:, pl.ds(first, cols)], down_ref.at[j], down_sem.at[j]
        )

    for j in range(head_count):
        out_copy(j).start()
    for j in range(head_count):
        down_copy(j).start()

    if heads_local < SUBLANES:
        query_s[...] = jnp.zeros_like(query_s)
        key_s[...] = jnp.zeros_like(key_s)
        value_s[...] = jnp.zeros_like(value_s)
    states = jnp.concatenate([piece[...] for piece in pieces], axis=1)
    square = jnp.sum(jnp.square(states.astype(jnp.float32)), axis=1, keepdims=True)
    scale = lax.rsqrt(square / (cols * head_count) + norm_eps)
    cosine, sine = cos_ref[...], sin_ref[...]
    for c, target in enumerate((query_s, key_s, value_s)):
        projected = scale * jnp.dot(
            states,
            w_qkv_ref[c].reshape(head_count * cols, cols),
            preferred_element_type=jnp.float32,
        )
        for h in range(heads_local):
            part = projected[:, h * LANES : (h + 1) * LANES]
            if c < 2:
                part = part * cosine + pltpu.roll(part, LANES // 2, 1) * sine
            target[:, h, :] = part.astype(jnp.bfloat16).astype(jnp.float32)

    column = lax.broadcasted_iota(jnp.int32, (2 * SUBLANES, chunk_rows), 1)
    row = lax.broadcasted_iota(jnp.int32, (2 * SUBLANES, chunk_rows), 0)
    same_head = column % heads_local == row % SUBLANES
    upper = row < SUBLANES
    score_scale = LANES**-0.5
    blank = jnp.zeros((SUBLANES, LANES), jnp.float32)

    def diagonal(a, b):
        return jnp.concatenate(
            [jnp.concatenate([a, blank], axis=1), jnp.concatenate([blank, b], axis=1)], axis=0
        )

    @pl.loop(0, rows // (GROUP * TOGETHER))
    def _(step):
        requests = [step * GROUP * TOGETHER + i for i in range(GROUP * TOGETHER)]
        pairs = list(zip(requests[::2], requests[1::2]))
        lengths = [lengths_ref[r] for r in requests]
        spans = list(zip(lengths[::2], lengths[1::2]))
        queries = [diagonal(query_s[a], query_s[b]).astype(jnp.bfloat16) for a, b in pairs]
        own = [
            jnp.sum(query_s[r] * key_s[r], axis=1, keepdims=True) * score_scale for r in requests
        ]
        own = [jnp.concatenate([a, b], axis=0) for a, b in zip(own[::2], own[1::2])]
        values = [diagonal(value_s[a], value_s[b]) for a, b in pairs]
        needed = []
        for i in range(TOGETHER):
            part = lengths[i * GROUP : (i + 1) * GROUP]
            needed.append((functools.reduce(jnp.maximum, part) + CHUNK - 1) // CHUNK)
            used = used_rows(sum((length + 7) // 8 * 8 for length in part), heads_local)
            first = requests[i * GROUP]
            cache_copy(k_ref, k_s, k_sem, first, used).wait()
            cache_copy(v_ref, v_s, v_sem, first, used).wait()

        def with_chunks(counts):
            counts = [count for count in counts for _ in range(GROUP // 2)]

            def both(ref, c, pair, span):
                parts = []
                for r, length in zip(pair, span):
                    first = jnp.minimum(c, (length - 1) // CHUNK) * chunk_rows if c else 0
                    first = pl.multiple_of(r * cache_rows + first, chunk_rows)
                    parts.append(ref[pl.ds(first, chunk_rows)])
                return jnp.concatenate(parts, axis=1)

            scores = [
                [
                    lax.dot_general(
                        query,
                        both(k_s, c, pair, span),
                        (((1,), (1,)), ((), ())),
                        preferred_element_type=jnp.float32,
                    )
                    for c in range(count)
                ]
                for count, query, pair, span in zip(counts, queries, pairs, spans)
            ]
            limits = [
                jnp.where(upper, span[0] * heads_local, span[1] * heads_local) for span in spans
            ]
            scores = [
                [
                    jnp.where(
                        same_head & (column < limit - c * chunk_rows), score * score_scale, MASKED
                    )
                    for c, score in enumerate(parts)
                ]
                for limit, parts in zip(limits, scores)
            ]
            tops = [
                jnp.maximum(
                    mine, jnp.max(functools.reduce(jnp.maximum, parts), axis=1, keepdims=True)
                )
                for mine, parts in zip(own, scores)
            ]
            weights = [[jnp.exp(part - top) for part in parts] for top, parts in zip(tops, scores)]
            faded = [jnp.exp(mine - top) for mine, top in zip(own, tops)]
            totals = [
                fade + jnp.sum(functools.reduce(jnp.add, parts), axis=1, keepdims=True)
                for fade, parts in zip(faded, weights)
            ]
            sums = [
                fade * value
                + sum(
                    jnp.dot(
                        part.astype(jnp.bfloat16),
                        both(v_s, c, pair, span),
                        preferred_element_type=jnp.float32,
                    )
                    for c, part in enumerate(parts)
                )
                for pair, span, fade, value, parts in zip(pairs, spans, faded, values, weights)
            ]
            for (a, b), total, summed in zip(pairs, totals, sums):
                summed = summed / total
                attended_s[a] = summed[:SUBLANES, :LANES]
                attended_s[b] = summed[SUBLANES:, LANES:]

        most = cache_rows // chunk_rows
        for counts in itertools.product(range(1, most + 1), repeat=TOGETHER):
            chosen = functools.reduce(
                jnp.logical_and, [have == count for have, count in zip(needed, counts)]
            )
            pl.when(chosen)(functools.partial(with_chunks, counts))

    attended = jnp.concatenate(
        [attended_s[:, h, :] for h in range(heads_local)], axis=1
    ).astype(jnp.bfloat16)
    for j in range(head_count):
        out_copy(j).wait()
        target = send_ref if j % 2 else keep_ref
        target[:, j // 2 * cols : (j // 2 + 1) * cols] = jnp.dot(
            attended, w_out_s[j], preferred_element_type=jnp.float32
        ).astype(jnp.bfloat16)
    for j in range(head_count):
        down_copy(j).wait()


def attention(pieces, me, lengths, cosine, sine, w_qkv, room, w_out, k_cache, v_cache, w_down):
    head_count = len(pieces)
    rows, cols = pieces[0].shape
    half = jax.ShapeDtypeStruct((rows, head_count // 2 * cols), jnp.bfloat16)
    return pl.pallas_call(
        functools.partial(attention_kernel, head_count),
        out_shape=(
            half,
            half,
            pltpu.VMEM(room.shape, jnp.bfloat16),
            pltpu.VMEM((head_count, w_down.shape[0], cols), jnp.bfloat16),
        ),
        in_specs=[SMEM, SMEM] + [VMEM] * (head_count + 4) + [ANY] * 4,
        out_specs=(VMEM, VMEM, VMEM, VMEM),
        input_output_aliases={head_count + 5: 2},
        scratch_shapes=[
            pltpu.VMEM((head_count, cols, cols), jnp.bfloat16),
            pltpu.VMEM(k_cache.shape, jnp.bfloat16),
        ]
        + [pltpu.VMEM((rows, SUBLANES, LANES), jnp.float32)] * 4
        + [
            pltpu.SemaphoreType.DMA((head_count,)),
            pltpu.SemaphoreType.DMA((rows // GROUP,)),
            pltpu.SemaphoreType.DMA((rows // GROUP,)),
            pltpu.SemaphoreType.DMA((head_count,)),
        ],
        compiler_params=pltpu.CompilerParams(vmem_limit_bytes=20 * 2**20),
        cost_estimate=pl.CostEstimate(
            flops=2 * rows * 4 * cols * head_count * cols,
            bytes_accessed=2 * w_down.size + k_cache.size // 2,
            transcendentals=0,
        ),
        name="attention",
    )(
        pltpu.with_memory_space_constraint(lengths, pltpu.SMEM), me, in_vmem(cosine), in_vmem(sine), *map(in_vmem, pieces), in_vmem(w_qkv), in_vmem(room),
        in_hbm(w_out), in_hbm(k_cache), in_hbm(v_cache), in_hbm(w_down),
    )


RELAYOUT_ROWS = 128
RELAYOUT_STEP = 16

def slot_of(j, head_count):
    return j // 2 + j % 2 * (head_count // 2)


def relayout_kernel(js, me_ref, w_ref, *refs):
    out_ref, token_ref, in_s, in_sem = refs[-4:]
    token_ref[...] = jnp.zeros_like(token_ref)
    experts, head_count, cols, _ = out_ref.shape
    step = in_s.shape[1]
    per_block = cols // step
    copies = []
    for at, j in enumerate(js):
        base = (me_ref[0] ^ j) * cols
        for i in range(per_block):
            slot = at * per_block + i
            first = pl.multiple_of(base + i * step, step)
            copies.append(
                pltpu.make_async_copy(
                    w_ref.at[pl.ds(first, step)], in_s.at[slot], in_sem.at[slot]
                )
            )
    for copy in copies:
        copy.start()
    for slot, copy in enumerate(copies):
        j, i = js[slot // per_block], slot % per_block
        copy.wait()
        for s in range(step // RELAYOUT_STEP):
            part = in_s[slot, pl.ds(s * RELAYOUT_STEP, RELAYOUT_STEP)]
            out_ref[:, slot_of(j, head_count), pl.ds(i * step + s * RELAYOUT_STEP, RELAYOUT_STEP), :] = jnp.swapaxes(
                part, 0, 1
            )


def by_expert(js, me, w_in, head_count, buffer, after):
    width, experts, columns = w_in.shape
    cols = width // head_count
    step = min(RELAYOUT_ROWS, cols)
    slots = len(js) * cols // step
    held = [] if buffer is None else [in_vmem(buffer)]
    return pl.pallas_call(
        functools.partial(relayout_kernel, js),
        out_shape=(
            pltpu.VMEM((experts, head_count, cols, columns), jnp.bfloat16),
            jax.ShapeDtypeStruct((SUBLANES, LANES), jnp.float32),
        ),
        in_specs=[SMEM, ANY] + [VMEM] * len(held) + [ANY],
        out_specs=(VMEM, VMEM),
        input_output_aliases={2: 0} if held else {},
        scratch_shapes=[
            pltpu.VMEM((slots, step, experts, columns), jnp.bfloat16),
            pltpu.SemaphoreType.DMA((slots,)),
        ],
        compiler_params=pltpu.CompilerParams(vmem_limit_bytes=16 * 2**20),
        cost_estimate=pl.CostEstimate(
            flops=0, bytes_accessed=4 * len(js) * cols * experts * columns, transcendentals=0
        ),
        name=f"by_expert_{js[0]}",
    )(me, in_hbm(w_in), *held, after)


def payload_kernel(head_count, *refs):
    blocks = head_count // 2
    pieces, (half_ref, *others), shares_ref = refs[:blocks], refs[blocks : 2 * blocks], refs[2 * blocks]
    payload_ref, resid_ref = refs[-2:]
    cols = pieces[0].shape[1]
    for t in range(blocks):
        total = pieces[t][...].astype(jnp.float32)
        for at, source in enumerate((half_ref, *others)):
            place = (t ^ at) * cols
            total += source[:, place : place + cols].astype(jnp.float32)
        payload_ref[:, t * cols : (t + 1) * cols] = total.astype(jnp.bfloat16)
        if t == 0:
            resid_ref[...] = total
    payload_ref[:, blocks * cols :] = shares_ref[...]


def payload_part(pieces, half, others, shares, after):
    blocks = len(pieces)
    rows, cols = pieces[0].shape
    return pl.pallas_call(
        functools.partial(payload_kernel, 2 * blocks),
        out_shape=(
            jax.ShapeDtypeStruct((rows, blocks * cols + shares.shape[1]), jnp.bfloat16),
            jax.ShapeDtypeStruct((rows, cols), jnp.float32),
        ),
        in_specs=[VMEM] * (2 * blocks + 1) + [ANY],
        out_specs=(VMEM, VMEM),
        compiler_params=pltpu.CompilerParams(vmem_limit_bytes=8 * 2**20),
        name="payload",
    )(*pieces, half, *others, shares, after)


def stack_kernel(count, *refs):
    all_ref, states_ref = refs[-2:]
    rows = refs[0].shape[0]
    for i in range(count):
        part = slice(i * rows, (i + 1) * rows)
        all_ref[part, :] = refs[i][...]
        states_ref[part, :] = refs[i][:, : states_ref.shape[1]]


def stack_part(parts, width, after):
    rows, columns = parts[0].shape
    return pl.pallas_call(
        functools.partial(stack_kernel, len(parts)),
        out_shape=[
            jax.ShapeDtypeStruct((len(parts) * rows, n), jnp.bfloat16) for n in (columns, width)
        ],
        in_specs=[VMEM] * len(parts) + [ANY],
        out_specs=[VMEM] * 2,
        compiler_params=pltpu.CompilerParams(vmem_limit_bytes=8 * 2**20),
        name="stack",
    )(*parts, after)


def expert_products(states, w_ref, first, p, per_step):
    columns = w_ref.shape[3]
    depth = states.shape[1]
    taken = pl.ds(first, depth // w_ref.shape[2])
    products = [
        jnp.dot(
            states,
            w_ref[p * per_step + i, taken].reshape(depth, columns),
            preferred_element_type=jnp.float32,
        )
        for i in range(per_step)
    ]
    return products[0] if per_step == 1 else jnp.concatenate(products, axis=1)


def steps_of(w_shape):
    per_step = max(1, 2 * LANES // w_shape[3])
    return w_shape[0] // per_step, per_step


def square_sum(ref, depth):
    return jnp.sum(jnp.square(ref[:, :depth].astype(jnp.float32)), axis=1, keepdims=True)


def local_shares(me, shares, experts):
    lanes = shares.shape[1]
    return pltpu.roll(shares.astype(jnp.float32), lax.rem(lanes - me * experts, lanes), 1)


def units_step(p, per_step, product, scale, shares):
    tokens = product.shape[0]
    first_half = lax.broadcasted_iota(jnp.int32, (tokens, LANES), 1) < LANES // 2
    expert = p * per_step
    share = shares[:, expert : expert + 1]
    if per_step == 2:
        share = jnp.where(first_half, share, shares[:, expert + 1 : expert + 2])
    a, b = product[:, :LANES], product[:, LANES:]
    gate = jnp.where(first_half, a, pltpu.roll(b, LANES // 2, 1)) * scale
    upward = jnp.where(first_half, pltpu.roll(a, LANES // 2, 1), b) * (scale * 0.5)
    return (share * (gate * (1.0 + jnp.tanh(gate * 0.5)) * upward)).astype(jnp.bfloat16)


def whole_kernel(me_ref, mine_ref, other_ref, w_ref, _, units_ref, states_s):
    experts, head_count, cols, _ = w_ref.shape
    depth = head_count // 2 * cols
    states_s[:, :depth] = mine_ref[:, :depth]
    states_s[:, depth:] = other_ref[:, :depth]
    square = square_sum(mine_ref, depth) + square_sum(other_ref, depth)
    scale = lax.rsqrt(square / (2 * depth) + norm_eps)
    shares = local_shares(me_ref[0], mine_ref[:, depth:], experts)
    steps, per_step = steps_of(w_ref.shape)
    for p in range(steps):
        product = expert_products(states_s[...], w_ref, 0, p, per_step)
        units_ref[:, p * LANES : (p + 1) * LANES] = units_step(
            p, per_step, product, scale, shares
        )


def first_kernel(mine_ref, w_ref, _, product_ref):
    _, head_count, cols, _ = w_ref.shape
    steps, per_step = steps_of(w_ref.shape)
    for p in range(steps):
        states = mine_ref[:, : head_count // 2 * cols]
        product_ref[p] = expert_products(states, w_ref, 0, p, per_step)


def second_kernel(me_ref, mine_ref, other_ref, product_ref, w_ref, w_down_ref, units_ref, send_ref):
    experts, head_count, cols, _ = w_ref.shape
    depth = head_count // 2 * cols
    square = square_sum(mine_ref, depth) + square_sum(other_ref, depth)
    scale = lax.rsqrt(square / (2 * depth) + norm_eps)
    shares = local_shares(me_ref[0], mine_ref[:, depth:], experts)
    steps, per_step = steps_of(w_ref.shape)
    for p in range(steps):
        product = product_ref[p] + expert_products(
            other_ref[:, :depth], w_ref, head_count // 2, p, per_step
        )
        units_ref[:, p * LANES : (p + 1) * LANES] = units_step(
            p, per_step, product, scale, shares
        )

    down_blocks(units_ref[...], w_down_ref, 1, send_ref)


def experts_whole(me, mine, other, weights, after, total_units):
    experts, head_count, cols, columns = weights.shape
    tokens = mine.shape[0]
    return pl.pallas_call(
        whole_kernel,
        out_shape=jax.ShapeDtypeStruct((tokens, total_units), jnp.bfloat16),
        in_specs=[SMEM] + [VMEM] * 3 + [ANY],
        out_specs=VMEM,
        scratch_shapes=[pltpu.VMEM((tokens, head_count * cols), jnp.bfloat16)],
        compiler_params=pltpu.CompilerParams(vmem_limit_bytes=12 * 2**20),
        cost_estimate=pl.CostEstimate(flops=0, bytes_accessed=0, transcendentals=0),
        name="experts_whole",
    )(me, mine, other, in_vmem(weights), after)


def experts_first(mine, weights, after):
    experts, head_count, cols, columns = weights.shape
    tokens = mine.shape[0]
    steps, per_step = steps_of(weights.shape)
    return pl.pallas_call(
        first_kernel,
        out_shape=jax.ShapeDtypeStruct((steps, tokens, per_step * columns), jnp.float32),
        in_specs=[VMEM] * 2 + [ANY],
        out_specs=VMEM,
        compiler_params=pltpu.CompilerParams(vmem_limit_bytes=12 * 2**20),
        cost_estimate=pl.CostEstimate(
            flops=tokens * head_count * cols * experts * columns,
            bytes_accessed=head_count * cols * experts * columns,
            transcendentals=0,
        ),
        name="experts_first",
    )(mine, in_vmem(weights), after)


def experts_second(me, mine, other, products, weights, w_down):
    experts, head_count, cols, columns = weights.shape
    tokens = mine.shape[0]
    return pl.pallas_call(
        second_kernel,
        out_shape=(
            jax.ShapeDtypeStruct((tokens, w_down.shape[1]), jnp.bfloat16),
            jax.ShapeDtypeStruct((tokens, head_count // 2 * cols), jnp.bfloat16),
        ),
        in_specs=[SMEM] + [VMEM] * 5,
        out_specs=(VMEM, VMEM),
        compiler_params=pltpu.CompilerParams(vmem_limit_bytes=12 * 2**20),
        cost_estimate=pl.CostEstimate(
            flops=tokens * head_count * cols * experts * columns,
            bytes_accessed=head_count * cols * experts * columns,
            transcendentals=0,
        ),
        name="experts_second",
    )(me, mine, other, products, in_vmem(weights), in_vmem(w_down))


def down_blocks(units, w_ref, first, out_ref):
    cols = w_ref.shape[2]
    for t in range(w_ref.shape[0] // 2):
        out_ref[:, t * cols : (t + 1) * cols] = jnp.dot(
            units, w_ref[2 * t + first], preferred_element_type=jnp.float32
        ).astype(jnp.bfloat16)


def down_kernel(firsts, units_ref, w_ref, _, *outs):
    for first, out_ref in zip(firsts, outs):
        down_blocks(units_ref[...], w_ref, first, out_ref)


def down_part(units, w_down, firsts, after):
    head_count, total_units, cols = w_down.shape
    tokens = units.shape[0]
    half = jax.ShapeDtypeStruct((tokens, head_count // 2 * cols), jnp.bfloat16)
    return pl.pallas_call(
        functools.partial(down_kernel, firsts),
        out_shape=[half] * len(firsts),
        in_specs=[VMEM, VMEM, ANY],
        out_specs=[VMEM] * len(firsts),
        compiler_params=pltpu.CompilerParams(vmem_limit_bytes=12 * 2**20),
        cost_estimate=pl.CostEstimate(flops=0, bytes_accessed=0, transcendentals=0),
        name="down",
    )(units, in_vmem(w_down), after)


def hold_kernel(value_ref, after_ref, out_ref):
    pass


def hold(value, after):
    return pl.pallas_call(
        hold_kernel,
        out_shape=jax.ShapeDtypeStruct(value.shape, value.dtype),
        in_specs=[ANY, ANY],
        out_specs=ANY,
        input_output_aliases={0: 0},
        compiler_params=pltpu.CompilerParams(vmem_limit_bytes=2**20),
        name="hold",
    )(value, after)


def sum_kernel(keep_ref, sent_ref, *outs):
    *outs, token_ref = outs
    token_ref[...] = jnp.zeros_like(token_ref)
    cols = outs[0].shape[1]
    for t, out in enumerate(outs):
        part = slice(t * cols, (t + 1) * cols)
        total = keep_ref[:, part].astype(jnp.float32) + sent_ref[:, part].astype(jnp.float32)
        out[...] = total.astype(out.dtype)


def sum_part(keep, sent, cols, first_type):
    tokens, columns = keep.shape
    blocks = columns // cols
    return pl.pallas_call(
        sum_kernel,
        out_shape=[
            jax.ShapeDtypeStruct((tokens, cols), jnp.bfloat16 if t else first_type)
            for t in range(blocks)
        ]
        + [jax.ShapeDtypeStruct((SUBLANES, LANES), jnp.float32)],
        in_specs=[VMEM, VMEM],
        out_specs=[VMEM] * (blocks + 1),
        compiler_params=pltpu.CompilerParams(vmem_limit_bytes=8 * 2**20),
        name="sum",
    )(keep, sent)


def swap(value, axis, size, mask):
    return lax.ppermute(value, axis, [(i, i ^ mask) for i in range(size)])


def per_device(
    hidden, lengths, expert_ids, route_weights, w_qkv, w_out, k_cache, v_cache, w_in, w_down
):
    req_size = lax.axis_size("req")
    head_size = lax.axis_size("head")
    me = lax.axis_index("head")
    me_ref = me[None].astype(jnp.int32)
    rows, cols = hidden.shape
    experts_local, units_local, width = w_down.shape
    even = range(0, head_size, 2)

    pieces = [hidden] + [swap(hidden, "head", head_size, j) for j in range(1, head_size)]
    flat = (rows * k_cache.shape[1] * k_cache.shape[2], k_cache.shape[3])
    own, w_near, room, cosine, sine, lengths_near, shares = fetch(
        me_ref, lengths, hidden, w_qkv, flat, head_size, expert_ids, route_weights,
        head_size * experts_local,
    )
    pieces[0] = own
    keep, send, _, w_down_near = attention(
        pieces,
        me_ref,
        lengths_near,
        cosine,
        sine,
        w_near,
        room,
        w_out,
        k_cache.reshape(flat),
        v_cache.reshape(flat),
        w_down.reshape(experts_local * units_local, width),
    )
    half, _ = sum_part(keep, swap(send, "head", head_size, 1), keep.shape[1], jnp.bfloat16)
    others = [swap(half, "head", head_size, j) for j in even if j]
    early, late = range(head_size // 2), range(head_size // 2, head_size)
    buffer, token = by_expert(tuple(early), me_ref, w_in, head_size, None, half)

    payload, resid = payload_part(
        [pieces[j] for j in even], half, others, shares, token
    )

    steps = range(2, req_size, 2)
    line = [payload] + [swap(payload, "req", req_size, k) for k in steps]
    buffer, token = by_expert(tuple(late), me_ref, w_in, head_size, buffer, payload)
    line, line_states = stack_part(line, head_size // 2 * cols, token)
    line_other = swap(line_states, "head", head_size, 1)
    crossed = swap(line, "req", req_size, 1)
    units = experts_whole(me_ref, line, line_other, buffer, token, w_down_near.shape[1])
    keep, send = down_part(units, w_down_near, (0, 1), token)
    *line_sums, token = sum_part(keep, swap(send, "head", head_size, 1), cols, jnp.float32)
    crossed = hold(crossed, send)
    crossed_other = swap(crossed, "head", head_size, 1)
    products = experts_first(crossed, buffer, token)
    units, send = experts_second(me_ref, crossed, crossed_other, products, buffer, w_down_near)
    (keep,) = down_part(units, w_down_near, (0,), send)
    *crossed_sums, token = sum_part(keep, swap(send, "head", head_size, 1), cols, jnp.bfloat16)
    total = line_sums[0]
    got = []
    for j in even:
        pairs = [
            (r * head_size + h, (r ^ 1) * head_size + (h ^ j))
            for r in range(req_size)
            for h in range(head_size)
        ]
        got.append(lax.ppermute(hold(crossed_sums[j // 2], token), ("req", "head"), pairs))
    got += [
        swap(hold(line_sums[j // 2], token), "head", head_size, j) for j in even if j
    ]
    for part in got:
        total = total + part.astype(jnp.float32)
    chunks = total.astype(jnp.bfloat16).reshape(req_size // 2, rows, cols)
    out = chunks[0].astype(jnp.float32)
    for k in steps:
        out = out + swap(chunks[k // 2], "req", req_size, k).astype(jnp.float32)
    return (out + resid).astype(jnp.bfloat16)


def solution(mesh):
    in_specs = (
        P("req", "head"),
        P("req"),
        P("req", None),
        P("req", None),
        P(None, None, "head"),
        P("head", None),
        P("req", None, "head", None),
        P("req", None, "head", None),
        P(None, "head", "req"),
        P("head", "req", None),
    )
    out_specs = P("req", "head")
    return jax.shard_map(
        per_device, mesh=mesh, in_specs=in_specs, out_specs=out_specs, check_vma=False
    )
```

```python
import functools
import itertools
import jax
import jax.numpy as jnp
from jax import lax
from jax.experimental import pallas as pl
from jax.experimental.pallas import tpu as pltpu
from jax.sharding import PartitionSpec as P

rope_theta = 50000.0
norm_eps = 1e-05
LANES = 128
SUBLANES = 8
CHUNK = 128
GROUP = 8
MASKED = -1e30


VMEM = pl.BlockSpec(memory_space=pltpu.VMEM)
SMEM = pl.BlockSpec(memory_space=pltpu.SMEM)
ANY = pl.BlockSpec(memory_space=pl.ANY)


def in_hbm(array):
    return pltpu.with_memory_space_constraint(array, pltpu.HBM)


def in_vmem(array):
    return pltpu.with_memory_space_constraint(array, pltpu.VMEM)


def used_rows(length, heads_local):
    return pl.multiple_of((length + 7) // 8 * (8 * heads_local), 8 * heads_local)


def exchanges(count):
    steps = []
    size = 1
    while size < count:
        gap = size
        while gap >= 1:
            for start in range(gap % size, count - gap, 2 * gap):
                for i in range(min(gap, count - start - gap)):
                    if (start + i) // (2 * size) == (start + i + gap) // (2 * size):
                        steps.append((start + i, start + i + gap))
            gap //= 2
        size *= 2
    return steps


def packed(length, request):
    return (length << 16) + request


def unpacked(key):
    return key >> 16, key & 0xFFFF


def fetch_kernel(
    lengths_hbm, me_ref, freqs_ref, own_ref, w_ref, ids_ref, route_ref,
    own_out_ref, w_out_ref, blank_ref, cos_ref, sin_ref, keys_ref, shares_ref,
    lengths_ref, angle_s, ids_s, route_s, sem, small_sem,
):
    head_count, cols = w_out_ref.shape[1:3]
    chunk_rows = CHUNK * cols // LANES
    me = me_ref[0]
    lengths_copy, *copies = [
        pltpu.make_async_copy(source, target, small_sem.at[i])
        for i, (source, target) in enumerate(
            (
                (lengths_hbm, lengths_ref),
                (ids_ref, ids_s),
                (route_ref, route_s),
                (own_ref, own_out_ref),
            )
        )
    ]
    small = copies[:2]
    for c in range(w_ref.shape[0]):
        for j in range(head_count):
            first = pl.multiple_of((me ^ j) * cols, cols)
            copies.append(
                pltpu.make_async_copy(
                    w_ref.at[c, pl.ds(first, cols)], w_out_ref.at[c, j], sem.at[c, j]
                )
            )
    lengths_copy.start()
    for copy in copies:
        copy.start()
    lengths_copy.wait()

    rows = angle_s.shape[0]
    cache_rows = blank_ref.shape[0] // rows

    @pl.loop(0, rows)
    def _(r):
        last = r * cache_rows + (lengths_ref[r] - 1) // CHUNK * chunk_rows
        blank_ref[pl.ds(pl.multiple_of(last, chunk_rows), chunk_rows)] = jnp.zeros(
            (chunk_rows, LANES), jnp.bfloat16
        )
        angle_s[pl.ds(r, 1), :] = lengths_ref[r].astype(jnp.float32) * freqs_ref[...]

    cos_ref[...] = jnp.cos(angle_s[...])
    lane = lax.broadcasted_iota(jnp.int32, sin_ref.shape, 1)
    sine = jnp.sin(angle_s[...])
    sin_ref[...] = jnp.where(lane < LANES // 2, -sine, sine)
    @pl.loop(0, rows // GROUP)
    def _(g):
        keys = [packed(lengths_ref[g * GROUP + i], g * GROUP + i) for i in range(GROUP)]
        for low, high in exchanges(GROUP):
            larger, smaller = jnp.maximum(keys[low], keys[high]), jnp.minimum(keys[low], keys[high])
            keys[low], keys[high] = larger, smaller
        for i in range(GROUP):
            keys_ref[g * GROUP + i] = keys[i]

    for copy in small:
        copy.wait()
    expert = lax.broadcasted_iota(jnp.int32, (shares_ref.shape[1], rows), 0)
    shares = jnp.zeros(expert.shape, jnp.float32)
    for k in range(ids_s.shape[0]):
        shares += jnp.where(expert == ids_s[k : k + 1, :], route_s[k : k + 1, :], 0.0)
    shares_ref[...] = jnp.transpose(shares, (1, 0)).astype(jnp.bfloat16)
    for copy in copies[2:]:
        copy.wait()


def fetch(me, lengths, hidden, w_qkv, v_shape, head_count, expert_ids, route_weights, experts):
    cols = w_qkv.shape[2]
    rows = hidden.shape[0]
    exponents = jnp.arange(LANES, dtype=jnp.float32) % (LANES // 2) / (LANES // 2)
    freqs = (rope_theta**-exponents)[None, :]
    return pl.pallas_call(
        fetch_kernel,
        out_shape=(
            pltpu.VMEM(hidden.shape, jnp.bfloat16),
            pltpu.VMEM((w_qkv.shape[0], head_count, cols, cols), jnp.bfloat16),
            pltpu.VMEM(v_shape, jnp.bfloat16),
            pltpu.VMEM((rows, LANES), jnp.float32),
            pltpu.VMEM((rows, LANES), jnp.float32),
            pltpu.SMEM(lengths.shape, lengths.dtype),
            pltpu.VMEM((rows, -(-experts // LANES) * LANES), jnp.bfloat16),
        ),
        in_specs=[ANY, SMEM, VMEM] + [ANY] * 4,
        out_specs=[VMEM] * 5 + [SMEM, VMEM],
        scratch_shapes=[
            pltpu.SMEM(lengths.shape, lengths.dtype),
            pltpu.VMEM((rows, LANES), jnp.float32),
            pltpu.VMEM(expert_ids.shape[::-1], expert_ids.dtype),
            pltpu.VMEM(route_weights.shape[::-1], route_weights.dtype),
            pltpu.SemaphoreType.DMA((w_qkv.shape[0], head_count)),
            pltpu.SemaphoreType.DMA((4,)),
        ],
        compiler_params=pltpu.CompilerParams(vmem_limit_bytes=8 * 2**20),
        cost_estimate=pl.CostEstimate(
            flops=0, bytes_accessed=4 * w_qkv.size, transcendentals=0
        ),
        name="fetch",
    )(
        in_hbm(lengths), me, freqs, in_hbm(hidden), in_hbm(w_qkv), in_hbm(expert_ids.T),
        in_hbm(route_weights.T),
    )


def attention_kernel(head_count, keys_ref, me_ref, cos_ref, sin_ref, *refs):
    pieces = refs[:head_count]
    (
        w_qkv_ref, _, w_out_ref, k_ref, v_ref, w_down_ref, keep_ref, send_ref, v_s, down_ref,
        w_out_s, k_s, query_s, key_s, value_s, attended_s, out_sem, k_sem, v_sem, down_sem,
    ) = refs[head_count:]
    rows, cols = pieces[0].shape
    heads_local = cols // LANES
    chunk_rows = CHUNK * heads_local
    me = me_ref[0]

    def out_copy(j):
        first = pl.multiple_of((me ^ j) * cols, cols)
        return pltpu.make_async_copy(
            w_out_ref.at[:, pl.ds(first, cols)], w_out_s.at[j], out_sem.at[j]
        )

    cache_rows = k_s.shape[0] // rows

    def cache_copy(source, target, sem, r, used):
        taken = pl.ds(pl.multiple_of(r * cache_rows, cache_rows), used)
        return pltpu.make_async_copy(
            source.at[taken], target.at[taken], sem.at[r // GROUP]
        )

    @pl.loop(0, rows, unroll=4)
    def _(i):
        length, r = unpacked(keys_ref[i])
        used = used_rows(length, heads_local)
        cache_copy(k_ref, k_s, k_sem, r, used).start()
        cache_copy(v_ref, v_s, v_sem, r, used).start()

    def down_copy(j):
        first = pl.multiple_of((me ^ j) * cols, cols)
        return pltpu.make_async_copy(
            w_down_ref.at[:, pl.ds(first, cols)], down_ref.at[j], down_sem.at[j]
        )

    for j in range(head_count):
        out_copy(j).start()
    for j in range(head_count):
        down_copy(j).start()

    if heads_local < SUBLANES:
        query_s[...] = jnp.zeros_like(query_s)
        key_s[...] = jnp.zeros_like(key_s)
        value_s[...] = jnp.zeros_like(value_s)
    states = jnp.concatenate([piece[...] for piece in pieces], axis=1)
    square = jnp.sum(jnp.square(states.astype(jnp.float32)), axis=1, keepdims=True)
    scale = lax.rsqrt(square / (cols * head_count) + norm_eps)
    cosine, sine = cos_ref[...], sin_ref[...]
    for c, target in enumerate((query_s, key_s, value_s)):
        projected = scale * jnp.dot(
            states,
            w_qkv_ref[c].reshape(head_count * cols, cols),
            preferred_element_type=jnp.float32,
        )
        for h in range(heads_local):
            part = projected[:, h * LANES : (h + 1) * LANES]
            if c < 2:
                part = part * cosine + pltpu.roll(part, LANES // 2, 1) * sine
            target[:, h, :] = part.astype(jnp.bfloat16).astype(jnp.float32)

    column = lax.broadcasted_iota(jnp.int32, (2 * SUBLANES, chunk_rows), 1)
    row = lax.broadcasted_iota(jnp.int32, (2 * SUBLANES, chunk_rows), 0)
    same_head = column % heads_local == row % SUBLANES
    upper = row < SUBLANES
    score_scale = LANES**-0.5
    blank = jnp.zeros((SUBLANES, LANES), jnp.float32)

    def diagonal(a, b):
        return jnp.concatenate(
            [jnp.concatenate([a, blank], axis=1), jnp.concatenate([blank, b], axis=1)], axis=0
        )

    @pl.loop(0, rows // GROUP)
    def _(g):
        lengths, requests = zip(*[unpacked(keys_ref[g * GROUP + i]) for i in range(GROUP)])
        pairs = list(zip(requests[::2], requests[1::2]))
        spans = list(zip(lengths[::2], lengths[1::2]))
        queries = [diagonal(query_s[a], query_s[b]).astype(jnp.bfloat16) for a, b in pairs]
        own = [
            jnp.sum(query_s[r] * key_s[r], axis=1, keepdims=True) * score_scale for r in requests
        ]
        own = [jnp.concatenate([a, b], axis=0) for a, b in zip(own[::2], own[1::2])]
        values = [diagonal(value_s[a], value_s[b]) for a, b in pairs]
        used = used_rows(sum((length + 7) // 8 * 8 for length in lengths), heads_local)
        cache_copy(k_ref, k_s, k_sem, g * GROUP, used).wait()
        cache_copy(v_ref, v_s, v_sem, g * GROUP, used).wait()
        needed = [(lengths[i] + CHUNK - 1) // CHUNK for i in (0, GROUP // 2)]

        def with_chunks(counts):
            counts = [count for count in counts for _ in range(GROUP // 4)]

            def both(ref, c, pair, span):
                parts = []
                for r, length in zip(pair, span):
                    first = jnp.minimum(c, (length - 1) // CHUNK) * chunk_rows if c else 0
                    first = pl.multiple_of(r * cache_rows + first, chunk_rows)
                    parts.append(ref[pl.ds(first, chunk_rows)])
                return jnp.concatenate(parts, axis=1)

            scores = [
                [
                    lax.dot_general(
                        query,
                        both(k_s, c, pair, span),
                        (((1,), (1,)), ((), ())),
                        preferred_element_type=jnp.float32,
                    )
                    for c in range(count)
                ]
                for count, query, pair, span in zip(counts, queries, pairs, spans)
            ]
            limits = [
                jnp.where(upper, span[0] * heads_local, span[1] * heads_local) for span in spans
            ]
            scores = [
                [
                    jnp.where(
                        same_head & (column < limit - c * chunk_rows), score * score_scale, MASKED
                    )
                    for c, score in enumerate(parts)
                ]
                for limit, parts in zip(limits, scores)
            ]
            tops = [
                jnp.maximum(
                    mine, jnp.max(functools.reduce(jnp.maximum, parts), axis=1, keepdims=True)
                )
                for mine, parts in zip(own, scores)
            ]
            weights = [[jnp.exp(part - top) for part in parts] for top, parts in zip(tops, scores)]
            faded = [jnp.exp(mine - top) for mine, top in zip(own, tops)]
            totals = [
                fade + jnp.sum(functools.reduce(jnp.add, parts), axis=1, keepdims=True)
                for fade, parts in zip(faded, weights)
            ]
            sums = [
                fade * value
                + sum(
                    jnp.dot(
                        part.astype(jnp.bfloat16),
                        both(v_s, c, pair, span),
                        preferred_element_type=jnp.float32,
                    )
                    for c, part in enumerate(parts)
                )
                for pair, span, fade, value, parts in zip(pairs, spans, faded, values, weights)
            ]
            for (a, b), total, summed in zip(pairs, totals, sums):
                summed = summed / total
                attended_s[a] = summed[:SUBLANES, :LANES]
                attended_s[b] = summed[SUBLANES:, LANES:]

        most = cache_rows // chunk_rows
        for longer, shorter in itertools.product(range(1, most + 1), repeat=2):
            if longer >= shorter:
                pl.when((needed[0] == longer) & (needed[1] == shorter))(
                    functools.partial(with_chunks, (longer, shorter))
                )

    attended = jnp.concatenate(
        [attended_s[:, h, :] for h in range(heads_local)], axis=1
    ).astype(jnp.bfloat16)
    for j in range(head_count):
        out_copy(j).wait()
        target = send_ref if j % 2 else keep_ref
        target[:, j // 2 * cols : (j // 2 + 1) * cols] = jnp.dot(
            attended, w_out_s[j], preferred_element_type=jnp.float32
        ).astype(jnp.bfloat16)
    for j in range(head_count):
        down_copy(j).wait()


def attention(pieces, me, keys, cosine, sine, w_qkv, room, w_out, k_cache, v_cache, w_down):
    head_count = len(pieces)
    rows, cols = pieces[0].shape
    half = jax.ShapeDtypeStruct((rows, head_count // 2 * cols), jnp.bfloat16)
    return pl.pallas_call(
        functools.partial(attention_kernel, head_count),
        out_shape=(
            half,
            half,
            pltpu.VMEM(room.shape, jnp.bfloat16),
            pltpu.VMEM((head_count, w_down.shape[0], cols), jnp.bfloat16),
        ),
        in_specs=[SMEM, SMEM] + [VMEM] * (head_count + 4) + [ANY] * 4,
        out_specs=(VMEM, VMEM, VMEM, VMEM),
        input_output_aliases={head_count + 5: 2},
        scratch_shapes=[
            pltpu.VMEM((head_count, cols, cols), jnp.bfloat16),
            pltpu.VMEM(k_cache.shape, jnp.bfloat16),
        ]
        + [pltpu.VMEM((rows, SUBLANES, LANES), jnp.float32)] * 4
        + [
            pltpu.SemaphoreType.DMA((head_count,)),
            pltpu.SemaphoreType.DMA((rows // GROUP,)),
            pltpu.SemaphoreType.DMA((rows // GROUP,)),
            pltpu.SemaphoreType.DMA((head_count,)),
        ],
        compiler_params=pltpu.CompilerParams(vmem_limit_bytes=20 * 2**20),
        cost_estimate=pl.CostEstimate(
            flops=2 * rows * 4 * cols * head_count * cols,
            bytes_accessed=2 * w_down.size + k_cache.size // 2,
            transcendentals=0,
        ),
        name="attention",
    )(
        pltpu.with_memory_space_constraint(keys, pltpu.SMEM), me, in_vmem(cosine), in_vmem(sine), *map(in_vmem, pieces), in_vmem(w_qkv), in_vmem(room),
        in_hbm(w_out), in_hbm(k_cache), in_hbm(v_cache), in_hbm(w_down),
    )


RELAYOUT_ROWS = 128
RELAYOUT_STEP = 16

def slot_of(j, head_count):
    return j // 2 + j % 2 * (head_count // 2)


def relayout_kernel(js, me_ref, w_ref, *refs):
    out_ref, token_ref, in_s, in_sem = refs[-4:]
    token_ref[...] = jnp.zeros_like(token_ref)
    experts, head_count, cols, _ = out_ref.shape
    step = in_s.shape[1]
    per_block = cols // step
    copies = []
    for at, j in enumerate(js):
        base = (me_ref[0] ^ j) * cols
        for i in range(per_block):
            slot = at * per_block + i
            first = pl.multiple_of(base + i * step, step)
            copies.append(
                pltpu.make_async_copy(
                    w_ref.at[pl.ds(first, step)], in_s.at[slot], in_sem.at[slot]
                )
            )
    for copy in copies:
        copy.start()
    for slot, copy in enumerate(copies):
        j, i = js[slot // per_block], slot % per_block
        copy.wait()
        for s in range(step // RELAYOUT_STEP):
            part = in_s[slot, pl.ds(s * RELAYOUT_STEP, RELAYOUT_STEP)]
            out_ref[:, slot_of(j, head_count), pl.ds(i * step + s * RELAYOUT_STEP, RELAYOUT_STEP), :] = jnp.swapaxes(
                part, 0, 1
            )


def by_expert(js, me, w_in, head_count, buffer, after):
    width, experts, columns = w_in.shape
    cols = width // head_count
    step = min(RELAYOUT_ROWS, cols)
    slots = len(js) * cols // step
    held = [] if buffer is None else [in_vmem(buffer)]
    return pl.pallas_call(
        functools.partial(relayout_kernel, js),
        out_shape=(
            pltpu.VMEM((experts, head_count, cols, columns), jnp.bfloat16),
            jax.ShapeDtypeStruct((SUBLANES, LANES), jnp.float32),
        ),
        in_specs=[SMEM, ANY] + [VMEM] * len(held) + [ANY],
        out_specs=(VMEM, VMEM),
        input_output_aliases={2: 0} if held else {},
        scratch_shapes=[
            pltpu.VMEM((slots, step, experts, columns), jnp.bfloat16),
            pltpu.SemaphoreType.DMA((slots,)),
        ],
        compiler_params=pltpu.CompilerParams(vmem_limit_bytes=16 * 2**20),
        cost_estimate=pl.CostEstimate(
            flops=0, bytes_accessed=4 * len(js) * cols * experts * columns, transcendentals=0
        ),
        name=f"by_expert_{js[0]}",
    )(me, in_hbm(w_in), *held, after)


def payload_kernel(head_count, *refs):
    blocks = head_count // 2
    pieces, (half_ref, *others), shares_ref = refs[:blocks], refs[blocks : 2 * blocks], refs[2 * blocks]
    payload_ref, resid_ref = refs[-2:]
    cols = pieces[0].shape[1]
    for t in range(blocks):
        total = pieces[t][...].astype(jnp.float32)
        for at, source in enumerate((half_ref, *others)):
            place = (t ^ at) * cols
            total += source[:, place : place + cols].astype(jnp.float32)
        payload_ref[:, t * cols : (t + 1) * cols] = total.astype(jnp.bfloat16)
        if t == 0:
            resid_ref[...] = total
    payload_ref[:, blocks * cols :] = shares_ref[...]


def payload_part(pieces, half, others, shares, after):
    blocks = len(pieces)
    rows, cols = pieces[0].shape
    return pl.pallas_call(
        functools.partial(payload_kernel, 2 * blocks),
        out_shape=(
            jax.ShapeDtypeStruct((rows, blocks * cols + shares.shape[1]), jnp.bfloat16),
            jax.ShapeDtypeStruct((rows, cols), jnp.float32),
        ),
        in_specs=[VMEM] * (2 * blocks + 1) + [ANY],
        out_specs=(VMEM, VMEM),
        compiler_params=pltpu.CompilerParams(vmem_limit_bytes=8 * 2**20),
        name="payload",
    )(*pieces, half, *others, shares, after)


def stack_kernel(count, *refs):
    rows = refs[0].shape[0]
    for i in range(count):
        refs[-1][i * rows : (i + 1) * rows, :] = refs[i][...]


def stack_part(parts, after):
    rows, columns = parts[0].shape
    return pl.pallas_call(
        functools.partial(stack_kernel, len(parts)),
        out_shape=jax.ShapeDtypeStruct((len(parts) * rows, columns), jnp.bfloat16),
        in_specs=[VMEM] * len(parts) + [ANY],
        out_specs=VMEM,
        compiler_params=pltpu.CompilerParams(vmem_limit_bytes=8 * 2**20),
        name="stack",
    )(*parts, after)


def expert_products(states, w_ref, first, p, per_step):
    columns = w_ref.shape[3]
    depth = states.shape[1]
    taken = pl.ds(first, depth // w_ref.shape[2])
    products = [
        jnp.dot(
            states,
            w_ref[p * per_step + i, taken].reshape(depth, columns),
            preferred_element_type=jnp.float32,
        )
        for i in range(per_step)
    ]
    return products[0] if per_step == 1 else jnp.concatenate(products, axis=1)


def steps_of(w_shape):
    per_step = max(1, 2 * LANES // w_shape[3])
    return w_shape[0] // per_step, per_step


def square_sum(ref, depth):
    return jnp.sum(jnp.square(ref[:, :depth].astype(jnp.float32)), axis=1, keepdims=True)


def local_shares(me, shares, experts):
    lanes = shares.shape[1]
    return pltpu.roll(shares.astype(jnp.float32), lax.rem(lanes - me * experts, lanes), 1)


def units_step(p, per_step, product, scale, shares):
    tokens = product.shape[0]
    first_half = lax.broadcasted_iota(jnp.int32, (tokens, LANES), 1) < LANES // 2
    expert = p * per_step
    share = shares[:, expert : expert + 1]
    if per_step == 2:
        share = jnp.where(first_half, share, shares[:, expert + 1 : expert + 2])
    a, b = product[:, :LANES], product[:, LANES:]
    gate = jnp.where(first_half, a, pltpu.roll(b, LANES // 2, 1)) * scale
    upward = jnp.where(first_half, pltpu.roll(a, LANES // 2, 1), b) * (scale * 0.5)
    return (share * (gate * (1.0 + jnp.tanh(gate * 0.5)) * upward)).astype(jnp.bfloat16)


def whole_kernel(me_ref, mine_ref, other_ref, w_ref, _, units_ref, states_s):
    experts, head_count, cols, _ = w_ref.shape
    depth = head_count // 2 * cols
    states_s[:, :depth] = mine_ref[:, :depth]
    states_s[:, depth:] = other_ref[:, :depth]
    square = square_sum(mine_ref, depth) + square_sum(other_ref, depth)
    scale = lax.rsqrt(square / (2 * depth) + norm_eps)
    shares = local_shares(me_ref[0], mine_ref[:, depth:], experts)
    steps, per_step = steps_of(w_ref.shape)
    for p in range(steps):
        product = expert_products(states_s[...], w_ref, 0, p, per_step)
        units_ref[:, p * LANES : (p + 1) * LANES] = units_step(
            p, per_step, product, scale, shares
        )


def first_kernel(mine_ref, w_ref, _, product_ref):
    _, head_count, cols, _ = w_ref.shape
    steps, per_step = steps_of(w_ref.shape)
    for p in range(steps):
        states = mine_ref[:, : head_count // 2 * cols]
        product_ref[p] = expert_products(states, w_ref, 0, p, per_step)


def second_kernel(me_ref, mine_ref, other_ref, product_ref, w_ref, w_down_ref, units_ref, send_ref):
    experts, head_count, cols, _ = w_ref.shape
    depth = head_count // 2 * cols
    square = square_sum(mine_ref, depth) + square_sum(other_ref, depth)
    scale = lax.rsqrt(square / (2 * depth) + norm_eps)
    shares = local_shares(me_ref[0], mine_ref[:, depth:], experts)
    steps, per_step = steps_of(w_ref.shape)
    for p in range(steps):
        product = product_ref[p] + expert_products(
            other_ref[:, :depth], w_ref, head_count // 2, p, per_step
        )
        units_ref[:, p * LANES : (p + 1) * LANES] = units_step(
            p, per_step, product, scale, shares
        )

    down_blocks(units_ref[...], w_down_ref, 1, send_ref)


def experts_whole(me, mine, other, weights, after, total_units):
    experts, head_count, cols, columns = weights.shape
    tokens = mine.shape[0]
    return pl.pallas_call(
        whole_kernel,
        out_shape=jax.ShapeDtypeStruct((tokens, total_units), jnp.bfloat16),
        in_specs=[SMEM] + [VMEM] * 3 + [ANY],
        out_specs=VMEM,
        scratch_shapes=[pltpu.VMEM((tokens, head_count * cols), jnp.bfloat16)],
        compiler_params=pltpu.CompilerParams(vmem_limit_bytes=12 * 2**20),
        cost_estimate=pl.CostEstimate(
            flops=2 * tokens * head_count * cols * experts * columns,
            bytes_accessed=2 * head_count * cols * experts * columns,
            transcendentals=0,
        ),
        name="experts_whole",
    )(me, mine, other, in_vmem(weights), after)


def experts_first(mine, weights, after):
    experts, head_count, cols, columns = weights.shape
    tokens = mine.shape[0]
    steps, per_step = steps_of(weights.shape)
    return pl.pallas_call(
        first_kernel,
        out_shape=jax.ShapeDtypeStruct((steps, tokens, per_step * columns), jnp.float32),
        in_specs=[VMEM] * 2 + [ANY],
        out_specs=VMEM,
        compiler_params=pltpu.CompilerParams(vmem_limit_bytes=12 * 2**20),
        cost_estimate=pl.CostEstimate(
            flops=tokens * head_count * cols * experts * columns,
            bytes_accessed=head_count * cols * experts * columns,
            transcendentals=0,
        ),
        name="experts_first",
    )(mine, in_vmem(weights), after)


def experts_second(me, mine, other, products, weights, w_down):
    experts, head_count, cols, columns = weights.shape
    tokens = mine.shape[0]
    return pl.pallas_call(
        second_kernel,
        out_shape=(
            jax.ShapeDtypeStruct((tokens, w_down.shape[1]), jnp.bfloat16),
            jax.ShapeDtypeStruct((tokens, head_count // 2 * cols), jnp.bfloat16),
        ),
        in_specs=[SMEM] + [VMEM] * 5,
        out_specs=(VMEM, VMEM),
        compiler_params=pltpu.CompilerParams(vmem_limit_bytes=12 * 2**20),
        cost_estimate=pl.CostEstimate(
            flops=tokens * head_count * cols * experts * columns,
            bytes_accessed=head_count * cols * experts * columns,
            transcendentals=0,
        ),
        name="experts_second",
    )(me, mine, other, products, in_vmem(weights), in_vmem(w_down))


def down_blocks(units, w_ref, first, out_ref):
    cols = w_ref.shape[2]
    for t in range(w_ref.shape[0] // 2):
        out_ref[:, t * cols : (t + 1) * cols] = jnp.dot(
            units, w_ref[2 * t + first], preferred_element_type=jnp.float32
        ).astype(jnp.bfloat16)


def down_kernel(firsts, units_ref, w_ref, _, *outs):
    for first, out_ref in zip(firsts, outs):
        down_blocks(units_ref[...], w_ref, first, out_ref)


def down_part(units, w_down, firsts, after):
    head_count, total_units, cols = w_down.shape
    tokens = units.shape[0]
    half = jax.ShapeDtypeStruct((tokens, head_count // 2 * cols), jnp.bfloat16)
    return pl.pallas_call(
        functools.partial(down_kernel, firsts),
        out_shape=[half] * len(firsts),
        in_specs=[VMEM, VMEM, ANY],
        out_specs=[VMEM] * len(firsts),
        compiler_params=pltpu.CompilerParams(vmem_limit_bytes=12 * 2**20),
        cost_estimate=pl.CostEstimate(
            flops=len(firsts) * tokens * total_units * head_count * cols,
            bytes_accessed=len(firsts) * total_units * head_count * cols,
            transcendentals=0,
        ),
        name="down",
    )(units, in_vmem(w_down), after)


def hold_kernel(value_ref, after_ref, out_ref):
    pass


def hold(value, after):
    return pl.pallas_call(
        hold_kernel,
        out_shape=jax.ShapeDtypeStruct(value.shape, value.dtype),
        in_specs=[ANY, ANY],
        out_specs=ANY,
        input_output_aliases={0: 0},
        compiler_params=pltpu.CompilerParams(vmem_limit_bytes=2**20),
        name="hold",
    )(value, after)


def sum_kernel(keep_ref, sent_ref, *outs):
    cols = outs[0].shape[1]
    for t, out in enumerate(outs):
        part = slice(t * cols, (t + 1) * cols)
        total = keep_ref[:, part].astype(jnp.float32) + sent_ref[:, part].astype(jnp.float32)
        out[...] = total.astype(out.dtype)


def sum_part(keep, sent, cols, first_type):
    tokens, columns = keep.shape
    blocks = columns // cols
    return pl.pallas_call(
        sum_kernel,
        out_shape=[
            jax.ShapeDtypeStruct((tokens, cols), jnp.bfloat16 if t else first_type)
            for t in range(blocks)
        ],
        in_specs=[VMEM, VMEM],
        out_specs=[VMEM] * blocks,
        compiler_params=pltpu.CompilerParams(vmem_limit_bytes=8 * 2**20),
        name="sum",
    )(keep, sent)


def swap(value, axis, size, mask):
    return lax.ppermute(value, axis, [(i, i ^ mask) for i in range(size)])


def per_device(
    hidden, lengths, expert_ids, route_weights, w_qkv, w_out, k_cache, v_cache, w_in, w_down
):
    req_size = lax.axis_size("req")
    head_size = lax.axis_size("head")
    me = lax.axis_index("head")
    me_ref = me[None].astype(jnp.int32)
    rows, cols = hidden.shape
    experts_local, units_local, width = w_down.shape
    even = range(0, head_size, 2)

    pieces = [hidden] + [swap(hidden, "head", head_size, j) for j in range(1, head_size)]
    flat = (rows * k_cache.shape[1] * k_cache.shape[2], k_cache.shape[3])
    own, w_near, room, cosine, sine, keys, shares = fetch(
        me_ref, lengths, hidden, w_qkv, flat, head_size, expert_ids, route_weights,
        head_size * experts_local,
    )
    pieces[0] = own
    keep, send, _, w_down_near = attention(
        pieces,
        me_ref,
        keys,
        cosine,
        sine,
        w_near,
        room,
        w_out,
        k_cache.reshape(flat),
        v_cache.reshape(flat),
        w_down.reshape(experts_local * units_local, width),
    )
    (half,) = sum_part(keep, swap(send, "head", head_size, 1), keep.shape[1], jnp.bfloat16)
    others = [swap(half, "head", head_size, j) for j in even if j]
    early, late = range(head_size // 2), range(head_size // 2, head_size)
    buffer, token = by_expert(tuple(early), me_ref, w_in, head_size, None, half)

    payload, resid = payload_part(
        [pieces[j] for j in even], half, others, shares, token
    )

    steps = range(2, req_size, 2)
    line = [payload] + [swap(payload, "req", req_size, k) for k in steps]
    buffer, token = by_expert(tuple(late), me_ref, w_in, head_size, buffer, payload)
    line = stack_part(line, token)
    line_other = swap(line, "head", head_size, 1)
    crossed = swap(line, "req", req_size, 1)
    units = experts_whole(me_ref, line, line_other, buffer, token, w_down_near.shape[1])
    keep, send = down_part(units, w_down_near, (0, 1), token)
    line_sums = sum_part(keep, swap(send, "head", head_size, 1), cols, jnp.float32)
    crossed = hold(crossed, send)
    crossed_other = swap(crossed, "head", head_size, 1)
    products = experts_first(crossed, buffer, line_sums[-1])
    units, send = experts_second(me_ref, crossed, crossed_other, products, buffer, w_down_near)
    (keep,) = down_part(units, w_down_near, (0,), send)
    crossed_sums = sum_part(keep, swap(send, "head", head_size, 1), cols, jnp.bfloat16)
    total = line_sums[0]
    got = [swap(hold(line_sums[j // 2], keep), "head", head_size, j) for j in even if j]
    for j in even:
        pairs = [
            (r * head_size + h, (r ^ 1) * head_size + (h ^ j))
            for r in range(req_size)
            for h in range(head_size)
        ]
        got.append(lax.ppermute(crossed_sums[j // 2], ("req", "head"), pairs))
    for part in got:
        total = total + part.astype(jnp.float32)
    chunks = total.astype(jnp.bfloat16).reshape(req_size // 2, rows, cols)
    out = chunks[0].astype(jnp.float32)
    for k in steps:
        out = out + swap(chunks[k // 2], "req", req_size, k).astype(jnp.float32)
    return (out + resid).astype(jnp.bfloat16)


def solution(mesh):
    in_specs = (
        P("req", "head"),
        P("req"),
        P("req", None),
        P("req", None),
        P(None, None, "head"),
        P("head", None),
        P("req", None, "head", None),
        P("req", None, "head", None),
        P(None, "head", "req"),
        P("head", "req", None),
    )
    out_specs = P("req", "head")
    return jax.shard_map(
        per_device, mesh=mesh, in_specs=in_specs, out_specs=out_specs, check_vma=False
    )
```

```python
import functools
import itertools
import jax
import jax.numpy as jnp
from jax import lax
from jax.experimental import pallas as pl
from jax.experimental.pallas import tpu as pltpu
from jax.sharding import PartitionSpec as P

rope_theta = 50000.0
norm_eps = 1e-05
LANES = 128
SUBLANES = 8
CHUNK = 128
GROUP = 8
MASKED = -1e30


VMEM = pl.BlockSpec(memory_space=pltpu.VMEM)
SMEM = pl.BlockSpec(memory_space=pltpu.SMEM)
ANY = pl.BlockSpec(memory_space=pl.ANY)


def in_hbm(array):
    return pltpu.with_memory_space_constraint(array, pltpu.HBM)


def in_vmem(array):
    return pltpu.with_memory_space_constraint(array, pltpu.VMEM)


def used_rows(length, heads_local):
    return pl.multiple_of((length + 7) // 8 * (8 * heads_local), 8 * heads_local)


def exchanges(count):
    steps = []
    size = 1
    while size < count:
        gap = size
        while gap >= 1:
            for start in range(gap % size, count - gap, 2 * gap):
                for i in range(min(gap, count - start - gap)):
                    if (start + i) // (2 * size) == (start + i + gap) // (2 * size):
                        steps.append((start + i, start + i + gap))
            gap //= 2
        size *= 2
    return steps


def packed(length, request):
    return (length << 16) + request


def unpacked(key):
    return key >> 16, key & 0xFFFF


def fetch_kernel(
    lengths_hbm, me_ref, freqs_ref, own_ref, w_ref, ids_ref, route_ref,
    own_out_ref, w_out_ref, blank_ref, cos_ref, sin_ref, keys_ref, shares_ref, part_ref,
    lengths_ref, angle_s, ids_s, route_s, sem, small_sem,
):
    head_count, cols = w_out_ref.shape[1:3]
    chunk_rows = CHUNK * cols // LANES
    me = me_ref[0]
    lengths_copy, *copies = [
        pltpu.make_async_copy(source, target, small_sem.at[i])
        for i, (source, target) in enumerate(
            (
                (lengths_hbm, lengths_ref),
                (ids_ref, ids_s),
                (route_ref, route_s),
                (own_ref, own_out_ref),
            )
        )
    ]
    small = copies[:2]
    for j in range(head_count):
        for c in range(w_ref.shape[0]):
            first = pl.multiple_of((me ^ j) * cols, cols)
            copies.append(
                pltpu.make_async_copy(
                    w_ref.at[c, pl.ds(first, cols)], w_out_ref.at[c, j], sem.at[c, j]
                )
            )
    lengths_copy.start()
    for copy in copies:
        copy.start()
    lengths_copy.wait()

    rows = angle_s.shape[0]
    cache_rows = blank_ref.shape[0] // rows

    @pl.loop(0, rows)
    def _(r):
        last = r * cache_rows + (lengths_ref[r] - 1) // CHUNK * chunk_rows
        blank_ref[pl.ds(pl.multiple_of(last, chunk_rows), chunk_rows)] = jnp.zeros(
            (chunk_rows, LANES), jnp.bfloat16
        )
        angle_s[pl.ds(r, 1), :] = lengths_ref[r].astype(jnp.float32) * freqs_ref[...]

    cos_ref[...] = jnp.cos(angle_s[...])
    lane = lax.broadcasted_iota(jnp.int32, sin_ref.shape, 1)
    sine = jnp.sin(angle_s[...])
    sin_ref[...] = jnp.where(lane < LANES // 2, -sine, sine)
    @pl.loop(0, rows // GROUP)
    def _(g):
        keys = [packed(lengths_ref[g * GROUP + i], g * GROUP + i) for i in range(GROUP)]
        for low, high in exchanges(GROUP):
            larger, smaller = jnp.maximum(keys[low], keys[high]), jnp.minimum(keys[low], keys[high])
            keys[low], keys[high] = larger, smaller
        for i in range(GROUP):
            keys_ref[g * GROUP + i] = keys[i]

    for copy in small:
        copy.wait()
    expert = lax.broadcasted_iota(jnp.int32, (shares_ref.shape[1], rows), 0)
    shares = jnp.zeros(expert.shape, jnp.float32)
    for k in range(ids_s.shape[0]):
        shares += jnp.where(expert == ids_s[k : k + 1, :], route_s[k : k + 1, :], 0.0)
    shares_ref[...] = jnp.transpose(shares, (1, 0)).astype(jnp.bfloat16)
    kinds = w_ref.shape[0]
    for copy in copies[2 : 3 + kinds]:
        copy.wait()
    for c in range(kinds):
        part_ref[c] = jnp.dot(
            own_out_ref[...], w_out_ref[c, 0], preferred_element_type=jnp.float32
        )
    for copy in copies[3 + kinds :]:
        copy.wait()


def fetch(me, lengths, hidden, w_qkv, v_shape, head_count, expert_ids, route_weights, experts):
    cols = w_qkv.shape[2]
    rows = hidden.shape[0]
    exponents = jnp.arange(LANES, dtype=jnp.float32) % (LANES // 2) / (LANES // 2)
    freqs = (rope_theta**-exponents)[None, :]
    return pl.pallas_call(
        fetch_kernel,
        out_shape=(
            pltpu.VMEM(hidden.shape, jnp.bfloat16),
            pltpu.VMEM((w_qkv.shape[0], head_count, cols, cols), jnp.bfloat16),
            pltpu.VMEM(v_shape, jnp.bfloat16),
            pltpu.VMEM((rows, LANES), jnp.float32),
            pltpu.VMEM((rows, LANES), jnp.float32),
            pltpu.SMEM(lengths.shape, lengths.dtype),
            pltpu.VMEM((rows, -(-experts // LANES) * LANES), jnp.bfloat16),
            pltpu.VMEM((w_qkv.shape[0], rows, cols), jnp.float32),
        ),
        in_specs=[ANY, SMEM, VMEM] + [ANY] * 4,
        out_specs=[VMEM] * 5 + [SMEM, VMEM, VMEM],
        scratch_shapes=[
            pltpu.SMEM(lengths.shape, lengths.dtype),
            pltpu.VMEM((rows, LANES), jnp.float32),
            pltpu.VMEM(expert_ids.shape[::-1], expert_ids.dtype),
            pltpu.VMEM(route_weights.shape[::-1], route_weights.dtype),
            pltpu.SemaphoreType.DMA((w_qkv.shape[0], head_count)),
            pltpu.SemaphoreType.DMA((4,)),
        ],
        compiler_params=pltpu.CompilerParams(vmem_limit_bytes=8 * 2**20),
        cost_estimate=pl.CostEstimate(
            flops=0, bytes_accessed=4 * w_qkv.size, transcendentals=0
        ),
        name="fetch",
    )(
        in_hbm(lengths), me, freqs, in_hbm(hidden), in_hbm(w_qkv), in_hbm(expert_ids.T),
        in_hbm(route_weights.T),
    )


def attention_kernel(head_count, keys_ref, me_ref, cos_ref, sin_ref, part_ref, *refs):
    pieces = refs[:head_count]
    (
        w_qkv_ref, _, w_out_ref, k_ref, v_ref, w_down_ref, keep_ref, send_ref, v_s, down_ref,
        w_out_s, k_s, query_s, key_s, value_s, attended_s, out_sem, k_sem, v_sem, down_sem,
    ) = refs[head_count:]
    rows, cols = pieces[0].shape
    heads_local = cols // LANES
    chunk_rows = CHUNK * heads_local
    me = me_ref[0]

    def out_copy(j):
        first = pl.multiple_of((me ^ j) * cols, cols)
        return pltpu.make_async_copy(
            w_out_ref.at[:, pl.ds(first, cols)], w_out_s.at[j], out_sem.at[j]
        )

    cache_rows = k_s.shape[0] // rows

    def cache_copy(source, target, sem, r, used):
        taken = pl.ds(pl.multiple_of(r * cache_rows, cache_rows), used)
        return pltpu.make_async_copy(
            source.at[taken], target.at[taken], sem.at[r // GROUP]
        )

    @pl.loop(0, rows, unroll=4)
    def _(i):
        length, r = unpacked(keys_ref[i])
        used = used_rows(length, heads_local)
        cache_copy(k_ref, k_s, k_sem, r, used).start()
        cache_copy(v_ref, v_s, v_sem, r, used).start()

    def down_copy(j):
        first = pl.multiple_of((me ^ j) * cols, cols)
        return pltpu.make_async_copy(
            w_down_ref.at[:, pl.ds(first, cols)], down_ref.at[j], down_sem.at[j]
        )

    for j in range(head_count):
        out_copy(j).start()
    for j in range(head_count):
        down_copy(j).start()

    if heads_local < SUBLANES:
        query_s[...] = jnp.zeros_like(query_s)
        key_s[...] = jnp.zeros_like(key_s)
        value_s[...] = jnp.zeros_like(value_s)
    states = jnp.concatenate([piece[...] for piece in pieces], axis=1)
    square = jnp.sum(jnp.square(states.astype(jnp.float32)), axis=1, keepdims=True)
    scale = lax.rsqrt(square / (cols * head_count) + norm_eps)
    cosine, sine = cos_ref[...], sin_ref[...]
    for c, target in enumerate((query_s, key_s, value_s)):
        projected = scale * (
            part_ref[c]
            + jnp.dot(
                states[:, cols:],
                w_qkv_ref[c, pl.ds(1, head_count - 1)].reshape((head_count - 1) * cols, cols),
                preferred_element_type=jnp.float32,
            )
        )
        for h in range(heads_local):
            part = projected[:, h * LANES : (h + 1) * LANES]
            if c < 2:
                part = part * cosine + pltpu.roll(part, LANES // 2, 1) * sine
            target[:, h, :] = part.astype(jnp.bfloat16).astype(jnp.float32)

    column = lax.broadcasted_iota(jnp.int32, (2 * SUBLANES, chunk_rows), 1)
    row = lax.broadcasted_iota(jnp.int32, (2 * SUBLANES, chunk_rows), 0)
    same_head = column % heads_local == row % SUBLANES
    upper = row < SUBLANES
    score_scale = LANES**-0.5
    blank = jnp.zeros((SUBLANES, LANES), jnp.float32)

    def diagonal(a, b):
        return jnp.concatenate(
            [jnp.concatenate([a, blank], axis=1), jnp.concatenate([blank, b], axis=1)], axis=0
        )

    @pl.loop(0, rows // GROUP)
    def _(g):
        lengths, requests = zip(*[unpacked(keys_ref[g * GROUP + i]) for i in range(GROUP)])
        pairs = list(zip(requests[::2], requests[1::2]))
        spans = list(zip(lengths[::2], lengths[1::2]))
        queries = [diagonal(query_s[a], query_s[b]).astype(jnp.bfloat16) for a, b in pairs]
        own = [
            jnp.sum(query_s[r] * key_s[r], axis=1, keepdims=True) * score_scale for r in requests
        ]
        own = [jnp.concatenate([a, b], axis=0) for a, b in zip(own[::2], own[1::2])]
        values = [diagonal(value_s[a], value_s[b]) for a, b in pairs]
        used = used_rows(sum((length + 7) // 8 * 8 for length in lengths), heads_local)
        cache_copy(k_ref, k_s, k_sem, g * GROUP, used).wait()
        cache_copy(v_ref, v_s, v_sem, g * GROUP, used).wait()
        needed = [(lengths[i] + CHUNK - 1) // CHUNK for i in (0, GROUP // 2)]

        def with_chunks(counts):
            counts = [count for count in counts for _ in range(GROUP // 4)]

            def both(ref, c, pair, span):
                parts = []
                for r, length in zip(pair, span):
                    first = jnp.minimum(c, (length - 1) // CHUNK) * chunk_rows if c else 0
                    first = pl.multiple_of(r * cache_rows + first, chunk_rows)
                    parts.append(ref[pl.ds(first, chunk_rows)])
                return jnp.concatenate(parts, axis=1)

            scores = [
                [
                    lax.dot_general(
                        query,
                        both(k_s, c, pair, span),
                        (((1,), (1,)), ((), ())),
                        preferred_element_type=jnp.float32,
                    )
                    for c in range(count)
                ]
                for count, query, pair, span in zip(counts, queries, pairs, spans)
            ]
            limits = [
                jnp.where(upper, span[0] * heads_local, span[1] * heads_local) for span in spans
            ]
            scores = [
                [
                    jnp.where(
                        same_head & (column < limit - c * chunk_rows), score * score_scale, MASKED
                    )
                    for c, score in enumerate(parts)
                ]
                for limit, parts in zip(limits, scores)
            ]
            tops = [
                jnp.maximum(
                    mine, jnp.max(functools.reduce(jnp.maximum, parts), axis=1, keepdims=True)
                )
                for mine, parts in zip(own, scores)
            ]
            weights = [[jnp.exp(part - top) for part in parts] for top, parts in zip(tops, scores)]
            faded = [jnp.exp(mine - top) for mine, top in zip(own, tops)]
            totals = [
                fade + jnp.sum(functools.reduce(jnp.add, parts), axis=1, keepdims=True)
                for fade, parts in zip(faded, weights)
            ]
            sums = [
                fade * value
                + sum(
                    jnp.dot(
                        part.astype(jnp.bfloat16),
                        both(v_s, c, pair, span),
                        preferred_element_type=jnp.float32,
                    )
                    for c, part in enumerate(parts)
                )
                for pair, span, fade, value, parts in zip(pairs, spans, faded, values, weights)
            ]
            for (a, b), total, summed in zip(pairs, totals, sums):
                summed = summed / total
                attended_s[a] = summed[:SUBLANES, :LANES]
                attended_s[b] = summed[SUBLANES:, LANES:]

        most = cache_rows // chunk_rows
        for longer, shorter in itertools.product(range(1, most + 1), repeat=2):
            if longer >= shorter:
                pl.when((needed[0] == longer) & (needed[1] == shorter))(
                    functools.partial(with_chunks, (longer, shorter))
                )

    attended = jnp.concatenate(
        [attended_s[:, h, :] for h in range(heads_local)], axis=1
    ).astype(jnp.bfloat16)
    for j in range(head_count):
        out_copy(j).wait()
        target = send_ref if j % 2 else keep_ref
        target[:, j // 2 * cols : (j // 2 + 1) * cols] = jnp.dot(
            attended, w_out_s[j], preferred_element_type=jnp.float32
        ).astype(jnp.bfloat16)
    for j in range(head_count):
        down_copy(j).wait()


def attention(pieces, me, keys, cosine, sine, part, w_qkv, room, w_out, k_cache, v_cache, w_down):
    head_count = len(pieces)
    rows, cols = pieces[0].shape
    half = jax.ShapeDtypeStruct((rows, head_count // 2 * cols), jnp.bfloat16)
    return pl.pallas_call(
        functools.partial(attention_kernel, head_count),
        out_shape=(
            half,
            half,
            pltpu.VMEM(room.shape, jnp.bfloat16),
            pltpu.VMEM((head_count, w_down.shape[0], cols), jnp.bfloat16),
        ),
        in_specs=[SMEM, SMEM] + [VMEM] * (head_count + 5) + [ANY] * 4,
        out_specs=(VMEM, VMEM, VMEM, VMEM),
        input_output_aliases={head_count + 6: 2},
        scratch_shapes=[
            pltpu.VMEM((head_count, cols, cols), jnp.bfloat16),
            pltpu.VMEM(k_cache.shape, jnp.bfloat16),
        ]
        + [pltpu.VMEM((rows, SUBLANES, LANES), jnp.float32)] * 4
        + [
            pltpu.SemaphoreType.DMA((head_count,)),
            pltpu.SemaphoreType.DMA((rows // GROUP,)),
            pltpu.SemaphoreType.DMA((rows // GROUP,)),
            pltpu.SemaphoreType.DMA((head_count,)),
        ],
        compiler_params=pltpu.CompilerParams(vmem_limit_bytes=20 * 2**20),
        cost_estimate=pl.CostEstimate(
            flops=2 * rows * 4 * cols * head_count * cols,
            bytes_accessed=2 * w_down.size + k_cache.size // 2,
            transcendentals=0,
        ),
        name="attention",
    )(
        pltpu.with_memory_space_constraint(keys, pltpu.SMEM), me, in_vmem(cosine), in_vmem(sine), in_vmem(part), *map(in_vmem, pieces), in_vmem(w_qkv), in_vmem(room),
        in_hbm(w_out), in_hbm(k_cache), in_hbm(v_cache), in_hbm(w_down),
    )


RELAYOUT_ROWS = 128
RELAYOUT_STEP = 16

def slot_of(j, head_count):
    return j // 2 + j % 2 * (head_count // 2)


def relayout_kernel(js, me_ref, w_ref, *refs):
    out_ref, token_ref, in_s, in_sem = refs[-4:]
    token_ref[...] = jnp.zeros_like(token_ref)
    experts, head_count, cols, _ = out_ref.shape
    step = in_s.shape[1]
    per_block = cols // step
    copies = []
    for at, j in enumerate(js):
        base = (me_ref[0] ^ j) * cols
        for i in range(per_block):
            slot = at * per_block + i
            first = pl.multiple_of(base + i * step, step)
            copies.append(
                pltpu.make_async_copy(
                    w_ref.at[pl.ds(first, step)], in_s.at[slot], in_sem.at[slot]
                )
            )
    for copy in copies:
        copy.start()
    for slot, copy in enumerate(copies):
        j, i = js[slot // per_block], slot % per_block
        copy.wait()
        for s in range(step // RELAYOUT_STEP):
            part = in_s[slot, pl.ds(s * RELAYOUT_STEP, RELAYOUT_STEP)]
            out_ref[:, slot_of(j, head_count), pl.ds(i * step + s * RELAYOUT_STEP, RELAYOUT_STEP), :] = jnp.swapaxes(
                part, 0, 1
            )


def by_expert(js, me, w_in, head_count, buffer, after):
    width, experts, columns = w_in.shape
    cols = width // head_count
    step = min(RELAYOUT_ROWS, cols)
    slots = len(js) * cols // step
    held = [] if buffer is None else [in_vmem(buffer)]
    return pl.pallas_call(
        functools.partial(relayout_kernel, js),
        out_shape=(
            pltpu.VMEM((experts, head_count, cols, columns), jnp.bfloat16),
            jax.ShapeDtypeStruct((SUBLANES, LANES), jnp.float32),
        ),
        in_specs=[SMEM, ANY] + [VMEM] * len(held) + [ANY],
        out_specs=(VMEM, VMEM),
        input_output_aliases={2: 0} if held else {},
        scratch_shapes=[
            pltpu.VMEM((slots, step, experts, columns), jnp.bfloat16),
            pltpu.SemaphoreType.DMA((slots,)),
        ],
        compiler_params=pltpu.CompilerParams(vmem_limit_bytes=16 * 2**20),
        cost_estimate=pl.CostEstimate(
            flops=0, bytes_accessed=4 * len(js) * cols * experts * columns, transcendentals=0
        ),
        name=f"by_expert_{js[0]}",
    )(me, in_hbm(w_in), *held, after)


def payload_kernel(head_count, *refs):
    blocks = head_count // 2
    pieces, (half_ref, *others), shares_ref = refs[:blocks], refs[blocks : 2 * blocks], refs[2 * blocks]
    payload_ref, resid_ref = refs[-2:]
    cols = pieces[0].shape[1]
    for t in range(blocks):
        total = pieces[t][...].astype(jnp.float32)
        for at, source in enumerate((half_ref, *others)):
            place = (t ^ at) * cols
            total += source[:, place : place + cols].astype(jnp.float32)
        payload_ref[:, t * cols : (t + 1) * cols] = total.astype(jnp.bfloat16)
        if t == 0:
            resid_ref[...] = total
    payload_ref[:, blocks * cols :] = shares_ref[...]


def payload_part(pieces, half, others, shares, after):
    blocks = len(pieces)
    rows, cols = pieces[0].shape
    return pl.pallas_call(
        functools.partial(payload_kernel, 2 * blocks),
        out_shape=(
            jax.ShapeDtypeStruct((rows, blocks * cols + shares.shape[1]), jnp.bfloat16),
            jax.ShapeDtypeStruct((rows, cols), jnp.float32),
        ),
        in_specs=[VMEM] * (2 * blocks + 1) + [ANY],
        out_specs=(VMEM, VMEM),
        compiler_params=pltpu.CompilerParams(vmem_limit_bytes=8 * 2**20),
        name="payload",
    )(*pieces, half, *others, shares, after)


def stack_kernel(count, *refs):
    rows = refs[0].shape[0]
    for i in range(count):
        refs[-1][i * rows : (i + 1) * rows, :] = refs[i][...]


def stack_part(parts, after):
    rows, columns = parts[0].shape
    return pl.pallas_call(
        functools.partial(stack_kernel, len(parts)),
        out_shape=jax.ShapeDtypeStruct((len(parts) * rows, columns), jnp.bfloat16),
        in_specs=[VMEM] * len(parts) + [ANY],
        out_specs=VMEM,
        compiler_params=pltpu.CompilerParams(vmem_limit_bytes=8 * 2**20),
        name="stack",
    )(*parts, after)


def expert_products(states, w_ref, first, p, per_step):
    columns = w_ref.shape[3]
    depth = states.shape[1]
    taken = pl.ds(first, depth // w_ref.shape[2])
    products = [
        jnp.dot(
            states,
            w_ref[p * per_step + i, taken].reshape(depth, columns),
            preferred_element_type=jnp.float32,
        )
        for i in range(per_step)
    ]
    return products[0] if per_step == 1 else jnp.concatenate(products, axis=1)


def steps_of(w_shape):
    per_step = max(1, 2 * LANES // w_shape[3])
    return w_shape[0] // per_step, per_step


def square_sum(ref, depth):
    return jnp.sum(jnp.square(ref[:, :depth].astype(jnp.float32)), axis=1, keepdims=True)


def local_shares(me, shares, experts):
    lanes = shares.shape[1]
    return pltpu.roll(shares.astype(jnp.float32), lax.rem(lanes - me * experts, lanes), 1)


def units_step(p, per_step, product, scale, shares):
    tokens = product.shape[0]
    first_half = lax.broadcasted_iota(jnp.int32, (tokens, LANES), 1) < LANES // 2
    expert = p * per_step
    share = shares[:, expert : expert + 1]
    if per_step == 2:
        share = jnp.where(first_half, share, shares[:, expert + 1 : expert + 2])
    a, b = product[:, :LANES], product[:, LANES:]
    gate = jnp.where(first_half, a, pltpu.roll(b, LANES // 2, 1)) * scale
    upward = jnp.where(first_half, pltpu.roll(a, LANES // 2, 1), b) * (scale * 0.5)
    return (share * (gate * (1.0 + jnp.tanh(gate * 0.5)) * upward)).astype(jnp.bfloat16)


def whole_kernel(me_ref, mine_ref, other_ref, w_ref, _, units_ref, states_s):
    experts, head_count, cols, _ = w_ref.shape
    depth = head_count // 2 * cols
    states_s[:, :depth] = mine_ref[:, :depth]
    states_s[:, depth:] = other_ref[:, :depth]
    square = square_sum(mine_ref, depth) + square_sum(other_ref, depth)
    scale = lax.rsqrt(square / (2 * depth) + norm_eps)
    shares = local_shares(me_ref[0], mine_ref[:, depth:], experts)
    steps, per_step = steps_of(w_ref.shape)
    for p in range(steps):
        product = expert_products(states_s[...], w_ref, 0, p, per_step)
        units_ref[:, p * LANES : (p + 1) * LANES] = units_step(
            p, per_step, product, scale, shares
        )


def first_kernel(mine_ref, w_ref, _, product_ref):
    _, head_count, cols, _ = w_ref.shape
    steps, per_step = steps_of(w_ref.shape)
    for p in range(steps):
        states = mine_ref[:, : head_count // 2 * cols]
        product_ref[p] = expert_products(states, w_ref, 0, p, per_step)


def second_kernel(me_ref, mine_ref, other_ref, product_ref, w_ref, w_down_ref, units_ref, send_ref):
    experts, head_count, cols, _ = w_ref.shape
    depth = head_count // 2 * cols
    square = square_sum(mine_ref, depth) + square_sum(other_ref, depth)
    scale = lax.rsqrt(square / (2 * depth) + norm_eps)
    shares = local_shares(me_ref[0], mine_ref[:, depth:], experts)
    steps, per_step = steps_of(w_ref.shape)
    for p in range(steps):
        product = product_ref[p] + expert_products(
            other_ref[:, :depth], w_ref, head_count // 2, p, per_step
        )
        units_ref[:, p * LANES : (p + 1) * LANES] = units_step(
            p, per_step, product, scale, shares
        )

    down_blocks(units_ref[...], w_down_ref, 1, send_ref)


def experts_whole(me, mine, other, weights, after, total_units):
    experts, head_count, cols, columns = weights.shape
    tokens = mine.shape[0]
    return pl.pallas_call(
        whole_kernel,
        out_shape=jax.ShapeDtypeStruct((tokens, total_units), jnp.bfloat16),
        in_specs=[SMEM] + [VMEM] * 3 + [ANY],
        out_specs=VMEM,
        scratch_shapes=[pltpu.VMEM((tokens, head_count * cols), jnp.bfloat16)],
        compiler_params=pltpu.CompilerParams(vmem_limit_bytes=12 * 2**20),
        cost_estimate=pl.CostEstimate(
            flops=2 * tokens * head_count * cols * experts * columns,
            bytes_accessed=2 * head_count * cols * experts * columns,
            transcendentals=0,
        ),
        name="experts_whole",
    )(me, mine, other, in_vmem(weights), after)


def experts_first(mine, weights, after):
    experts, head_count, cols, columns = weights.shape
    tokens = mine.shape[0]
    steps, per_step = steps_of(weights.shape)
    return pl.pallas_call(
        first_kernel,
        out_shape=jax.ShapeDtypeStruct((steps, tokens, per_step * columns), jnp.float32),
        in_specs=[VMEM] * 2 + [ANY],
        out_specs=VMEM,
        compiler_params=pltpu.CompilerParams(vmem_limit_bytes=12 * 2**20),
        cost_estimate=pl.CostEstimate(
            flops=tokens * head_count * cols * experts * columns,
            bytes_accessed=head_count * cols * experts * columns,
            transcendentals=0,
        ),
        name="experts_first",
    )(mine, in_vmem(weights), after)


def experts_second(me, mine, other, products, weights, w_down):
    experts, head_count, cols, columns = weights.shape
    tokens = mine.shape[0]
    return pl.pallas_call(
        second_kernel,
        out_shape=(
            jax.ShapeDtypeStruct((tokens, w_down.shape[1]), jnp.bfloat16),
            jax.ShapeDtypeStruct((tokens, head_count // 2 * cols), jnp.bfloat16),
        ),
        in_specs=[SMEM] + [VMEM] * 5,
        out_specs=(VMEM, VMEM),
        compiler_params=pltpu.CompilerParams(vmem_limit_bytes=12 * 2**20),
        cost_estimate=pl.CostEstimate(
            flops=tokens * head_count * cols * experts * columns,
            bytes_accessed=head_count * cols * experts * columns,
            transcendentals=0,
        ),
        name="experts_second",
    )(me, mine, other, products, in_vmem(weights), in_vmem(w_down))


def down_blocks(units, w_ref, first, out_ref):
    cols = w_ref.shape[2]
    for t in range(w_ref.shape[0] // 2):
        out_ref[:, t * cols : (t + 1) * cols] = jnp.dot(
            units, w_ref[2 * t + first], preferred_element_type=jnp.float32
        ).astype(jnp.bfloat16)


def down_kernel(firsts, units_ref, w_ref, _, *outs):
    for first, out_ref in zip(firsts, outs):
        down_blocks(units_ref[...], w_ref, first, out_ref)


def down_part(units, w_down, firsts, after):
    head_count, total_units, cols = w_down.shape
    tokens = units.shape[0]
    half = jax.ShapeDtypeStruct((tokens, head_count // 2 * cols), jnp.bfloat16)
    return pl.pallas_call(
        functools.partial(down_kernel, firsts),
        out_shape=[half] * len(firsts),
        in_specs=[VMEM, VMEM, ANY],
        out_specs=[VMEM] * len(firsts),
        compiler_params=pltpu.CompilerParams(vmem_limit_bytes=12 * 2**20),
        cost_estimate=pl.CostEstimate(
            flops=len(firsts) * tokens * total_units * head_count * cols,
            bytes_accessed=len(firsts) * total_units * head_count * cols,
            transcendentals=0,
        ),
        name="down",
    )(units, in_vmem(w_down), after)


def hold_kernel(value_ref, after_ref, out_ref):
    pass


def hold(value, after):
    return pl.pallas_call(
        hold_kernel,
        out_shape=jax.ShapeDtypeStruct(value.shape, value.dtype),
        in_specs=[ANY, ANY],
        out_specs=ANY,
        input_output_aliases={0: 0},
        compiler_params=pltpu.CompilerParams(vmem_limit_bytes=2**20),
        name="hold",
    )(value, after)


def sum_kernel(keep_ref, sent_ref, *outs):
    cols = outs[0].shape[1]
    for t, out in enumerate(outs):
        part = slice(t * cols, (t + 1) * cols)
        total = keep_ref[:, part].astype(jnp.float32) + sent_ref[:, part].astype(jnp.float32)
        out[...] = total.astype(out.dtype)


def sum_part(keep, sent, cols, first_type):
    tokens, columns = keep.shape
    blocks = columns // cols
    return pl.pallas_call(
        sum_kernel,
        out_shape=[
            jax.ShapeDtypeStruct((tokens, cols), jnp.bfloat16 if t else first_type)
            for t in range(blocks)
        ],
        in_specs=[VMEM, VMEM],
        out_specs=[VMEM] * blocks,
        compiler_params=pltpu.CompilerParams(vmem_limit_bytes=8 * 2**20),
        name="sum",
    )(keep, sent)


def swap(value, axis, size, mask):
    return lax.ppermute(value, axis, [(i, i ^ mask) for i in range(size)])


def per_device(
    hidden, lengths, expert_ids, route_weights, w_qkv, w_out, k_cache, v_cache, w_in, w_down
):
    req_size = lax.axis_size("req")
    head_size = lax.axis_size("head")
    me = lax.axis_index("head")
    me_ref = me[None].astype(jnp.int32)
    rows, cols = hidden.shape
    experts_local, units_local, width = w_down.shape
    even = range(0, head_size, 2)

    pieces = [hidden] + [swap(hidden, "head", head_size, j) for j in range(1, head_size)]
    flat = (rows * k_cache.shape[1] * k_cache.shape[2], k_cache.shape[3])
    own, w_near, room, cosine, sine, keys, shares, part = fetch(
        me_ref, lengths, hidden, w_qkv, flat, head_size, expert_ids, route_weights,
        head_size * experts_local,
    )
    pieces[0] = own
    keep, send, _, w_down_near = attention(
        pieces,
        me_ref,
        keys,
        cosine,
        sine,
        part,
        w_near,
        room,
        w_out,
        k_cache.reshape(flat),
        v_cache.reshape(flat),
        w_down.reshape(experts_local * units_local, width),
    )
    (half,) = sum_part(keep, swap(send, "head", head_size, 1), keep.shape[1], jnp.bfloat16)
    others = [swap(half, "head", head_size, j) for j in even if j]
    early, late = range(head_size // 2), range(head_size // 2, head_size)
    buffer, token = by_expert(tuple(early), me_ref, w_in, head_size, None, half)

    payload, resid = payload_part(
        [pieces[j] for j in even], half, others, shares, token
    )

    steps = range(2, req_size, 2)
    line = [payload] + [swap(payload, "req", req_size, k) for k in steps]
    buffer, token = by_expert(tuple(late), me_ref, w_in, head_size, buffer, payload)
    line = stack_part(line, token)
    line_other = swap(line, "head", head_size, 1)
    crossed = swap(line, "req", req_size, 1)
    units = experts_whole(me_ref, line, line_other, buffer, token, w_down_near.shape[1])
    keep, send = down_part(units, w_down_near, (0, 1), token)
    line_sums = sum_part(keep, swap(send, "head", head_size, 1), cols, jnp.float32)
    crossed = hold(crossed, send)
    crossed_other = swap(crossed, "head", head_size, 1)
    products = experts_first(crossed, buffer, line_sums[-1])
    units, send = experts_second(me_ref, crossed, crossed_other, products, buffer, w_down_near)
    (keep,) = down_part(units, w_down_near, (0,), send)
    crossed_sums = sum_part(keep, swap(send, "head", head_size, 1), cols, jnp.bfloat16)
    total = line_sums[0]
    got = [swap(hold(line_sums[j // 2], keep), "head", head_size, j) for j in even if j]
    for j in even:
        pairs = [
            (r * head_size + h, (r ^ 1) * head_size + (h ^ j))
            for r in range(req_size)
            for h in range(head_size)
        ]
        got.append(lax.ppermute(crossed_sums[j // 2], ("req", "head"), pairs))
    for part in got:
        total = total + part.astype(jnp.float32)
    chunks = total.astype(jnp.bfloat16).reshape(req_size // 2, rows, cols)
    out = chunks[0].astype(jnp.float32)
    for k in steps:
        out = out + swap(chunks[k // 2], "req", req_size, k).astype(jnp.float32)
    return (out + resid).astype(jnp.bfloat16)


def solution(mesh):
    in_specs = (
        P("req", "head"),
        P("req"),
        P("req", None),
        P("req", None),
        P(None, None, "head"),
        P("head", None),
        P("req", None, "head", None),
        P("req", None, "head", None),
        P(None, "head", "req"),
        P("head", "req", None),
    )
    out_specs = P("req", "head")
    return jax.shard_map(
        per_device, mesh=mesh, in_specs=in_specs, out_specs=out_specs, check_vma=False
    )
```
